32 devices in a mesh: mode: 4 (over x, core), batch: 4 (over z), cores: 2 (over y).
Axes of the slice: x: 2, y: 2, z: 4, core: 2. Of those that a mesh axis runs over, the one named last changes fastest.
Arguments:
- fields: bfloat16 [4, 20, 1024, 1024], P('batch', None, ('mode', 'cores')), may hold values from -6 to 6
- lift_weight: bfloat16 [20, 128], replicated, may hold values from -1.25 to 1.25
- lift_bias: float32 [128], replicated, may hold values from -3 to 3
- first_core: bfloat16 [128, 32, 32], P('batch'), may hold values from -1 to 1
- second_core: bfloat16 [128, 32, 32], P(('mode', 'cores')), may hold values from -1 to 1
- input_core: bfloat16 [128, 32, 32], P('batch'), may hold values from -0.09375 to 0.09375
- output_core: bfloat16 [128, 2, 32, 32], P('batch'), may hold values from -3 to 3
- skip_weight: bfloat16 [128, 128], replicated, may hold values from -0.5 to 0.5
- skip_bias: float32 [128], replicated, may hold values from -3 to 3
- out_weight: bfloat16 [128, 20], replicated, may hold values from -0.5 to 0.5
- out_bias: float32 [20], replicated, may hold values from -3 to 3
Outputs:
- updated: bfloat16 [4, 20, 1024, 1024], P('batch', None, ('mode', 'cores'))
The draws below stay inside these ranges and needn't reach their ends.
All inputs are finite; a program needn't handle non-finite values.
Results may differ from the reference program's by a relative error of at most 0.012.
Values may be sent and summed in bfloat16 or wider, within the bound.
A program may use at most 256 MiB of HBM per device.

```python
import math
import jax
import jax.numpy as jnp
from jax import lax

V = 20
C = 128
NX = 1024
NY = 1024
MX = 128
MY = 128
R = 32
FIELDS = 4
ROWS_DEV = 128


def levels(key, extent, split, smallest, largest):
    level, own = 1.0, jax.random.fold_in(key, 6)
    for position, parts in split:
        steps = jnp.exp(jax.random.uniform(jax.random.fold_in(own, position), (parts,), jnp.float32, smallest / len(split), largest / len(split)))
        level = level * jnp.repeat(steps, extent[position] // parts).reshape([-1 if axis == position else 1 for axis in range(len(extent))])
    return level


def scatter_about(key, dims, width, limit, shards=(), held_as=jnp.bfloat16):
    values = jax.random.normal(key, dims, jnp.float32) * width
    if len(shards) > 0:
        values = levels(key, dims, shards, -0.22, 0.18) * values
    return jnp.clip(values, min=-limit, max=limit).astype(held_as)


def setup_inputs(seed: int = 0) -> dict:
    arg_keys = jax.random.split(jax.random.key(seed), 12)
    return {
        "fields": scatter_about(arg_keys[0], (FIELDS, V, NX, NY), 1.0, 6.0, ((0, 4), (2, 8))),
        "lift_weight": scatter_about(arg_keys[1], (V, C), V ** -0.5, 1.25),
        "lift_bias": scatter_about(arg_keys[2], (C,), 0.5, 3.0, (), jnp.float32),
        "first_core": scatter_about(arg_keys[3], (MX, R, R), R ** -0.5, 1.0, ((0, 4),)),
        "second_core": scatter_about(arg_keys[4], (MY, R, R), R ** -0.5, 1.0, ((0, 8),)),
        "input_core": scatter_about(arg_keys[5], (C, R, R), (C * R) ** -0.5, 0.09375, ((0, 4),)),
        "output_core": scatter_about(arg_keys[6], (C, 2, R, R), 0.5, 3.0, ((0, 4),)),
        "skip_weight": scatter_about(arg_keys[7], (C, C), C ** -0.5, 0.5),
        "skip_bias": scatter_about(arg_keys[8], (C,), 0.5, 3.0, (), jnp.float32),
        "out_weight": scatter_about(arg_keys[9], (C, V), C ** -0.5, 0.5),
        "out_bias": scatter_about(arg_keys[10], (V,), 0.5, 3.0, (), jnp.float32),
    }


TWO_PI = 2.0 * math.pi

def wave_pair(waves, points, length):
    phase_step = waves[:, None] * points[None, :] % length
    angles = phase_step.astype(jnp.float32) * (TWO_PI / length)
    return (jnp.cos(angles), jnp.sin(angles))

def width_forward(length, wave_count):
    points = jnp.arange(length, dtype=jnp.int32)
    waves = jnp.arange(wave_count, dtype=jnp.int32)
    cosines, sine_part = wave_pair(points, waves, length)
    stacked = jnp.stack([cosines, -sine_part], axis=1) / math.sqrt(length)
    return stacked.astype(jnp.bfloat16)

def height_forward(row_index, wave_count, length):
    waves = jnp.arange(wave_count, dtype=jnp.int32) - wave_count // 2
    cosines, sine_part = wave_pair(waves, row_index, length)
    upper = jnp.stack([cosines, sine_part], axis=1)
    lower = jnp.stack([-sine_part, cosines], axis=1)
    return (jnp.stack([upper, lower], axis=0) / math.sqrt(length)).astype(jnp.bfloat16)

def height_inverse(row_index, wave_count, length):
    waves = jnp.arange(wave_count, dtype=jnp.int32) - wave_count // 2
    cosines, sine_part = wave_pair(row_index, waves, length)
    upper = jnp.stack([cosines, -sine_part], axis=1)
    lower = jnp.stack([sine_part, cosines], axis=1)
    return (jnp.stack([upper, lower], axis=0) / math.sqrt(length)).astype(jnp.bfloat16)

def width_inverse(waves, length):
    points = jnp.arange(length, dtype=jnp.int32)
    cosines, sine_part = wave_pair(waves, points, length)
    weight = jnp.where(waves == 0, 1.0, 2.0).astype(jnp.float32)[:, None]
    stacked = jnp.stack([cosines * weight, -sine_part * weight], axis=0) / math.sqrt(length)
    return stacked.astype(jnp.bfloat16)

def as_float(value):
    return value.astype(jnp.float32)

def bias_modes(lift_bias, wave_index, length):
    real_row = jnp.where(wave_index == 0, 1.0, 0.0).astype(jnp.float32)[:, None] * (math.sqrt(length) * lift_bias)[None, :]
    return jnp.stack([real_row, jnp.zeros_like(real_row)], axis=0)

def mix_modes(spectrum, mode_factor, input_core, output_core):
    projected = jnp.einsum('qkmc,cbe->qkmbe', as_float(spectrum), as_float(input_core)).astype(jnp.bfloat16)
    carried = jnp.einsum('kmab,qkmbe->qkmae', as_float(mode_factor), as_float(projected)).astype(jnp.bfloat16)
    traced = jnp.einsum('qkmae,osea->qkmso', as_float(carried), as_float(output_core))
    real_part = traced[0, :, :, 0, :] - traced[1, :, :, 1, :]
    imaginary = traced[0, :, :, 1, :] + traced[1, :, :, 0, :]
    return jnp.stack([real_part, imaginary], axis=0).astype(jnp.bfloat16)

def reference(fields, lift_weight, lift_bias, first_core, second_core, input_core, output_core, skip_weight, skip_bias, out_weight, out_bias):
    width_table = width_forward(NY, MY)
    stored = jnp.arange(NX, dtype=jnp.int32)
    row_index = (stored % ROWS_DEV * (NX // ROWS_DEV) + stored // ROWS_DEV).astype(jnp.int32)
    height_table = height_forward(row_index, MX, NX)
    height_back = height_inverse(row_index, MX, NX)
    width_back = width_inverse(jnp.arange(MY, dtype=jnp.int32), NY)
    mode_factor = jnp.einsum('kab,mbd->kmad', as_float(first_core), as_float(second_core)).astype(jnp.bfloat16)
    bias_term = bias_modes(lift_bias, jnp.arange(MY, dtype=jnp.int32), NY)

    def one_field(single):
        lifted = (jnp.einsum('vxy,vc->xyc', as_float(single), as_float(lift_weight)) + lift_bias).astype(jnp.bfloat16)
        field_modes = jnp.einsum('vxy,ypk->xpkv', as_float(single), as_float(width_table)).astype(jnp.bfloat16)
        row_modes = (jnp.einsum('xpkv,vc->xpkc', as_float(field_modes), as_float(lift_weight)) + bias_term).astype(jnp.bfloat16)
        spectrum = jnp.einsum('qkpx,xpmc->qkmc', as_float(height_table), as_float(row_modes)).astype(jnp.bfloat16)
        mixed_modes = mix_modes(spectrum, mode_factor, input_core, output_core)
        col_modes = jnp.einsum('pxqk,qkmc->xpmc', as_float(height_back), as_float(mixed_modes)).astype(jnp.bfloat16)
        spatial = jnp.einsum('xpmc,pmy->xyc', as_float(col_modes), as_float(width_back))
        skip_term = jnp.einsum('xyc,cd->xyd', as_float(lifted), as_float(skip_weight))
        active = jax.nn.gelu(spatial + skip_term + skip_bias, approximate=False).astype(jnp.bfloat16)
        result = jnp.einsum('xyc,cv->vxy', as_float(active), as_float(out_weight)) + out_bias[:, None, None]
        return result.astype(jnp.bfloat16)
    return lax.map(one_field, fields)
```

```python
import functools
import math

import jax
import jax.numpy as jnp
import ml_dtypes
import numpy as np
from jax import lax
from jax.experimental import pallas as pl
from jax.experimental.pallas import tpu as pltpu
from jax.sharding import PartitionSpec as P

NX = 1024
NY = 1024
MX = 128
MY = 128


TWO_PI = 2.0 * math.pi


def wave_pair(waves, points, length):
    phase_step = waves[:, None] * points[None, :] % length
    angles = phase_step.astype(jnp.float32) * (TWO_PI / length)
    return (jnp.cos(angles), jnp.sin(angles))


def width_forward(length, wave_count):
    points = jnp.arange(length, dtype=jnp.int32)
    waves = jnp.arange(wave_count, dtype=jnp.int32)
    cosines, sine_part = wave_pair(points, waves, length)
    stacked = jnp.stack([cosines, -sine_part], axis=1) / math.sqrt(length)
    return stacked.astype(jnp.bfloat16)


def height_forward(row_index, wave_count, length):
    waves = jnp.arange(wave_count, dtype=jnp.int32) - wave_count // 2
    cosines, sine_part = wave_pair(waves, row_index, length)
    upper = jnp.stack([cosines, sine_part], axis=1)
    lower = jnp.stack([-sine_part, cosines], axis=1)
    return (jnp.stack([upper, lower], axis=0) / math.sqrt(length)).astype(jnp.bfloat16)


def height_inverse(row_index, wave_count, length):
    waves = jnp.arange(wave_count, dtype=jnp.int32) - wave_count // 2
    cosines, sine_part = wave_pair(row_index, waves, length)
    upper = jnp.stack([cosines, -sine_part], axis=1)
    lower = jnp.stack([sine_part, cosines], axis=1)
    return (jnp.stack([upper, lower], axis=0) / math.sqrt(length)).astype(jnp.bfloat16)


def width_inverse(waves, length):
    points = jnp.arange(length, dtype=jnp.int32)
    cosines, sine_part = wave_pair(waves, points, length)
    weight = jnp.where(waves == 0, 1.0, 2.0).astype(jnp.float32)[:, None]
    stacked = jnp.stack([cosines * weight, -sine_part * weight], axis=0) / math.sqrt(length)
    return stacked.astype(jnp.bfloat16)


def bias_modes(lift_bias, wave_index, length):
    real_row = (
        jnp.where(wave_index == 0, 1.0, 0.0).astype(jnp.float32)[:, None]
        * (math.sqrt(length) * lift_bias)[None, :]
    )
    return jnp.stack([real_row, jnp.zeros_like(real_row)], axis=0)


def lift_modes(modes, lift_weight, lift_bias, wave_index):
    lifted_modes = jnp.einsum(
        "fabpmv,vc->fabpmc", modes, lift_weight, preferred_element_type=jnp.float32
    )
    return (lifted_modes + bias_modes(lift_bias, wave_index, NY)).astype(jnp.bfloat16)


def grid_rows(stored, row_count, holder_count):
    return stored % row_count * holder_count + stored // row_count


def shards(
    fields,
    lift_weight,
    lift_bias,
    first_core,
    second_core,
    input_core,
    output_core,
    skip_weight,
    skip_bias,
    out_weight,
    out_bias,
):
    mode_count = lax.axis_size("mode")
    core_count = lax.axis_size("cores")
    row_count = fields.shape[2]
    block_size = second_core.shape[0]
    block_start = (lax.axis_index("mode") * core_count + lax.axis_index("cores")) * block_size
    local_waves = block_start + jnp.arange(block_size, dtype=jnp.int32)
    lifted = (
        jnp.einsum("fvxy,vc->fxyc", fields, lift_weight, preferred_element_type=jnp.float32)
        + lift_bias
    ).astype(jnp.bfloat16)
    field_modes = jnp.einsum(
        "fvxy,ypk->fxpkv", fields, width_forward(NY, MY), preferred_element_type=jnp.float32
    ).astype(jnp.bfloat16)
    field_modes = field_modes[:, None]
    gathered = (
        lax.all_gather(first_core, "batch", axis=0, tiled=True),
        lax.all_gather(input_core, "batch", axis=0, tiled=True),
        lax.all_gather(output_core, "batch", axis=0, tiled=True),
    )
    first_whole, input_whole, output_whole = gathered
    mode_factor = jnp.einsum(
        "kab,mbd->kmad", first_whole, second_core, preferred_element_type=jnp.float32
    ).astype(jnp.bfloat16)
    arrived = lax.all_to_all(
        field_modes, ("mode", "cores"), split_axis=4, concat_axis=2, tiled=True
    )
    rows_held = jnp.arange(NX, dtype=jnp.int32)[None, :]
    by_mode = lift_modes(arrived, lift_weight, lift_bias, local_waves)
    lead_rows = rows_held.shape[0]
    side_rows = rows_held.shape[1]
    flat_rows = grid_rows(rows_held.reshape(-1), row_count, mode_count * core_count)
    height_table = height_forward(flat_rows, MX, NX).reshape(2, MX, 2, lead_rows, side_rows)
    spectrum = jnp.einsum(
        "qkpab,fabpmc->fqkmc", height_table, by_mode, preferred_element_type=jnp.float32
    ).astype(jnp.bfloat16)
    projected = jnp.einsum(
        "fqkmc,cbe->fqkmbe", spectrum, input_whole, preferred_element_type=jnp.float32
    ).astype(jnp.bfloat16)
    carried = jnp.einsum(
        "kmab,fqkmbe->fqkmae", mode_factor, projected, preferred_element_type=jnp.float32
    ).astype(jnp.bfloat16)
    traced = jnp.einsum(
        "fqkmae,osea->fqkmso", carried, output_whole, preferred_element_type=jnp.float32
    )
    real_part = traced[:, 0, :, :, 0, :] - traced[:, 1, :, :, 1, :]
    imaginary = traced[:, 0, :, :, 1, :] + traced[:, 1, :, :, 0, :]
    mixed_modes = jnp.stack([real_part, imaginary], axis=1).astype(jnp.bfloat16)
    height_back = height_inverse(flat_rows, MX, NX).reshape(2, lead_rows, side_rows, 2, MX)
    col_modes = jnp.einsum(
        "pabqk,fqkmc->fabpmc", height_back, mixed_modes, preferred_element_type=jnp.float32
    ).astype(jnp.bfloat16)
    returned = lax.all_to_all(col_modes, ("mode", "cores"), split_axis=2, concat_axis=4, tiled=True)
    waves_held = jnp.arange(MY, dtype=jnp.int32)
    width_back = width_inverse(waves_held, NY)
    spatial = jnp.einsum(
        "fxpmc,pmy->fxyc", returned[:, 0], width_back, preferred_element_type=jnp.float32
    )
    skip_term = jnp.einsum("fxyc,cd->fxyd", lifted, skip_weight, preferred_element_type=jnp.float32)
    active = jax.nn.gelu(spatial + skip_term + skip_bias, approximate=False).astype(jnp.bfloat16)
    result = (
        jnp.einsum("fxyc,cv->fvxy", active, out_weight, preferred_element_type=jnp.float32)
        + out_bias[:, None, None]
    )
    return result.astype(jnp.bfloat16)


def cyclic_rows(row_count, holders):
    return (np.arange(row_count)[None, :] * holders + np.arange(holders)[:, None]).reshape(-1)


def host_pair(waves, points, length):
    steps = np.asarray(waves)[:, None] * np.asarray(points)[None, :] % length
    angles = steps.astype(np.float32) * np.float32(TWO_PI / length)
    return np.cos(angles), np.sin(angles)


def dense(a, b, contract=((1,), (0,))):
    return lax.dot_general(a, b, (contract, ((), ())), preferred_element_type=jnp.float32)


MESH = pl.DeviceIdType.MESH
WAVES = 16
SLOTS = 32
EIGHT = 8
CHUNKS = 4
LANES = 512


def whole(a):
    return pl.BlockSpec(a.shape, lambda *_: (0,) * a.ndim)


def mix_kernel(
    arrived, height, place, bias_modes_row, inner, second, first, first_spread, outer, spread,
    mixed, stacked, placed, inner_wide, turned_inner, weights, rows, blocks, closing, carried, turned,
):
    holders, lead, flat = arrived.shape
    waves = lead // 2
    variables = stacked.shape[0] // waves
    row_count = flat // variables
    kx_count = height.shape[0] // 2
    rank = first.shape[1]
    channels = outer.shape[0] // 2
    pairs = waves // 2
    wide = 4 * rank
    slots = inner.shape[1] // rank
    packs = kx_count // EIGHT

    for d in range(holders):
        for p in range(2):
            for v in range(variables):
                stacked[v * waves:(v + 1) * waves, (d * 2 + p) * row_count:(d * 2 + p + 1) * row_count] = (
                    arrived[d, p * waves:(p + 1) * waves, v * row_count:(v + 1) * row_count]
                )
    by = dense(height[...], stacked[...], ((1,), (1,))).astype(jnp.bfloat16)
    placed[...] = (
        dense(by[:kx_count], place[0]) + dense(by[kx_count:], place[1]) + bias_modes_row[...]
    ).astype(jnp.bfloat16)

    for part in range(slots // 4):
        inner_wide[:, part * 4 * wide:(part + 1) * 4 * wide] = dense(
            inner[:, part * wide:(part + 1) * wide], spread[:wide, :4 * wide]
        ).astype(jnp.bfloat16)

    down = lax.broadcasted_iota(jnp.int32, (rank * EIGHT, rank * EIGHT), 0) % EIGHT
    across = lax.broadcasted_iota(jnp.int32, (rank * EIGHT, rank * EIGHT), 1) % EIGHT
    same = down == across

    def block_step(k, carry):
        start = pl.multiple_of(k * rank * EIGHT, rank * EIGHT)
        full = dense(first[pl.ds(start, rank * EIGHT), :], first_spread[...])
        blocks[k] = jnp.where(same, full, 0.0).astype(jnp.bfloat16)
        return carry

    lax.fori_loop(0, packs, block_step, 0)

    lanes = lax.broadcasted_iota(jnp.int32, (channels, 8 * wide), 1)
    part_of = lanes // rank % 2
    wave_of = lanes // (2 * rank) % 2
    for part in range(rank // 8):
        real = dense(outer[:channels, part * 8 * rank:(part + 1) * 8 * rank], spread[...])
        imaginary = dense(outer[channels:, part * 8 * rank:(part + 1) * 8 * rank], spread[...])
        for r in range(2):
            value = jnp.where(part_of == 0, imaginary, real) if r else jnp.where(part_of == 0, real, -imaginary)
            for m in range(2):
                closing[(m * 2 + r) * channels:(m * 2 + r + 1) * channels, part * 8 * wide:(part + 1) * 8 * wide] = (
                    jnp.where(wave_of == m, value, 0.0).astype(jnp.bfloat16)
                )

    turned_inner[...] = jnp.zeros_like(turned_inner)
    group_of = lax.broadcasted_iota(jnp.int32, (SLOTS, wide), 1) // rank

    def pair_step(j, carry):
        start = pl.multiple_of(j * 2 * rank, 2 * rank)
        column = pl.ds(pl.multiple_of(j * wide, wide), wide)
        joined = dense(second[pl.ds(start, 2 * rank), :], inner_wide[...])
        for m in range(2):
            for v in range(slots):
                turned_inner[m, :, v, :] = joined[m * rank:(m + 1) * rank, v * wide:(v + 1) * wide]
        for m in range(2):
            for b in range(rank):
                value = turned_inner[m, b]
                for q in range(2):
                    weights[(q * 2 + m) * SLOTS:(q * 2 + m + 1) * SLOTS, b * wide:(b + 1) * wide] = jnp.where(
                        group_of == m * 2 + q, value, 0.0
                    ).astype(jnp.bfloat16)
        own = placed[:, column]
        for part in range(rank // 8):
            got = dense(own, weights[:, part * 8 * wide:(part + 1) * 8 * wide])
            for k in range(packs):
                rows[k, part * 64:(part + 1) * 64, column] = jnp.concatenate(
                    [got[k * EIGHT:(k + 1) * EIGHT, b * wide:(b + 1) * wide] for b in range(8)], axis=0
                ).astype(jnp.bfloat16)
        return carry

    lax.fori_loop(0, pairs, pair_step, 0)

    def first_step(k, carry):
        here = pl.ds(pl.multiple_of(k * 2 * EIGHT, 2 * EIGHT), 2 * EIGHT)
        for part in range(pairs // 2):
            one, two = [
                dense(blocks[2 * k + i], rows[2 * k + i, :, part * 2 * wide:(part + 1) * 2 * wide]) for i in range(2)
            ]
            for j in range(2):
                side = slice(j * wide, (j + 1) * wide)
                for a in range(rank):
                    level = slice(a * EIGHT, (a + 1) * EIGHT)
                    carried[part * 2 + j, here, a * wide:(a + 1) * wide] = jnp.concatenate(
                        [one[level, side], two[level, side]], axis=0
                    ).astype(jnp.bfloat16)
        return carry

    lax.fori_loop(0, packs // 2, first_step, 0)

    for part in range(pairs // 2):
        both = carried[part * 2:part * 2 + 2].reshape(2 * kx_count, rank * wide)
        got = dense(closing[...], both, ((1,), (1,)))
        for m in range(2):
            for r in range(2):
                for j in range(2):
                    turned[:, (part * 2 + j) * 2 + m, r * kx_count:(r + 1) * kx_count] = got[
                        (m * 2 + r) * channels:(m * 2 + r + 1) * channels, j * kx_count:(j + 1) * kx_count
                    ]
    mixed[...] = turned[...].astype(jnp.bfloat16)


def mix(arrived, height, place, bias_row, inner, second, first, first_spread, outer, spread):
    holders, lead, flat = arrived.shape
    waves = lead // 2
    kx2, depth = height.shape
    rank = first.shape[1]
    channels = outer.shape[0] // 2
    wide = 4 * rank
    slots = inner.shape[1] // rank
    packs = kx2 // 2 // EIGHT
    operands = (arrived, height, place, bias_row, inner, second, first, first_spread, outer, spread)
    return pl.pallas_call(
        mix_kernel,
        in_specs=[pl.BlockSpec(memory_space=pltpu.VMEM) for _ in operands],
        out_specs=pl.BlockSpec(memory_space=pltpu.VMEM),
        out_shape=jax.ShapeDtypeStruct((channels, waves, kx2), jnp.bfloat16),
        scratch_shapes=[
            pltpu.VMEM((place.shape[1], depth), jnp.bfloat16),
            pltpu.VMEM((kx2 // 2, waves // 2 * wide), jnp.bfloat16),
            pltpu.VMEM((rank, slots * wide), jnp.bfloat16),
            pltpu.VMEM((2, rank, SLOTS, wide), jnp.float32),
            pltpu.VMEM((4 * SLOTS, rank * wide), jnp.bfloat16),
            pltpu.VMEM((packs, rank * EIGHT, waves // 2 * wide), jnp.bfloat16),
            pltpu.VMEM((packs, rank * EIGHT, rank * EIGHT), jnp.bfloat16),
            pltpu.VMEM((4 * channels, rank * wide), jnp.bfloat16),
            pltpu.VMEM((waves // 2, kx2 // 2, rank * wide), jnp.bfloat16),
            pltpu.VMEM((channels, waves, kx2), jnp.float32),
        ],
        compiler_params=pltpu.CompilerParams(vmem_limit_bytes=56 * 2**20),
        name="mix",
    )(*operands)


def gelu(h):
    return h * (0.5 + 0.5 * lax.erf(h * (1.0 / math.sqrt(2.0))))


def finish_kernel(
    mixed, back, fields, width, skip, bias, closing, out_bias,
    result, gathered, source, cols, total, send, recv,
):
    channels, waves, kx2 = mixed.shape
    variables, row_count, points = fields.shape
    share = channels // CHUNKS
    depth = share * EIGHT
    half = share // 2
    mode, batch, core = lax.axis_index("mode"), lax.axis_index("batch"), lax.axis_index("cores")
    near = (mode + 1 - 2 * (mode % 2), batch, core)
    by_x = ((mode + 2) % 4, batch, core)
    by_y = (mode, batch, 1 - core)

    def owner(device):
        return device[0] * 2 + device[2]

    me = owner((mode, batch, core))
    at_x, at_y = owner(by_x), owner(by_y)
    across = owner((by_x[0], batch, by_y[2]))

    barrier = pltpu.get_barrier_semaphore()
    for device in (near, by_x, by_y):
        pl.semaphore_signal(barrier, inc=1, device_id=device, device_id_type=MESH)
    pl.semaphore_wait(barrier, 3)

    def piece(holder, first, count):
        return gathered.at[pl.ds(first, count), pl.ds(pl.multiple_of(holder * waves, waves), waves), :]

    def copy(g, kind):
        low = g * share
        own = mixed.at[pl.ds(low, share)]
        home = piece(me, low, share)
        x_all, y_all = piece(at_x, low, share), piece(at_y, low, share)
        x_low, y_high = piece(at_x, low, half), piece(at_y, low + half, half)
        d_low, d_high = piece(across, low, half), piece(across, low + half, half)
        from_, to, device = (
            (own, home, near), (own, home, by_x), (own, home, by_y),
            (x_all, x_all, near), (y_all, y_all, near),
            (x_low, x_low, by_y), (y_high, y_high, by_x),
            (d_low, d_low, near), (d_high, d_high, near),
        )[kind]
        return pltpu.make_async_remote_copy(
            src_ref=from_, dst_ref=to, send_sem=send.at[g, kind], recv_sem=recv.at[g, kind],
            device_id=device, device_id_type=MESH,
        )

    def begin(g, kinds):
        for kind in kinds:
            copy(g, kind).start()

    def came(g, kinds):
        for kind in kinds:
            copy(g, kind).wait_recv()

    def relay(g):
        came(g, (1, 2))
        begin(g, (5, 6, 3, 4))
        if g + 1 < CHUNKS:
            begin(g + 1, (1, 2, 0))

    def relay_last(g):
        came(g, (5, 6))
        begin(g, (7, 8))

    begin(0, (1, 2, 0))
    gathered[:, pl.ds(pl.multiple_of(me * waves, waves), waves), :] = mixed[...]
    for x in range(row_count // EIGHT // 2):
        rows = fields[:, x * 2 * EIGHT:(x + 1) * 2 * EIGHT, :]
        for h in range(2):
            source[x * 2 + h] = rows[:, h * EIGHT:(h + 1) * EIGHT, :].reshape(variables * EIGHT, points)
    relay(0)
    relay_last(0)

    def turn(g):
        def step(c, carry):
            both = gathered[pl.ds(g * share + 2 * c, 2)].reshape(2 * waves * 8, kx2)
            got = dense(back[...], both, ((1,), (1,)))
            place = pl.ds(pl.multiple_of(c * 2 * EIGHT, 2 * EIGHT), 2 * EIGHT)
            size = got.shape[1] // 2
            for p in range(2):
                for x in range(row_count // EIGHT):
                    rows = got[p * row_count + x * EIGHT:p * row_count + (x + 1) * EIGHT, :]
                    cols[x, place, p * size:(p + 1) * size] = jnp.concatenate(
                        [rows[:, :size], rows[:, size:]], axis=0
                    ).astype(jnp.bfloat16)
            return carry

        lax.fori_loop(0, share // 2, step, 0)

    def finish_rows(g, low, high):
        part = slice(g * depth, (g + 1) * depth)

        def step(i, carry):
            for lane in range(points // LANES):
                lanes = slice(lane * LANES, (lane + 1) * LANES)
                done = []
                for h in range(2):
                    x = 2 * i + h
                    height = (
                        dense(cols[x], width[:, lanes]) + dense(skip[part, :], source[x, :, lanes]) + bias[part, :]
                    )
                    active = gelu(height).astype(jnp.bfloat16)
                    got = dense(closing[:, part], active)
                    got = got + (out_bias[...] if g == 0 else total[x, :, lanes])
                    if g + 1 < CHUNKS:
                        total[x, :, lanes] = got
                    else:
                        done.append(got.reshape(variables, EIGHT, LANES))
                if done:
                    place = pl.ds(pl.multiple_of(i * 2 * EIGHT, 2 * EIGHT), 2 * EIGHT)
                    result[:, place, lanes] = jnp.concatenate(done, axis=1).astype(jnp.bfloat16)
            return carry

        lax.fori_loop(low, high, step, 0)

    steps = row_count // EIGHT // 2
    for g in range(CHUNKS):
        came(g, (0, 3, 4, 7, 8))
        turn(g)
        if g + 1 < CHUNKS:
            finish_rows(g, 0, steps // 4)
            relay(g + 1)
            finish_rows(g, steps // 4, 5 * steps // 8)
            relay_last(g + 1)
            finish_rows(g, 5 * steps // 8, steps)
        else:
            finish_rows(g, 0, steps)
    for g in range(CHUNKS):
        for kind in range(9):
            copy(g, kind).wait_send()


def finish(mixed, back, fields, width, skip, bias, closing, out_bias):
    channels, waves, kx2 = mixed.shape
    variables, row_count, points = fields.shape
    operands = (mixed, back, fields, width, skip, bias, closing, out_bias)
    share = channels // CHUNKS
    blocks = row_count // EIGHT
    return pl.pallas_call(
        finish_kernel,
        in_specs=[pl.BlockSpec(memory_space=pltpu.VMEM) for _ in operands],
        out_specs=pl.BlockSpec(memory_space=pltpu.VMEM),
        out_shape=jax.ShapeDtypeStruct(fields.shape, jnp.bfloat16),
        scratch_shapes=[
            pltpu.VMEM((channels, 8 * waves, kx2), jnp.bfloat16),
            pltpu.VMEM((blocks, variables * EIGHT, points), jnp.bfloat16),
            pltpu.VMEM((blocks, share * EIGHT, width.shape[0]), jnp.bfloat16),
            pltpu.VMEM((blocks, variables * EIGHT, points), jnp.float32),
            pltpu.SemaphoreType.DMA((CHUNKS, 9)),
            pltpu.SemaphoreType.DMA((CHUNKS, 9)),
        ],
        compiler_params=pltpu.CompilerParams(
            collective_id=0, has_side_effects=True, vmem_limit_bytes=60 * 2**20
        ),
        name="finish",
    )(*operands)


def gather_factors(first_core, input_core, output_core):
    count, rank, _ = first_core.shape
    first_core = first_core.reshape(count // EIGHT, EIGHT, rank, rank).transpose(0, 2, 1, 3)
    output_core = output_core.transpose(1, 0, 3, 2)
    flat = jnp.concatenate(
        [first_core.reshape(-1), input_core.reshape(-1), output_core.reshape(-1)]
    ).reshape(-1, 128)
    gathered = lax.all_gather(flat, "batch", axis=0, tiled=False)
    parts = gathered.shape[0]
    size = first_core.size
    gathered = gathered.reshape(parts, -1)
    first = gathered[:, :size].reshape(-1, rank)
    inner = gathered[:, size:2 * size].reshape(parts * count, rank * rank)
    outer = gathered[:, 2 * size:].reshape(parts, 2, count, rank * rank).transpose(1, 0, 2, 3)
    return first, inner, outer.reshape(2 * parts * count, rank * rank)


def fast_shards(
    fields, lift_weight, lift_bias, first_core, second_core, input_core, output_core,
    skip_weight, skip_bias, out_weight, out_bias,
):
    holders = lax.axis_size("mode") * lax.axis_size("cores")
    waves, rank, _ = second_core.shape
    _, variables, row_count, points = fields.shape
    channels = lift_weight.shape[1]
    fields = fields[0]
    me = lax.axis_index("mode") * lax.axis_size("cores") + lax.axis_index("cores")

    cosines, sines = host_pair(np.arange(MY), np.arange(points), points)
    root = math.sqrt(points)
    forward = np.stack([cosines, -sines], 0).reshape(2, holders, waves, points).transpose(1, 0, 2, 3)
    forward = jnp.asarray((forward.reshape(2 * MY, points) / root).astype(np.float32)).astype(jnp.bfloat16)
    weight = np.where(np.arange(MY) == 0, 1.0, 2.0).astype(np.float32)[:, None]
    width = np.concatenate([cosines * weight, -sines * weight], 0) / root
    width = jnp.asarray(width.astype(ml_dtypes.bfloat16))
    order = cyclic_rows(row_count, holders)
    root = math.sqrt(NX)
    cosines, sines = host_pair(np.arange(MX) - MX // 2, order, NX)
    cosines, sines = [t.reshape(MX, holders, row_count) / root for t in (cosines, sines)]
    upper = np.stack([cosines, sines], 2)
    lower = np.stack([-sines, cosines], 2)
    height = np.stack([upper, lower], 0).reshape(2 * MX, -1).astype(ml_dtypes.bfloat16)
    real_part = np.asarray(height, np.float32).reshape(2 * MX, holders, 2, row_count)[:, :, 0]
    row_sum = real_part.sum((1, 2), dtype=np.float64).astype(np.float32)
    cos_t, sin_t = [t.transpose(1, 2, 0) for t in (cosines, sines)]
    up = np.concatenate([cos_t, -sin_t], 2)
    low = np.concatenate([sin_t, cos_t], 2)
    back_rows = jnp.asarray(np.concatenate([up, low], 1).astype(ml_dtypes.bfloat16))
    back_rows = lax.dynamic_index_in_dim(back_rows, me, 0, keepdims=False)
    pairs = waves // 2
    place = np.zeros((2, variables, waves, pairs, 2, 2, SLOTS), np.float32)
    for q in range(2):
        for v in range(variables):
            for m in range(waves):
                place[q, v, m, m // 2, q, m % 2, v] = 1.0
    place = jnp.asarray(place.reshape(2, variables * waves, -1).astype(ml_dtypes.bfloat16))
    bias_row = np.zeros((MX, pairs, 2, 2, SLOTS), np.float32)
    bias_row[:, 0, :, 0, variables] = row_sum.reshape(2, MX).T
    bias_row = jnp.asarray(bias_row.reshape(MX, -1)) * (me == 0).astype(jnp.float32)
    first_spread = jnp.asarray(np.repeat(np.eye(rank), EIGHT, axis=1).astype(ml_dtypes.bfloat16))
    spread = np.eye(8)[:, None, :, None, None] * np.eye(rank)[None, :, None, None, :] * np.ones((1, 1, 1, 4, 1))
    spread = jnp.asarray(spread.reshape(8 * rank, 32 * rank).astype(ml_dtypes.bfloat16))

    first, inner, outer = gather_factors(first_core, input_core, output_core)
    modes = jnp.einsum(
        "ry,vxy->rvx", forward, fields, preferred_element_type=jnp.float32
    ).astype(jnp.bfloat16)
    modes = modes.reshape(holders, 2 * waves, variables * row_count)
    arrived = lax.all_to_all(modes, ("mode", "cores"), split_axis=0, concat_axis=0, tiled=True)

    used = (variables + 4) // 4 * 4
    lift = jnp.concatenate(
        [lift_weight, (math.sqrt(points) * lift_bias).astype(jnp.bfloat16)[None],
         jnp.zeros((used - variables - 1, channels), jnp.bfloat16)], 0
    )
    inner = jnp.einsum(
        "vc,cde->dve", lift, inner.reshape(channels, rank, rank), preferred_element_type=jnp.float32
    ).astype(jnp.bfloat16).reshape(rank, used * rank)
    mixed = mix(
        arrived, jnp.asarray(height), place, bias_row, inner, second_core.reshape(waves * rank, rank),
        first, first_spread, outer, spread,
    )

    skip_wide = skip_weight.astype(jnp.float32)
    direct = jnp.dot(lift_weight.astype(jnp.float32), skip_wide, precision="highest")
    total_bias = jnp.dot(lift_bias, skip_wide, precision="highest") + skip_bias
    rows_eye = jnp.eye(EIGHT, dtype=jnp.float32)
    skip = (direct.T[:, None, :, None] * rows_eye[None, :, None, :]).astype(jnp.bfloat16)
    skip = skip.reshape(channels * EIGHT, variables * EIGHT)
    closing = out_weight.T[:, None, :, None] * rows_eye.astype(jnp.bfloat16)[None, :, None, :]
    closing = closing.reshape(variables * EIGHT, channels * EIGHT)
    bias = jnp.repeat(total_bias, EIGHT)[:, None]
    last_bias = jnp.repeat(out_bias, EIGHT)[:, None]
    return finish(mixed, back_rows, fields, width, skip, bias, closing, last_bias)[None]


def solution(mesh):
    placed = (
        P("batch", None, ("mode", "cores"), None),
        P(),
        P(),
        P("batch", None, None),
        P(("mode", "cores"), None, None),
        P("batch", None, None),
        P("batch", None, None, None),
        P(),
        P(),
        P(),
        P(),
    )
    fits = (
        mesh.shape["mode"] == 4 and mesh.shape["cores"] == 2 and MY // 8 == WAVES
        and MX // mesh.shape["batch"] % EIGHT == 0 and NX // 8 == 128
    )
    return jax.shard_map(
        fast_shards if fits else shards,
        mesh=mesh,
        in_specs=placed,
        out_specs=P("batch", None, ("mode", "cores"), None),
        check_vma=False,
    )
```

```python
import functools
import math

import jax
import jax.numpy as jnp
import ml_dtypes
import numpy as np
from jax import lax
from jax.experimental import pallas as pl
from jax.experimental.pallas import tpu as pltpu
from jax.sharding import PartitionSpec as P

NX = 1024
NY = 1024
MX = 128
MY = 128


TWO_PI = 2.0 * math.pi


def wave_pair(waves, points, length):
    phase_step = waves[:, None] * points[None, :] % length
    angles = phase_step.astype(jnp.float32) * (TWO_PI / length)
    return (jnp.cos(angles), jnp.sin(angles))


def width_forward(length, wave_count):
    points = jnp.arange(length, dtype=jnp.int32)
    waves = jnp.arange(wave_count, dtype=jnp.int32)
    cosines, sine_part = wave_pair(points, waves, length)
    stacked = jnp.stack([cosines, -sine_part], axis=1) / math.sqrt(length)
    return stacked.astype(jnp.bfloat16)


def height_forward(row_index, wave_count, length):
    waves = jnp.arange(wave_count, dtype=jnp.int32) - wave_count // 2
    cosines, sine_part = wave_pair(waves, row_index, length)
    upper = jnp.stack([cosines, sine_part], axis=1)
    lower = jnp.stack([-sine_part, cosines], axis=1)
    return (jnp.stack([upper, lower], axis=0) / math.sqrt(length)).astype(jnp.bfloat16)


def height_inverse(row_index, wave_count, length):
    waves = jnp.arange(wave_count, dtype=jnp.int32) - wave_count // 2
    cosines, sine_part = wave_pair(row_index, waves, length)
    upper = jnp.stack([cosines, -sine_part], axis=1)
    lower = jnp.stack([sine_part, cosines], axis=1)
    return (jnp.stack([upper, lower], axis=0) / math.sqrt(length)).astype(jnp.bfloat16)


def width_inverse(waves, length):
    points = jnp.arange(length, dtype=jnp.int32)
    cosines, sine_part = wave_pair(waves, points, length)
    weight = jnp.where(waves == 0, 1.0, 2.0).astype(jnp.float32)[:, None]
    stacked = jnp.stack([cosines * weight, -sine_part * weight], axis=0) / math.sqrt(length)
    return stacked.astype(jnp.bfloat16)


def bias_modes(lift_bias, wave_index, length):
    real_row = (
        jnp.where(wave_index == 0, 1.0, 0.0).astype(jnp.float32)[:, None]
        * (math.sqrt(length) * lift_bias)[None, :]
    )
    return jnp.stack([real_row, jnp.zeros_like(real_row)], axis=0)


def lift_modes(modes, lift_weight, lift_bias, wave_index):
    lifted_modes = jnp.einsum(
        "fabpmv,vc->fabpmc", modes, lift_weight, preferred_element_type=jnp.float32
    )
    return (lifted_modes + bias_modes(lift_bias, wave_index, NY)).astype(jnp.bfloat16)


def grid_rows(stored, row_count, holder_count):
    return stored % row_count * holder_count + stored // row_count


def shards(
    fields,
    lift_weight,
    lift_bias,
    first_core,
    second_core,
    input_core,
    output_core,
    skip_weight,
    skip_bias,
    out_weight,
    out_bias,
):
    mode_count = lax.axis_size("mode")
    core_count = lax.axis_size("cores")
    row_count = fields.shape[2]
    block_size = second_core.shape[0]
    block_start = (lax.axis_index("mode") * core_count + lax.axis_index("cores")) * block_size
    local_waves = block_start + jnp.arange(block_size, dtype=jnp.int32)
    lifted = (
        jnp.einsum("fvxy,vc->fxyc", fields, lift_weight, preferred_element_type=jnp.float32)
        + lift_bias
    ).astype(jnp.bfloat16)
    field_modes = jnp.einsum(
        "fvxy,ypk->fxpkv", fields, width_forward(NY, MY), preferred_element_type=jnp.float32
    ).astype(jnp.bfloat16)
    field_modes = field_modes[:, None]
    gathered = (
        lax.all_gather(first_core, "batch", axis=0, tiled=True),
        lax.all_gather(input_core, "batch", axis=0, tiled=True),
        lax.all_gather(output_core, "batch", axis=0, tiled=True),
    )
    first_whole, input_whole, output_whole = gathered
    mode_factor = jnp.einsum(
        "kab,mbd->kmad", first_whole, second_core, preferred_element_type=jnp.float32
    ).astype(jnp.bfloat16)
    arrived = lax.all_to_all(
        field_modes, ("mode", "cores"), split_axis=4, concat_axis=2, tiled=True
    )
    rows_held = jnp.arange(NX, dtype=jnp.int32)[None, :]
    by_mode = lift_modes(arrived, lift_weight, lift_bias, local_waves)
    lead_rows = rows_held.shape[0]
    side_rows = rows_held.shape[1]
    flat_rows = grid_rows(rows_held.reshape(-1), row_count, mode_count * core_count)
    height_table = height_forward(flat_rows, MX, NX).reshape(2, MX, 2, lead_rows, side_rows)
    spectrum = jnp.einsum(
        "qkpab,fabpmc->fqkmc", height_table, by_mode, preferred_element_type=jnp.float32
    ).astype(jnp.bfloat16)
    projected = jnp.einsum(
        "fqkmc,cbe->fqkmbe", spectrum, input_whole, preferred_element_type=jnp.float32
    ).astype(jnp.bfloat16)
    carried = jnp.einsum(
        "kmab,fqkmbe->fqkmae", mode_factor, projected, preferred_element_type=jnp.float32
    ).astype(jnp.bfloat16)
    traced = jnp.einsum(
        "fqkmae,osea->fqkmso", carried, output_whole, preferred_element_type=jnp.float32
    )
    real_part = traced[:, 0, :, :, 0, :] - traced[:, 1, :, :, 1, :]
    imaginary = traced[:, 0, :, :, 1, :] + traced[:, 1, :, :, 0, :]
    mixed_modes = jnp.stack([real_part, imaginary], axis=1).astype(jnp.bfloat16)
    height_back = height_inverse(flat_rows, MX, NX).reshape(2, lead_rows, side_rows, 2, MX)
    col_modes = jnp.einsum(
        "pabqk,fqkmc->fabpmc", height_back, mixed_modes, preferred_element_type=jnp.float32
    ).astype(jnp.bfloat16)
    returned = lax.all_to_all(col_modes, ("mode", "cores"), split_axis=2, concat_axis=4, tiled=True)
    waves_held = jnp.arange(MY, dtype=jnp.int32)
    width_back = width_inverse(waves_held, NY)
    spatial = jnp.einsum(
        "fxpmc,pmy->fxyc", returned[:, 0], width_back, preferred_element_type=jnp.float32
    )
    skip_term = jnp.einsum("fxyc,cd->fxyd", lifted, skip_weight, preferred_element_type=jnp.float32)
    active = jax.nn.gelu(spatial + skip_term + skip_bias, approximate=False).astype(jnp.bfloat16)
    result = (
        jnp.einsum("fxyc,cv->fvxy", active, out_weight, preferred_element_type=jnp.float32)
        + out_bias[:, None, None]
    )
    return result.astype(jnp.bfloat16)


def cyclic_rows(row_count, holders):
    return (np.arange(row_count)[None, :] * holders + np.arange(holders)[:, None]).reshape(-1)


def host_pair(waves, points, length):
    steps = np.asarray(waves)[:, None] * np.asarray(points)[None, :] % length
    angles = steps.astype(np.float32) * np.float32(TWO_PI / length)
    return np.cos(angles), np.sin(angles)


def dense(a, b, contract=((1,), (0,))):
    return lax.dot_general(a, b, (contract, ((), ())), preferred_element_type=jnp.float32)


MESH = pl.DeviceIdType.MESH
WAVES = 16
SLOTS = 32
EIGHT = 8
CHUNKS = (64, 64)
STARTS = (0, 64)
LANES = 512
ROWS = 256
PARTS = 2


def whole(a):
    return pl.BlockSpec(a.shape, lambda *_: (0,) * a.ndim)


def mix_kernel(
    fields_far, forward, first_own, inner_own, outer_own, height, place, bias_row, second, first_spread, spread,
    mixed, fields, modes, arrived, first, inner, outer, stacked, placed, inner_wide, turned_inner, weights, rows,
    blocks, closing, carried, turned, load, send_plane, recv_plane, send_near, recv_near, send_modes, recv_modes,
):
    variables, row_count, points = fields.shape
    holders, lead, flat = arrived.shape
    waves = lead // 2
    kx_count = height.shape[0] // 2
    planes = first.shape[0]
    rank = inner.shape[1]
    channels = mixed.shape[0]
    pairs = waves // 2
    wide = 4 * rank
    slots = inner.shape[2] // rank
    packs = kx_count // EIGHT
    share = variables // PARTS
    mode, batch, core = lax.axis_index("mode"), lax.axis_index("batch"), lax.axis_index("cores")
    me = mode * 2 + core
    near = (mode + 1 - 2 * (mode % 2), batch, core)

    def load_part(c):
        here = pl.ds(c * share, share)
        return pltpu.make_async_copy(fields_far.at[here], fields.at[here], load.at[c])

    for c in range(PARTS):
        load_part(c).start()

    def flip(bit, change):
        return bit + change - 2 * bit * change

    def peer(t):
        chip, side, line = flip(mode // 2, t // 4), flip(mode % 2, t // 2 % 2), flip(core, t % 2)
        return (chip * 2 + side, batch, line), chip * 4 + side * 2 + line

    def plane(step):
        return (mode, (batch + step) % planes, core)

    barrier = pltpu.get_barrier_semaphore()
    greeted = [peer(t)[0] for t in range(1, holders)] + [plane(step) for step in range(1, planes)]
    for device in greeted:
        pl.semaphore_signal(barrier, inc=1, device_id=device, device_id_type=MESH)
    pl.semaphore_wait(barrier, len(greeted))

    shards_own = (first_own, inner_own, outer_own)
    shards_all = (first, inner, outer)

    def half(n):
        size = shards_own[n].shape[0] // 2
        return pl.ds(pl.multiple_of((mode % 2) * size, size), size)

    def plane_copy(step, n):
        return pltpu.make_async_remote_copy(
            src_ref=shards_own[n].at[half(n)], dst_ref=shards_all[n].at[batch, half(n)],
            send_sem=send_plane.at[step - 1, n], recv_sem=recv_plane.at[step - 1, n],
            device_id=plane(step), device_id_type=MESH,
        )

    def near_copy(step, n):
        held = shards_all[n].at[(batch + planes - step) % planes, half(n)]
        return pltpu.make_async_remote_copy(
            src_ref=held, dst_ref=held, send_sem=send_near.at[step - 1, n], recv_sem=recv_near.at[step - 1, n],
            device_id=near, device_id_type=MESH,
        )

    def modes_copy(t, c):
        device, index = peer(t)
        lanes = pl.ds(c * share * row_count, share * row_count)
        return pltpu.make_async_remote_copy(
            src_ref=modes.at[index, :, lanes], dst_ref=arrived.at[me, :, lanes],
            send_sem=send_modes.at[t - 1, c], recv_sem=recv_modes.at[t - 1, c],
            device_id=device, device_id_type=MESH,
        )

    for n in range(3):
        for step in range(1, planes):
            plane_copy(step, n).start()
    for n in range(3):
        shards_all[n][batch] = shards_own[n][...]

    for c in range(PARTS):
        load_part(c).wait()
        for v in range(c * share, (c + 1) * share, 2):
            both = fields[v:v + 2].reshape(2 * row_count, points)
            got = dense(forward[...], both, ((1,), (1,))).astype(jnp.bfloat16)
            modes[:, :, v * row_count:(v + 2) * row_count] = got.reshape(holders, lead, 2 * row_count)
        for t in range(holders - 1, 0, -1):
            modes_copy(t, c).start()
    arrived[me] = modes[me]

    for n in range(2):
        for step in range(1, planes):
            plane_copy(step, n).wait_recv()
            near_copy(step, n).start()
    for n in range(2):
        for step in range(1, planes):
            near_copy(step, n).wait_recv()

    total = inner[0].astype(jnp.float32)
    for z in range(1, planes):
        total = total + inner[z].astype(jnp.float32)
    total = total.astype(jnp.bfloat16)
    for part in range(slots // 4):
        inner_wide[:, part * 4 * wide:(part + 1) * 4 * wide] = dense(
            total[:, part * wide:(part + 1) * wide], spread[:wide, :4 * wide]
        ).astype(jnp.bfloat16)

    down = lax.broadcasted_iota(jnp.int32, (rank * EIGHT, rank * EIGHT), 0) % EIGHT
    along = lax.broadcasted_iota(jnp.int32, (rank * EIGHT, rank * EIGHT), 1) % EIGHT
    same = down == along
    for z in range(planes):
        for k in range(packs // planes):
            full = dense(first[z], first_spread[k])
            blocks[z * (packs // planes) + k] = jnp.where(same, full, 0.0).astype(jnp.bfloat16)

    turned_inner[...] = jnp.zeros_like(turned_inner)
    group_of = lax.broadcasted_iota(jnp.int32, (SLOTS, wide), 1) // rank

    def weight_step(j, carry):
        start = pl.multiple_of(j * 2 * rank, 2 * rank)
        joined = dense(second[pl.ds(start, 2 * rank), :], inner_wide[...])
        for m in range(2):
            for v in range(slots):
                turned_inner[m, :, v, :] = joined[m * rank:(m + 1) * rank, v * wide:(v + 1) * wide]
        for m in range(2):
            for b in range(rank):
                value = turned_inner[m, b]
                for q in range(2):
                    weights[j, (q * 2 + m) * SLOTS:(q * 2 + m + 1) * SLOTS, b * wide:(b + 1) * wide] = jnp.where(
                        group_of == m * 2 + q, value, 0.0
                    ).astype(jnp.bfloat16)
        return carry

    lax.fori_loop(0, pairs, weight_step, 0)

    for step in range(1, planes):
        plane_copy(step, 2).wait_recv()
        near_copy(step, 2).start()
    for step in range(1, planes):
        near_copy(step, 2).wait_recv()
    count = channels // planes
    lanes = lax.broadcasted_iota(jnp.int32, (count, 8 * wide), 1)
    part_of = lanes // rank % 2
    wave_of = lanes // (2 * rank) % 2
    for part in range(rank // 8):
        for z in range(planes):
            columns = slice(part * 8 * rank, (part + 1) * 8 * rank)
            real = dense(outer[z, :count, columns], spread[...])
            imaginary = dense(outer[z, count:, columns], spread[...])
            for r in range(2):
                value = jnp.where(part_of == 0, imaginary, real) if r else jnp.where(part_of == 0, real, -imaginary)
                for m in range(2):
                    start = (m * 2 + r) * channels + z * count
                    closing[start:start + count, part * 8 * wide:(part + 1) * 8 * wide] = (
                        jnp.where(wave_of == m, value, 0.0).astype(jnp.bfloat16)
                    )

    for c in range(PARTS):
        for t in range(1, holders):
            modes_copy(t, c).wait_recv()
    for d in range(holders):
        for p in range(2):
            for v in range(variables):
                stacked[v * waves:(v + 1) * waves, (d * 2 + p) * row_count:(d * 2 + p + 1) * row_count] = (
                    arrived[d, p * waves:(p + 1) * waves, v * row_count:(v + 1) * row_count]
                )
    by = dense(height[...], stacked[...], ((1,), (1,))).astype(jnp.bfloat16)
    placed[...] = (
        dense(by[:kx_count], place[0]) + dense(by[kx_count:], place[1]) + bias_row[...]
    ).astype(jnp.bfloat16)

    def pair_step(j, carry):
        column = pl.ds(pl.multiple_of(j * wide, wide), wide)
        own = placed[:, column]
        for part in range(rank // 8):
            got = dense(own, weights[j, :, part * 8 * wide:(part + 1) * 8 * wide])
            for k in range(packs):
                rows[k, part * 64:(part + 1) * 64, column] = jnp.concatenate(
                    [got[k * EIGHT:(k + 1) * EIGHT, b * wide:(b + 1) * wide] for b in range(8)], axis=0
                ).astype(jnp.bfloat16)
        return carry

    lax.fori_loop(0, pairs, pair_step, 0)

    def first_step(k, carry):
        here = pl.ds(pl.multiple_of(k * 2 * EIGHT, 2 * EIGHT), 2 * EIGHT)
        for part in range(pairs // 2):
            one, two = [
                dense(blocks[2 * k + i], rows[2 * k + i, :, part * 2 * wide:(part + 1) * 2 * wide]) for i in range(2)
            ]
            for j in range(2):
                side = slice(j * wide, (j + 1) * wide)
                for a in range(rank):
                    level = slice(a * EIGHT, (a + 1) * EIGHT)
                    carried[part * 2 + j, here, a * wide:(a + 1) * wide] = jnp.concatenate(
                        [one[level, side], two[level, side]], axis=0
                    ).astype(jnp.bfloat16)
        return carry

    lax.fori_loop(0, packs // 2, first_step, 0)

    for part in range(pairs // 2):
        both = carried[part * 2:part * 2 + 2].reshape(2 * kx_count, rank * wide)
        got = dense(closing[...], both, ((1,), (1,)))
        for m in range(2):
            for r in range(2):
                for j in range(2):
                    turned[:, (part * 2 + j) * 2 + m, r * kx_count:(r + 1) * kx_count] = got[
                        (m * 2 + r) * channels:(m * 2 + r + 1) * channels, j * kx_count:(j + 1) * kx_count
                    ]
    mixed[...] = turned[...].astype(jnp.bfloat16)

    for n in range(3):
        for step in range(1, planes):
            plane_copy(step, n).wait_send()
            near_copy(step, n).wait_send()
    for c in range(PARTS):
        for t in range(1, holders):
            modes_copy(t, c).wait_send()


def mix(fields, forward, first, inner, outer, height, place, bias_row, second, first_spread, spread, planes):
    variables, row_count, points = fields.shape
    holders = forward.shape[0] // (2 * WAVES)
    waves = WAVES
    kx2, depth = height.shape
    rank = inner.shape[0]
    channels = outer.shape[0] // 2 * planes
    wide = 4 * rank
    slots = inner.shape[1] // rank
    packs = kx2 // 2 // EIGHT
    operands = (fields, forward, first, inner, outer, height, place, bias_row, second, first_spread, spread)
    return pl.pallas_call(
        mix_kernel,
        in_specs=[pl.BlockSpec(memory_space=pl.ANY)]
        + [pl.BlockSpec(memory_space=pltpu.VMEM) for _ in operands[1:]],
        out_specs=pl.BlockSpec(memory_space=pltpu.VMEM),
        out_shape=jax.ShapeDtypeStruct((channels, waves, kx2), jnp.bfloat16),
        scratch_shapes=[
            pltpu.VMEM(fields.shape, jnp.bfloat16),
            pltpu.VMEM((holders, 2 * waves, variables * row_count), jnp.bfloat16),
            pltpu.VMEM((holders, 2 * waves, variables * row_count), jnp.bfloat16),
            pltpu.VMEM((planes,) + first.shape, jnp.bfloat16),
            pltpu.VMEM((planes,) + inner.shape, jnp.bfloat16),
            pltpu.VMEM((planes,) + outer.shape, jnp.bfloat16),
            pltpu.VMEM((place.shape[1], depth), jnp.bfloat16),
            pltpu.VMEM((kx2 // 2, waves // 2 * wide), jnp.bfloat16),
            pltpu.VMEM((rank, slots * wide), jnp.bfloat16),
            pltpu.VMEM((2, rank, SLOTS, wide), jnp.float32),
            pltpu.VMEM((waves // 2, 4 * SLOTS, rank * wide), jnp.bfloat16),
            pltpu.VMEM((packs, rank * EIGHT, waves // 2 * wide), jnp.bfloat16),
            pltpu.VMEM((packs, rank * EIGHT, rank * EIGHT), jnp.bfloat16),
            pltpu.VMEM((4 * channels, rank * wide), jnp.bfloat16),
            pltpu.VMEM((waves // 2, kx2 // 2, rank * wide), jnp.bfloat16),
            pltpu.VMEM((channels, waves, kx2), jnp.float32),
            pltpu.SemaphoreType.DMA((PARTS,)),
            pltpu.SemaphoreType.DMA((planes - 1, 3)),
            pltpu.SemaphoreType.DMA((planes - 1, 3)),
            pltpu.SemaphoreType.DMA((planes - 1, 3)),
            pltpu.SemaphoreType.DMA((planes - 1, 3)),
            pltpu.SemaphoreType.DMA((holders - 1, PARTS)),
            pltpu.SemaphoreType.DMA((holders - 1, PARTS)),
        ],
        compiler_params=pltpu.CompilerParams(
            collective_id=1, has_side_effects=True, vmem_limit_bytes=60 * 2**20
        ),
        name="mix",
    )(*operands)


def gelu(h):
    return h * (0.5 + 0.5 * lax.erf(h * (1.0 / math.sqrt(2.0))))


def finish_kernel(
    mixed, back, fields, width, lift_weight, skip_weight, lift_bias, skip_bias, out_weight, out_bias, tall, wide,
    result, gathered, source, cols, total, skip, closing, last_bias, active, send, recv,
):
    channels, waves, kx2 = mixed.shape
    variables, row_count, points = fields.shape
    inner = variables * EIGHT
    steps = row_count // EIGHT // 2
    mode, batch, core = lax.axis_index("mode"), lax.axis_index("batch"), lax.axis_index("cores")
    near = (mode + 1 - 2 * (mode % 2), batch, core)
    by_x = ((mode + 2) % 4, batch, core)
    by_y = (mode, batch, 1 - core)

    def owner(device):
        return device[0] * 2 + device[2]

    me = owner((mode, batch, core))
    at_x, at_y = owner(by_x), owner(by_y)
    across = owner((by_x[0], batch, by_y[2]))

    barrier = pltpu.get_barrier_semaphore()
    for device in (near, by_x, by_y):
        pl.semaphore_signal(barrier, inc=1, device_id=device, device_id_type=MESH)
    pl.semaphore_wait(barrier, 3)

    def piece(holder, first, count):
        return gathered.at[pl.ds(first, count), pl.ds(pl.multiple_of(holder * waves, waves), waves), :]

    def copy(g, kind):
        low, share = STARTS[g], CHUNKS[g]
        half = share // 2
        own = mixed.at[pl.ds(low, share)]
        home = piece(me, low, share)
        x_all, y_all = piece(at_x, low, share), piece(at_y, low, share)
        x_low, y_high = piece(at_x, low, half), piece(at_y, low + half, half)
        d_low, d_high = piece(across, low, half), piece(across, low + half, half)
        from_, to, device = (
            (own, home, near), (own, home, by_x), (own, home, by_y),
            (x_all, x_all, near), (y_all, y_all, near),
            (x_low, x_low, by_y), (y_high, y_high, by_x),
            (d_low, d_low, near), (d_high, d_high, near),
        )[kind]
        return pltpu.make_async_remote_copy(
            src_ref=from_, dst_ref=to, send_sem=send.at[g, kind], recv_sem=recv.at[g, kind],
            device_id=device, device_id_type=MESH,
        )

    def begin(g, kinds):
        for kind in kinds:
            copy(g, kind).start()

    def came(g, kinds):
        for kind in kinds:
            copy(g, kind).wait_recv()

    def relay(g):
        came(g, (1, 2))
        begin(g, (5, 6, 3, 4))
        if g + 1 < len(CHUNKS):
            begin(g + 1, (1, 2, 0))

    def relay_last(g):
        came(g, (5, 6))
        begin(g, (7, 8))

    begin(0, (1, 2, 0))
    gathered[:, pl.ds(pl.multiple_of(me * waves, waves), waves), :] = mixed[...]

    depth = skip.shape[1]
    line = lax.broadcasted_iota(jnp.int32, (depth - inner, points), 0)
    ones = jnp.where(line < 2, 1.0, 0.0).astype(jnp.bfloat16)
    for x in range(steps):
        rows = fields[:, x * 2 * EIGHT:(x + 1) * 2 * EIGHT, :]
        for h in range(2):
            source[x * 2 + h, :inner, :] = rows[:, h * EIGHT:(h + 1) * EIGHT, :].reshape(inner, points)
            source[x * 2 + h, inner:, :] = ones
    relay(0)

    direct = dense(lift_weight[...], skip_weight[...]).astype(jnp.bfloat16)
    row_bias = lax.dot_general(
        jnp.broadcast_to(lift_bias[...], (8, channels)), skip_weight[...].astype(jnp.float32),
        (((1,), (0,)), ((), ())), preferred_element_type=jnp.float32, precision=lax.Precision.HIGHEST,
    )[:1] + skip_bias[...]
    size = 256
    down = lax.broadcasted_iota(jnp.int32, (size, depth), 0) % EIGHT
    along = lax.broadcasted_iota(jnp.int32, (size, depth), 1)
    for part in range(channels * EIGHT // size):
        here = slice(part * size, (part + 1) * size)
        picked = dense(tall[here, :], direct, ((1,), (1,))).astype(jnp.bfloat16)
        spread = dense(picked, wide[:variables, :depth])
        column = jnp.sum(tall[here, :].astype(jnp.float32) * row_bias, axis=1, keepdims=True)
        high = column.astype(jnp.bfloat16).astype(jnp.float32)
        rest = jnp.where(along == inner, high, jnp.where(along == inner + 1, column - high, 0.0))
        skip[here, :] = jnp.where(
            along < inner, jnp.where(down == along % EIGHT, spread, 0.0), rest
        ).astype(jnp.bfloat16)
    chosen = dense(tall[:inner, :variables], out_weight[...], ((1,), (1,))).astype(jnp.bfloat16)
    down = lax.broadcasted_iota(jnp.int32, (inner, channels * EIGHT), 0) % EIGHT
    along = lax.broadcasted_iota(jnp.int32, (inner, channels * EIGHT), 1) % EIGHT
    closing[...] = jnp.where(down == along, dense(chosen, wide[...]), 0.0).astype(jnp.bfloat16)
    column = jnp.sum(tall[:inner, :variables].astype(jnp.float32) * out_bias[...], axis=1, keepdims=True)
    last_bias[...] = jnp.broadcast_to(column, last_bias.shape)
    relay_last(0)

    def turn(g):
        def step(c, carry):
            both = gathered[pl.ds(STARTS[g] + 4 * c, 4)].reshape(4 * waves * 8, kx2)
            got = dense(back[...], both, ((1,), (1,)))
            size = got.shape[1] // 4
            for k in range(2):
                place = pl.ds(pl.multiple_of(c * 4 * EIGHT + k * 2 * EIGHT, 2 * EIGHT), 2 * EIGHT)
                for p in range(2):
                    for x in range(row_count // EIGHT):
                        rows = got[p * row_count + x * EIGHT:p * row_count + (x + 1) * EIGHT, :]
                        cols[x, place, p * size:(p + 1) * size] = jnp.concatenate(
                            [rows[:, 2 * k * size:(2 * k + 1) * size], rows[:, (2 * k + 1) * size:(2 * k + 2) * size]],
                            axis=0,
                        ).astype(jnp.bfloat16)
            return carry

        lax.fori_loop(0, CHUNKS[g] // 4, step, 0)

    def finish_rows(g, low, high):
        start, size = STARTS[g] * EIGHT, CHUNKS[g] * EIGHT

        def step(i, carry):
            for lane in range(points // LANES):
                lanes = slice(lane * LANES, (lane + 1) * LANES)
                done = []
                for h in range(2):
                    x = 2 * i + h
                    for part in range(0, size, ROWS):
                        height = (
                            dense(cols[x, part:part + ROWS, :], width[:, lanes])
                            + dense(skip[start + part:start + part + ROWS, :], source[x, :, lanes])
                        )
                        active[lane * 2 + h, part:part + ROWS, :] = gelu(height).astype(jnp.bfloat16)
                for h in range(2):
                    x = 2 * i + h
                    got = dense(closing[:, start:start + size], active[lane * 2 + h, :size, :])
                    if g == 0:
                        got = got + jnp.concatenate([last_bias[...]] * (LANES // 128), axis=1)
                    else:
                        got = got + total[x, :, lanes]
                    if g + 1 < len(CHUNKS):
                        total[x, :, lanes] = got
                    else:
                        done.append(got.reshape(variables, EIGHT, LANES))
                if done:
                    place = pl.ds(pl.multiple_of(i * 2 * EIGHT, 2 * EIGHT), 2 * EIGHT)
                    result[:, place, lanes] = jnp.concatenate(done, axis=1).astype(jnp.bfloat16)
            return carry

        lax.fori_loop(low, high, step, 0)

    for g in range(len(CHUNKS)):
        came(g, (0, 3, 4, 7, 8))
        turn(g)
        if g + 1 < len(CHUNKS):
            finish_rows(g, 0, steps // 4)
            relay(g + 1)
            finish_rows(g, steps // 4, 3 * steps // 4)
            relay_last(g + 1)
            finish_rows(g, 3 * steps // 4, steps)
        else:
            finish_rows(g, 0, steps)
    for g in range(len(CHUNKS)):
        for kind in range(9):
            copy(g, kind).wait_send()


def finish(mixed, back, fields, width, lift_weight, skip_weight, lift_bias, skip_bias, out_weight, out_bias):
    channels, waves, kx2 = mixed.shape
    variables, row_count, points = fields.shape
    tall = jnp.asarray(np.repeat(np.eye(channels), EIGHT, axis=0).astype(ml_dtypes.bfloat16))
    wide = jnp.asarray(np.repeat(np.eye(channels), EIGHT, axis=1).astype(ml_dtypes.bfloat16))
    operands = (
        mixed, back, fields, width, lift_weight, skip_weight, lift_bias[None], skip_bias[None], out_weight,
        out_bias[None], tall, wide,
    )
    blocks = row_count // EIGHT
    inner = variables * EIGHT
    depth = inner + 2 * EIGHT
    return pl.pallas_call(
        finish_kernel,
        in_specs=[pl.BlockSpec(memory_space=pltpu.VMEM) for _ in operands],
        out_specs=pl.BlockSpec(memory_space=pltpu.VMEM),
        out_shape=jax.ShapeDtypeStruct(fields.shape, jnp.bfloat16),
        scratch_shapes=[
            pltpu.VMEM((channels, 8 * waves, kx2), jnp.bfloat16),
            pltpu.VMEM((blocks, depth, points), jnp.bfloat16),
            pltpu.VMEM((blocks, max(CHUNKS) * EIGHT, width.shape[0]), jnp.bfloat16),
            pltpu.VMEM((blocks, inner, points), jnp.float32),
            pltpu.VMEM((channels * EIGHT, depth), jnp.bfloat16),
            pltpu.VMEM((inner, channels * EIGHT), jnp.bfloat16),
            pltpu.VMEM((inner, 128), jnp.float32),
            pltpu.VMEM((points // LANES * 2, max(CHUNKS) * EIGHT, LANES), jnp.bfloat16),
            pltpu.SemaphoreType.DMA((len(CHUNKS), 9)),
            pltpu.SemaphoreType.DMA((len(CHUNKS), 9)),
        ],
        compiler_params=pltpu.CompilerParams(
            collective_id=0, has_side_effects=True, vmem_limit_bytes=60 * 2**20
        ),
        name="finish",
    )(*operands)


def fast_shards(
    fields, lift_weight, lift_bias, first_core, second_core, input_core, output_core,
    skip_weight, skip_bias, out_weight, out_bias,
):
    holders = lax.axis_size("mode") * lax.axis_size("cores")
    waves, rank, _ = second_core.shape
    _, variables, row_count, points = fields.shape
    channels = lift_weight.shape[1]
    fields = fields[0]
    me = lax.axis_index("mode") * lax.axis_size("cores") + lax.axis_index("cores")

    cosines, sines = host_pair(np.arange(MY), np.arange(points), points)
    root = math.sqrt(points)
    forward = np.stack([cosines, -sines], 0).reshape(2, holders, waves, points).transpose(1, 0, 2, 3)
    forward = jnp.asarray((forward.reshape(2 * MY, points) / root).astype(np.float32)).astype(jnp.bfloat16)
    weight = np.where(np.arange(MY) == 0, 1.0, 2.0).astype(np.float32)[:, None]
    width = np.concatenate([cosines * weight, -sines * weight], 0) / root
    width = jnp.asarray(width.astype(ml_dtypes.bfloat16))
    order = cyclic_rows(row_count, holders)
    root = math.sqrt(NX)
    cosines, sines = host_pair(np.arange(MX) - MX // 2, order, NX)
    cosines, sines = [t.reshape(MX, holders, row_count) / root for t in (cosines, sines)]
    upper = np.stack([cosines, sines], 2)
    lower = np.stack([-sines, cosines], 2)
    height = np.stack([upper, lower], 0).reshape(2 * MX, -1).astype(ml_dtypes.bfloat16)
    real_part = np.asarray(height, np.float32).reshape(2 * MX, holders, 2, row_count)[:, :, 0]
    row_sum = real_part.sum((1, 2), dtype=np.float64).astype(np.float32)
    cos_t, sin_t = [t.transpose(1, 2, 0) for t in (cosines, sines)]
    up = np.concatenate([cos_t, -sin_t], 2)
    low = np.concatenate([sin_t, cos_t], 2)
    back_rows = jnp.asarray(np.concatenate([up, low], 1).astype(ml_dtypes.bfloat16))
    back_rows = lax.dynamic_index_in_dim(back_rows, me, 0, keepdims=False)
    pairs = waves // 2
    place = np.zeros((2, variables, waves, pairs, 2, 2, SLOTS), np.float32)
    for q in range(2):
        for v in range(variables):
            for m in range(waves):
                place[q, v, m, m // 2, q, m % 2, v] = 1.0
    place = jnp.asarray(place.reshape(2, variables * waves, -1).astype(ml_dtypes.bfloat16))
    bias_row = np.zeros((MX, pairs, 2, 2, SLOTS), np.float32)
    bias_row[:, 0, :, 0, variables] = row_sum.reshape(2, MX).T
    bias_row = jnp.asarray(bias_row.reshape(MX, -1)) * (me == 0).astype(jnp.float32)
    packs = first_core.shape[0] // EIGHT
    first_spread = np.einsum("pk,bc->kpbc", np.eye(packs), np.repeat(np.eye(rank), EIGHT, axis=1))
    first_spread = jnp.asarray(first_spread.reshape(packs, packs * rank, rank * EIGHT).astype(ml_dtypes.bfloat16))
    spread = np.eye(8)[:, None, :, None, None] * np.eye(rank)[None, :, None, None, :] * np.ones((1, 1, 1, 4, 1))
    spread = jnp.asarray(spread.reshape(8 * rank, 32 * rank).astype(ml_dtypes.bfloat16))

    used = (variables + 4) // 4 * 4
    lift = jnp.concatenate(
        [lift_weight, (math.sqrt(points) * lift_bias).astype(jnp.bfloat16)[None],
         jnp.zeros((used - variables - 1, channels), jnp.bfloat16)], 0
    )
    count = input_core.shape[0]
    lift = lax.dynamic_slice_in_dim(lift, lax.axis_index("batch") * count, count, 1)
    inner = jnp.einsum("vc,cde->dve", lift, input_core, preferred_element_type=jnp.float32)
    inner = inner.astype(jnp.bfloat16).reshape(rank, used * rank)
    first = first_core.reshape(packs, EIGHT, rank, rank).transpose(2, 1, 0, 3).reshape(rank * EIGHT, packs * rank)
    outer = output_core.transpose(1, 0, 3, 2).reshape(2 * count, rank * rank)
    mixed = mix(
        fields, forward, first, inner, outer, jnp.asarray(height), place, bias_row,
        second_core.reshape(waves * rank, rank), first_spread, spread, lax.axis_size("batch"),
    )
    return finish(
        mixed, back_rows, fields, width, lift_weight, skip_weight, lift_bias, skip_bias, out_weight, out_bias
    )[None]


def solution(mesh):
    placed = (
        P("batch", None, ("mode", "cores"), None),
        P(),
        P(),
        P("batch", None, None),
        P(("mode", "cores"), None, None),
        P("batch", None, None),
        P("batch", None, None, None),
        P(),
        P(),
        P(),
        P(),
    )
    fits = (
        mesh.shape["mode"] == 4 and mesh.shape["cores"] == 2 and MY // 8 == WAVES
        and mesh.shape["batch"] == 4 and MX // 4 % EIGHT == 0 and NX // 8 == 128
    )
    return jax.shard_map(
        fast_shards if fits else shards,
        mesh=mesh,
        in_specs=placed,
        out_specs=P("batch", None, ("mode", "cores"), None),
        check_vma=False,
    )
```

```python
import functools
import math

import jax
import jax.numpy as jnp
import ml_dtypes
import numpy as np
from jax import lax
from jax.experimental import pallas as pl
from jax.experimental.pallas import tpu as pltpu
from jax.sharding import PartitionSpec as P

NX = 1024
NY = 1024
MX = 128
MY = 128


TWO_PI = 2.0 * math.pi


def wave_pair(waves, points, length):
    phase_step = waves[:, None] * points[None, :] % length
    angles = phase_step.astype(jnp.float32) * (TWO_PI / length)
    return (jnp.cos(angles), jnp.sin(angles))


def width_forward(length, wave_count):
    points = jnp.arange(length, dtype=jnp.int32)
    waves = jnp.arange(wave_count, dtype=jnp.int32)
    cosines, sine_part = wave_pair(points, waves, length)
    stacked = jnp.stack([cosines, -sine_part], axis=1) / math.sqrt(length)
    return stacked.astype(jnp.bfloat16)


def height_forward(row_index, wave_count, length):
    waves = jnp.arange(wave_count, dtype=jnp.int32) - wave_count // 2
    cosines, sine_part = wave_pair(waves, row_index, length)
    upper = jnp.stack([cosines, sine_part], axis=1)
    lower = jnp.stack([-sine_part, cosines], axis=1)
    return (jnp.stack([upper, lower], axis=0) / math.sqrt(length)).astype(jnp.bfloat16)


def height_inverse(row_index, wave_count, length):
    waves = jnp.arange(wave_count, dtype=jnp.int32) - wave_count // 2
    cosines, sine_part = wave_pair(row_index, waves, length)
    upper = jnp.stack([cosines, -sine_part], axis=1)
    lower = jnp.stack([sine_part, cosines], axis=1)
    return (jnp.stack([upper, lower], axis=0) / math.sqrt(length)).astype(jnp.bfloat16)


def width_inverse(waves, length):
    points = jnp.arange(length, dtype=jnp.int32)
    cosines, sine_part = wave_pair(waves, points, length)
    weight = jnp.where(waves == 0, 1.0, 2.0).astype(jnp.float32)[:, None]
    stacked = jnp.stack([cosines * weight, -sine_part * weight], axis=0) / math.sqrt(length)
    return stacked.astype(jnp.bfloat16)


def bias_modes(lift_bias, wave_index, length):
    real_row = (
        jnp.where(wave_index == 0, 1.0, 0.0).astype(jnp.float32)[:, None]
        * (math.sqrt(length) * lift_bias)[None, :]
    )
    return jnp.stack([real_row, jnp.zeros_like(real_row)], axis=0)


def lift_modes(modes, lift_weight, lift_bias, wave_index):
    lifted_modes = jnp.einsum(
        "fabpmv,vc->fabpmc", modes, lift_weight, preferred_element_type=jnp.float32
    )
    return (lifted_modes + bias_modes(lift_bias, wave_index, NY)).astype(jnp.bfloat16)


def grid_rows(stored, row_count, holder_count):
    return stored % row_count * holder_count + stored // row_count


def shards(
    fields,
    lift_weight,
    lift_bias,
    first_core,
    second_core,
    input_core,
    output_core,
    skip_weight,
    skip_bias,
    out_weight,
    out_bias,
):
    mode_count = lax.axis_size("mode")
    core_count = lax.axis_size("cores")
    row_count = fields.shape[2]
    block_size = second_core.shape[0]
    block_start = (lax.axis_index("mode") * core_count + lax.axis_index("cores")) * block_size
    local_waves = block_start + jnp.arange(block_size, dtype=jnp.int32)
    lifted = (
        jnp.einsum("fvxy,vc->fxyc", fields, lift_weight, preferred_element_type=jnp.float32)
        + lift_bias
    ).astype(jnp.bfloat16)
    field_modes = jnp.einsum(
        "fvxy,ypk->fxpkv", fields, width_forward(NY, MY), preferred_element_type=jnp.float32
    ).astype(jnp.bfloat16)
    field_modes = field_modes[:, None]
    gathered = (
        lax.all_gather(first_core, "batch", axis=0, tiled=True),
        lax.all_gather(input_core, "batch", axis=0, tiled=True),
        lax.all_gather(output_core, "batch", axis=0, tiled=True),
    )
    first_whole, input_whole, output_whole = gathered
    mode_factor = jnp.einsum(
        "kab,mbd->kmad", first_whole, second_core, preferred_element_type=jnp.float32
    ).astype(jnp.bfloat16)
    arrived = lax.all_to_all(
        field_modes, ("mode", "cores"), split_axis=4, concat_axis=2, tiled=True
    )
    rows_held = jnp.arange(NX, dtype=jnp.int32)[None, :]
    by_mode = lift_modes(arrived, lift_weight, lift_bias, local_waves)
    lead_rows = rows_held.shape[0]
    side_rows = rows_held.shape[1]
    flat_rows = grid_rows(rows_held.reshape(-1), row_count, mode_count * core_count)
    height_table = height_forward(flat_rows, MX, NX).reshape(2, MX, 2, lead_rows, side_rows)
    spectrum = jnp.einsum(
        "qkpab,fabpmc->fqkmc", height_table, by_mode, preferred_element_type=jnp.float32
    ).astype(jnp.bfloat16)
    projected = jnp.einsum(
        "fqkmc,cbe->fqkmbe", spectrum, input_whole, preferred_element_type=jnp.float32
    ).astype(jnp.bfloat16)
    carried = jnp.einsum(
        "kmab,fqkmbe->fqkmae", mode_factor, projected, preferred_element_type=jnp.float32
    ).astype(jnp.bfloat16)
    traced = jnp.einsum(
        "fqkmae,osea->fqkmso", carried, output_whole, preferred_element_type=jnp.float32
    )
    real_part = traced[:, 0, :, :, 0, :] - traced[:, 1, :, :, 1, :]
    imaginary = traced[:, 0, :, :, 1, :] + traced[:, 1, :, :, 0, :]
    mixed_modes = jnp.stack([real_part, imaginary], axis=1).astype(jnp.bfloat16)
    height_back = height_inverse(flat_rows, MX, NX).reshape(2, lead_rows, side_rows, 2, MX)
    col_modes = jnp.einsum(
        "pabqk,fqkmc->fabpmc", height_back, mixed_modes, preferred_element_type=jnp.float32
    ).astype(jnp.bfloat16)
    returned = lax.all_to_all(col_modes, ("mode", "cores"), split_axis=2, concat_axis=4, tiled=True)
    waves_held = jnp.arange(MY, dtype=jnp.int32)
    width_back = width_inverse(waves_held, NY)
    spatial = jnp.einsum(
        "fxpmc,pmy->fxyc", returned[:, 0], width_back, preferred_element_type=jnp.float32
    )
    skip_term = jnp.einsum("fxyc,cd->fxyd", lifted, skip_weight, preferred_element_type=jnp.float32)
    active = jax.nn.gelu(spatial + skip_term + skip_bias, approximate=False).astype(jnp.bfloat16)
    result = (
        jnp.einsum("fxyc,cv->fvxy", active, out_weight, preferred_element_type=jnp.float32)
        + out_bias[:, None, None]
    )
    return result.astype(jnp.bfloat16)


def cyclic_rows(row_count, holders):
    return (np.arange(row_count)[None, :] * holders + np.arange(holders)[:, None]).reshape(-1)


def host_pair(waves, points, length):
    steps = np.asarray(waves)[:, None] * np.asarray(points)[None, :] % length
    angles = steps.astype(np.float32) * np.float32(TWO_PI / length)
    return np.cos(angles), np.sin(angles)


def dense(a, b, contract=((1,), (0,))):
    return lax.dot_general(a, b, (contract, ((), ())), preferred_element_type=jnp.float32)


MESH = pl.DeviceIdType.MESH
WAVES = 16
SLOTS = 32
EIGHT = 8
CHUNKS = (64, 64)
STARTS = (0, 64)
LANES = 512
ROWS = 256
PARTS = 2
TURN = 8


def whole(a):
    return pl.BlockSpec(a.shape, lambda *_: (0,) * a.ndim)


def mix_kernel(
    fields_far, forward, first_own, inner_own, outer_own, height_far, place_far, bias_row, second, first_spread, spread,
    mixed, fields, height, place, modes, arrived, first, inner, outer, stacked, placed, inner_wide, turned_inner, weights, rows,
    blocks, closing, carried, turned, load, send_plane, recv_plane, send_near, recv_near, send_modes, recv_modes,
):
    variables, row_count, points = fields.shape
    holders, lead, flat = arrived.shape
    waves = lead // 2
    kx_count = height.shape[0] // 2
    planes = first.shape[0]
    rank = inner.shape[1]
    channels = mixed.shape[0]
    pairs = waves // 2
    wide = 4 * rank
    slots = inner.shape[2] // rank
    packs = kx_count // EIGHT
    share = variables // PARTS
    mode, batch, core = lax.axis_index("mode"), lax.axis_index("batch"), lax.axis_index("cores")
    me = mode * 2 + core
    near = (mode + 1 - 2 * (mode % 2), batch, core)

    def load_part(c):
        here = pl.ds(c * share, share)
        return pltpu.make_async_copy(fields_far.at[here], fields.at[here], load.at[c])

    def load_table(n):
        return pltpu.make_async_copy((height_far, place_far)[n], (height, place)[n], load.at[PARTS + n])

    for c in range(PARTS):
        load_part(c).start()
    for n in range(2):
        load_table(n).start()

    def flip(bit, change):
        return bit + change - 2 * bit * change

    def peer(t):
        chip, side, line = flip(mode // 2, t // 4), flip(mode % 2, t // 2 % 2), flip(core, t % 2)
        return (chip * 2 + side, batch, line), chip * 4 + side * 2 + line

    def plane(step):
        return (mode, (batch + step) % planes, core)

    barrier = pltpu.get_barrier_semaphore()
    greeted = [peer(t)[0] for t in range(1, holders)] + [plane(step) for step in range(1, planes)]
    for device in greeted:
        pl.semaphore_signal(barrier, inc=1, device_id=device, device_id_type=MESH)
    pl.semaphore_wait(barrier, len(greeted))

    shards_own = (first_own, inner_own, outer_own)
    shards_all = (first, inner, outer)

    def half(n):
        size = shards_own[n].shape[0] // 2
        return pl.ds(pl.multiple_of((mode % 2) * size, size), size)

    def plane_copy(step, n):
        return pltpu.make_async_remote_copy(
            src_ref=shards_own[n].at[half(n)], dst_ref=shards_all[n].at[batch, half(n)],
            send_sem=send_plane.at[step - 1, n], recv_sem=recv_plane.at[step - 1, n],
            device_id=plane(step), device_id_type=MESH,
        )

    def near_copy(step, n):
        held = shards_all[n].at[(batch + planes - step) % planes, half(n)]
        return pltpu.make_async_remote_copy(
            src_ref=held, dst_ref=held, send_sem=send_near.at[step - 1, n], recv_sem=recv_near.at[step - 1, n],
            device_id=near, device_id_type=MESH,
        )

    def modes_copy(t, c):
        device, index = peer(t)
        lanes = pl.ds(c * share * row_count, share * row_count)
        return pltpu.make_async_remote_copy(
            src_ref=modes.at[index, :, lanes], dst_ref=arrived.at[me, :, lanes],
            send_sem=send_modes.at[t - 1, c], recv_sem=recv_modes.at[t - 1, c],
            device_id=device, device_id_type=MESH,
        )

    for n in range(3):
        for step in range(1, planes):
            plane_copy(step, n).start()
    for n in range(3):
        shards_all[n][batch] = shards_own[n][...]

    for c in range(PARTS):
        load_part(c).wait()
        for v in range(c * share, (c + 1) * share, 2):
            both = fields[v:v + 2].reshape(2 * row_count, points)
            got = dense(forward[...], both, ((1,), (1,))).astype(jnp.bfloat16)
            modes[:, :, v * row_count:(v + 2) * row_count] = got.reshape(holders, lead, 2 * row_count)
        for t in range(holders - 1, 0, -1):
            modes_copy(t, c).start()
    arrived[me] = modes[me]

    for n in range(2):
        for step in range(1, planes):
            plane_copy(step, n).wait_recv()
            near_copy(step, n).start()
    for n in range(2):
        for step in range(1, planes):
            near_copy(step, n).wait_recv()

    total = inner[0].astype(jnp.float32)
    for z in range(1, planes):
        total = total + inner[z].astype(jnp.float32)
    total = total.astype(jnp.bfloat16)
    for part in range(slots // 4):
        inner_wide[:, part * 4 * wide:(part + 1) * 4 * wide] = dense(
            total[:, part * wide:(part + 1) * wide], spread[:wide, :4 * wide]
        ).astype(jnp.bfloat16)

    down = lax.broadcasted_iota(jnp.int32, (rank * EIGHT, rank * EIGHT), 0) % EIGHT
    along = lax.broadcasted_iota(jnp.int32, (rank * EIGHT, rank * EIGHT), 1) % EIGHT
    same = down == along
    for z in range(planes):
        for k in range(packs // planes):
            full = dense(first[z], first_spread[k])
            blocks[z * (packs // planes) + k] = jnp.where(same, full, 0.0).astype(jnp.bfloat16)

    turned_inner[...] = jnp.zeros_like(turned_inner)
    group_of = lax.broadcasted_iota(jnp.int32, (SLOTS, wide), 1) // rank

    def weight_step(j, carry):
        start = pl.multiple_of(j * 2 * rank, 2 * rank)
        joined = dense(second[pl.ds(start, 2 * rank), :], inner_wide[...])
        for m in range(2):
            for v in range(slots):
                turned_inner[m, :, v, :] = joined[m * rank:(m + 1) * rank, v * wide:(v + 1) * wide]
        for m in range(2):
            for b in range(rank):
                value = turned_inner[m, b]
                for q in range(2):
                    weights[j, (q * 2 + m) * SLOTS:(q * 2 + m + 1) * SLOTS, b * wide:(b + 1) * wide] = jnp.where(
                        group_of == m * 2 + q, value, 0.0
                    ).astype(jnp.bfloat16)
        return carry

    lax.fori_loop(0, pairs, weight_step, 0)

    for step in range(1, planes):
        plane_copy(step, 2).wait_recv()
        near_copy(step, 2).start()
    for step in range(1, planes):
        near_copy(step, 2).wait_recv()
    count = channels // planes
    lanes = lax.broadcasted_iota(jnp.int32, (count, 8 * wide), 1)
    part_of = lanes // rank % 2
    wave_of = lanes // (2 * rank) % 2
    for part in range(rank // 8):
        for z in range(planes):
            columns = slice(part * 8 * rank, (part + 1) * 8 * rank)
            real = dense(outer[z, :count, columns], spread[...])
            imaginary = dense(outer[z, count:, columns], spread[...])
            for r in range(2):
                value = jnp.where(part_of == 0, imaginary, real) if r else jnp.where(part_of == 0, real, -imaginary)
                for m in range(2):
                    start = (m * 2 + r) * channels + z * count
                    closing[start:start + count, part * 8 * wide:(part + 1) * 8 * wide] = (
                        jnp.where(wave_of == m, value, 0.0).astype(jnp.bfloat16)
                    )

    for n in range(2):
        load_table(n).wait()
    for c in range(PARTS):
        for t in range(1, holders):
            modes_copy(t, c).wait_recv()
    for d in range(holders):
        for p in range(2):
            for v in range(variables):
                stacked[v * waves:(v + 1) * waves, (d * 2 + p) * row_count:(d * 2 + p + 1) * row_count] = (
                    arrived[d, p * waves:(p + 1) * waves, v * row_count:(v + 1) * row_count]
                )
    by = dense(height[...], stacked[...], ((1,), (1,))).astype(jnp.bfloat16)
    first_wave = (me == 0).astype(jnp.float32)
    placed[...] = (
        dense(by[:kx_count], place[0]) + dense(by[kx_count:], place[1]) + bias_row[...] * first_wave
    ).astype(jnp.bfloat16)

    def pair_step(j, carry):
        column = pl.ds(pl.multiple_of(j * wide, wide), wide)
        own = placed[:, column]
        for part in range(rank // 8):
            got = dense(own, weights[j, :, part * 8 * wide:(part + 1) * 8 * wide])
            for k in range(packs):
                rows[k, part * 64:(part + 1) * 64, column] = jnp.concatenate(
                    [got[k * EIGHT:(k + 1) * EIGHT, b * wide:(b + 1) * wide] for b in range(8)], axis=0
                ).astype(jnp.bfloat16)
        return carry

    lax.fori_loop(0, pairs, pair_step, 0)

    def first_step(k, carry):
        here = pl.ds(pl.multiple_of(k * 2 * EIGHT, 2 * EIGHT), 2 * EIGHT)
        for part in range(pairs // 2):
            one, two = [
                dense(blocks[2 * k + i], rows[2 * k + i, :, part * 2 * wide:(part + 1) * 2 * wide]) for i in range(2)
            ]
            for j in range(2):
                side = slice(j * wide, (j + 1) * wide)
                for a in range(rank):
                    level = slice(a * EIGHT, (a + 1) * EIGHT)
                    carried[part * 2 + j, here, a * wide:(a + 1) * wide] = jnp.concatenate(
                        [one[level, side], two[level, side]], axis=0
                    ).astype(jnp.bfloat16)
        return carry

    lax.fori_loop(0, packs // 2, first_step, 0)

    for part in range(pairs // 2):
        both = carried[part * 2:part * 2 + 2].reshape(2 * kx_count, rank * wide)
        got = dense(closing[...], both, ((1,), (1,)))
        for m in range(2):
            for r in range(2):
                for j in range(2):
                    turned[:, (part * 2 + j) * 2 + m, r * kx_count:(r + 1) * kx_count] = got[
                        (m * 2 + r) * channels:(m * 2 + r + 1) * channels, j * kx_count:(j + 1) * kx_count
                    ]
    mixed[...] = turned[...].astype(jnp.bfloat16)

    for n in range(3):
        for step in range(1, planes):
            plane_copy(step, n).wait_send()
            near_copy(step, n).wait_send()
    for c in range(PARTS):
        for t in range(1, holders):
            modes_copy(t, c).wait_send()


def mix(fields, forward, first, inner, outer, height, place, bias_row, second, first_spread, spread, planes):
    variables, row_count, points = fields.shape
    holders = forward.shape[0] // (2 * WAVES)
    waves = WAVES
    kx2, depth = height.shape
    rank = inner.shape[0]
    channels = outer.shape[0] // 2 * planes
    wide = 4 * rank
    slots = inner.shape[1] // rank
    packs = kx2 // 2 // EIGHT
    operands = (fields, forward, first, inner, outer, height, place, bias_row, second, first_spread, spread)
    return pl.pallas_call(
        mix_kernel,
        in_specs=[pl.BlockSpec(memory_space=pl.ANY if n in (0, 5, 6) else pltpu.VMEM) for n in range(len(operands))],
        out_specs=pl.BlockSpec(memory_space=pltpu.VMEM),
        out_shape=jax.ShapeDtypeStruct((channels, waves, kx2), jnp.bfloat16),
        scratch_shapes=[
            pltpu.VMEM(fields.shape, jnp.bfloat16),
            pltpu.VMEM(height.shape, jnp.bfloat16),
            pltpu.VMEM(place.shape, jnp.bfloat16),
            pltpu.VMEM((holders, 2 * waves, variables * row_count), jnp.bfloat16),
            pltpu.VMEM((holders, 2 * waves, variables * row_count), jnp.bfloat16),
            pltpu.VMEM((planes,) + first.shape, jnp.bfloat16),
            pltpu.VMEM((planes,) + inner.shape, jnp.bfloat16),
            pltpu.VMEM((planes,) + outer.shape, jnp.bfloat16),
            pltpu.VMEM((place.shape[1], depth), jnp.bfloat16),
            pltpu.VMEM((kx2 // 2, waves // 2 * wide), jnp.bfloat16),
            pltpu.VMEM((rank, slots * wide), jnp.bfloat16),
            pltpu.VMEM((2, rank, SLOTS, wide), jnp.float32),
            pltpu.VMEM((waves // 2, 4 * SLOTS, rank * wide), jnp.bfloat16),
            pltpu.VMEM((packs, rank * EIGHT, waves // 2 * wide), jnp.bfloat16),
            pltpu.VMEM((packs, rank * EIGHT, rank * EIGHT), jnp.bfloat16),
            pltpu.VMEM((4 * channels, rank * wide), jnp.bfloat16),
            pltpu.VMEM((waves // 2, kx2 // 2, rank * wide), jnp.bfloat16),
            pltpu.VMEM((channels, waves, kx2), jnp.float32),
            pltpu.SemaphoreType.DMA((PARTS + 2,)),
            pltpu.SemaphoreType.DMA((planes - 1, 3)),
            pltpu.SemaphoreType.DMA((planes - 1, 3)),
            pltpu.SemaphoreType.DMA((planes - 1, 3)),
            pltpu.SemaphoreType.DMA((planes - 1, 3)),
            pltpu.SemaphoreType.DMA((holders - 1, PARTS)),
            pltpu.SemaphoreType.DMA((holders - 1, PARTS)),
        ],
        compiler_params=pltpu.CompilerParams(
            collective_id=1, has_side_effects=True, vmem_limit_bytes=60 * 2**20
        ),
        name="mix",
    )(*operands)


def gelu(h):
    return h * (0.5 + 0.5 * lax.erf(h * (1.0 / math.sqrt(2.0))))


def finish_kernel(
    mixed, back_far, fields_far, width, lift_weight, skip_weight, lift_bias, skip_bias, out_weight, out_bias, tall, wide,
    result_far, gathered, back, fields, source, cols, total, skip, closing, last_bias, active, load, leave, send, recv,
):
    channels, waves, kx2 = mixed.shape
    variables, row_count, points = fields.shape
    inner = variables * EIGHT
    steps = row_count // EIGHT // 2
    mode, batch, core = lax.axis_index("mode"), lax.axis_index("batch"), lax.axis_index("cores")
    near = (mode + 1 - 2 * (mode % 2), batch, core)
    by_x = ((mode + 2) % 4, batch, core)
    by_y = (mode, batch, 1 - core)

    def owner(device):
        return device[0] * 2 + device[2]

    me = owner((mode, batch, core))
    at_x, at_y = owner(by_x), owner(by_y)
    across = owner((by_x[0], batch, by_y[2]))

    barrier = pltpu.get_barrier_semaphore()
    for device in (near, by_x, by_y):
        pl.semaphore_signal(barrier, inc=1, device_id=device, device_id_type=MESH)
    pl.semaphore_wait(barrier, 3)

    def piece(holder, first, count):
        return gathered.at[pl.ds(first, count), pl.ds(pl.multiple_of(holder * waves, waves), waves), :]

    def copy(g, kind):
        low, share = STARTS[g], CHUNKS[g]
        half = share // 2
        own = mixed.at[pl.ds(low, share)]
        home = piece(me, low, share)
        x_all, y_all = piece(at_x, low, share), piece(at_y, low, share)
        x_low, y_high = piece(at_x, low, half), piece(at_y, low + half, half)
        d_low, d_high = piece(across, low, half), piece(across, low + half, half)
        from_, to, device = (
            (own, home, near), (own, home, by_x), (own, home, by_y),
            (x_all, x_all, near), (y_all, y_all, near),
            (x_low, x_low, by_y), (y_high, y_high, by_x),
            (d_low, d_low, near), (d_high, d_high, near),
        )[kind]
        return pltpu.make_async_remote_copy(
            src_ref=from_, dst_ref=to, send_sem=send.at[g, kind], recv_sem=recv.at[g, kind],
            device_id=device, device_id_type=MESH,
        )

    def begin(g, kinds):
        for kind in kinds:
            copy(g, kind).start()

    def came(g, kinds):
        for kind in kinds:
            copy(g, kind).wait_recv()

    def relay(g):
        came(g, (1, 2))
        begin(g, (5, 6, 3, 4))
        if g + 1 < len(CHUNKS):
            begin(g + 1, (1, 2, 0))

    def relay_last(g):
        came(g, (5, 6))
        begin(g, (7, 8))

    begin(0, (1, 2, 0))
    loads = [
        pltpu.make_async_copy(fields_far, fields, load.at[0]),
        pltpu.make_async_copy(back_far.at[me], back, load.at[1]),
    ]
    for one in loads:
        one.start()
    gathered[:, pl.ds(pl.multiple_of(me * waves, waves), waves), :] = mixed[...]

    depth = skip.shape[1]
    line = lax.broadcasted_iota(jnp.int32, (depth - inner, points), 0)
    ones = jnp.where(line < 2, 1.0, 0.0).astype(jnp.bfloat16)
    for one in loads:
        one.wait()
    for x in range(steps):
        rows = fields[:, x * 2 * EIGHT:(x + 1) * 2 * EIGHT, :]
        for h in range(2):
            source[x * 2 + h, :inner, :] = rows[:, h * EIGHT:(h + 1) * EIGHT, :].reshape(inner, points)
            source[x * 2 + h, inner:, :] = ones
    relay(0)

    direct = dense(lift_weight[...], skip_weight[...]).astype(jnp.bfloat16)
    row_bias = lax.dot_general(
        jnp.broadcast_to(lift_bias[...], (8, channels)), skip_weight[...].astype(jnp.float32),
        (((1,), (0,)), ((), ())), preferred_element_type=jnp.float32, precision=lax.Precision.HIGHEST,
    )[:1] + skip_bias[...]
    size = 256
    down = lax.broadcasted_iota(jnp.int32, (size, depth), 0) % EIGHT
    along = lax.broadcasted_iota(jnp.int32, (size, depth), 1)
    for part in range(channels * EIGHT // size):
        here = slice(part * size, (part + 1) * size)
        picked = dense(tall[here, :], direct, ((1,), (1,))).astype(jnp.bfloat16)
        spread = dense(picked, wide[:variables, :depth])
        column = jnp.sum(tall[here, :].astype(jnp.float32) * row_bias, axis=1, keepdims=True)
        high = column.astype(jnp.bfloat16).astype(jnp.float32)
        rest = jnp.where(along == inner, high, jnp.where(along == inner + 1, column - high, 0.0))
        skip[here, :] = jnp.where(
            along < inner, jnp.where(down == along % EIGHT, spread, 0.0), rest
        ).astype(jnp.bfloat16)
    chosen = dense(tall[:inner, :variables], out_weight[...]).astype(jnp.bfloat16)
    down = lax.broadcasted_iota(jnp.int32, (inner, channels * EIGHT), 0) % EIGHT
    along = lax.broadcasted_iota(jnp.int32, (inner, channels * EIGHT), 1) % EIGHT
    closing[...] = jnp.where(down == along, dense(chosen, wide[...]), 0.0).astype(jnp.bfloat16)
    column = jnp.sum(tall[:inner, :variables].astype(jnp.float32) * out_bias[...], axis=1, keepdims=True)
    last_bias[...] = jnp.broadcast_to(column, last_bias.shape)
    relay_last(0)

    def turn(g):
        def step(c, carry):
            both = gathered[pl.ds(STARTS[g] + TURN * c, TURN)].reshape(TURN * waves * 8, kx2)
            got = dense(back[...], both, ((1,), (1,)))
            size = got.shape[1] // TURN
            for k in range(TURN // 2):
                place = pl.ds(pl.multiple_of(c * TURN * EIGHT + k * 2 * EIGHT, 2 * EIGHT), 2 * EIGHT)
                for p in range(2):
                    for x in range(row_count // EIGHT):
                        rows = got[p * row_count + x * EIGHT:p * row_count + (x + 1) * EIGHT, :]
                        cols[x, place, p * size:(p + 1) * size] = jnp.concatenate(
                            [rows[:, 2 * k * size:(2 * k + 1) * size], rows[:, (2 * k + 1) * size:(2 * k + 2) * size]],
                            axis=0,
                        ).astype(jnp.bfloat16)
            return carry

        lax.fori_loop(0, CHUNKS[g] // TURN, step, 0)

    def leave_rows(i):
        place = pl.ds(pl.multiple_of(i * 2 * EIGHT, 2 * EIGHT), 2 * EIGHT)
        return pltpu.make_async_copy(fields.at[:, place, :], result_far.at[:, place, :], leave.at[i])

    def finish_rows(g, low, high):
        start, size = STARTS[g] * EIGHT, CHUNKS[g] * EIGHT

        def step(i, carry):
            for lane in range(points // LANES):
                lanes = slice(lane * LANES, (lane + 1) * LANES)
                done = []
                for h in range(2):
                    x = 2 * i + h
                    for part in range(0, size, ROWS):
                        height = (
                            dense(cols[x, part:part + ROWS, :], width[:, lanes])
                            + dense(skip[start + part:start + part + ROWS, :], source[x, :, lanes])
                        )
                        active[lane * 2 + h, part:part + ROWS, :] = gelu(height).astype(jnp.bfloat16)
                for h in range(2):
                    x = 2 * i + h
                    got = dense(closing[:, start:start + size], active[lane * 2 + h, :size, :])
                    if g == 0:
                        got = got + jnp.concatenate([last_bias[...]] * (LANES // 128), axis=1)
                    else:
                        got = got + total[x, :, lanes]
                    if g + 1 < len(CHUNKS):
                        total[x, :, lanes] = got
                    else:
                        done.append(got.reshape(variables, EIGHT, LANES))
                if done:
                    place = pl.ds(pl.multiple_of(i * 2 * EIGHT, 2 * EIGHT), 2 * EIGHT)
                    fields[:, place, lanes] = jnp.concatenate(done, axis=1).astype(jnp.bfloat16)
            if g + 1 == len(CHUNKS):
                leave_rows(i).start()
            return carry

        lax.fori_loop(low, high, step, 0)

    for g in range(len(CHUNKS)):
        came(g, (0, 3, 4, 7, 8))
        turn(g)
        if g + 1 < len(CHUNKS):
            finish_rows(g, 0, steps // 4)
            relay(g + 1)
            finish_rows(g, steps // 4, 3 * steps // 4)
            relay_last(g + 1)
            finish_rows(g, 3 * steps // 4, steps)
        else:
            finish_rows(g, 0, steps)
    for g in range(len(CHUNKS)):
        for kind in range(9):
            copy(g, kind).wait_send()

    def leave_step(i, carry):
        leave_rows(i).wait()
        return carry

    lax.fori_loop(0, steps, leave_step, 0)


def finish(mixed, back, fields, width, lift_weight, skip_weight, lift_bias, skip_bias, out_weight, out_bias):
    channels, waves, kx2 = mixed.shape
    variables, row_count, points = fields.shape
    tall = jnp.asarray(np.repeat(np.eye(channels), EIGHT, axis=0).astype(ml_dtypes.bfloat16))
    wide = jnp.asarray(np.repeat(np.eye(channels), EIGHT, axis=1).astype(ml_dtypes.bfloat16))
    operands = (
        mixed, back, fields, width, lift_weight, skip_weight, lift_bias[None], skip_bias[None], out_weight,
        out_bias[None], tall, wide,
    )
    blocks = row_count // EIGHT
    inner = variables * EIGHT
    depth = inner + 2 * EIGHT
    return pl.pallas_call(
        finish_kernel,
        in_specs=[pl.BlockSpec(memory_space=pl.ANY if n in (1, 2) else pltpu.VMEM) for n in range(len(operands))],
        out_specs=pl.BlockSpec(memory_space=pl.ANY),
        out_shape=jax.ShapeDtypeStruct(fields.shape, jnp.bfloat16),
        scratch_shapes=[
            pltpu.VMEM((channels, 8 * waves, kx2), jnp.bfloat16),
            pltpu.VMEM(back.shape[1:], jnp.bfloat16),
            pltpu.VMEM(fields.shape, jnp.bfloat16),
            pltpu.VMEM((blocks, depth, points), jnp.bfloat16),
            pltpu.VMEM((blocks, max(CHUNKS) * EIGHT, width.shape[0]), jnp.bfloat16),
            pltpu.VMEM((blocks, inner, points), jnp.float32),
            pltpu.VMEM((channels * EIGHT, depth), jnp.bfloat16),
            pltpu.VMEM((inner, channels * EIGHT), jnp.bfloat16),
            pltpu.VMEM((inner, 128), jnp.float32),
            pltpu.VMEM((points // LANES * 2, max(CHUNKS) * EIGHT, LANES), jnp.bfloat16),
            pltpu.SemaphoreType.DMA((2,)),
            pltpu.SemaphoreType.DMA((blocks // 2,)),
            pltpu.SemaphoreType.DMA((len(CHUNKS), 9)),
            pltpu.SemaphoreType.DMA((len(CHUNKS), 9)),
        ],
        compiler_params=pltpu.CompilerParams(
            collective_id=0, has_side_effects=True, vmem_limit_bytes=60 * 2**20
        ),
        name="finish",
    )(*operands)


def fast_shards(
    fields, lift_weight, lift_bias, first_core, second_core, input_core, output_core,
    skip_weight, skip_bias, out_weight, out_bias,
):
    holders = lax.axis_size("mode") * lax.axis_size("cores")
    waves, rank, _ = second_core.shape
    _, variables, row_count, points = fields.shape
    channels = lift_weight.shape[1]
    fields = fields[0]

    cosines, sines = host_pair(np.arange(MY), np.arange(points), points)
    root = math.sqrt(points)
    forward = np.stack([cosines, -sines], 0).reshape(2, holders, waves, points).transpose(1, 0, 2, 3)
    forward = jnp.asarray((forward.reshape(2 * MY, points) / root).astype(np.float32).astype(ml_dtypes.bfloat16))
    weight = np.where(np.arange(MY) == 0, 1.0, 2.0).astype(np.float32)[:, None]
    width = np.concatenate([cosines * weight, -sines * weight], 0) / root
    width = jnp.asarray(width.astype(ml_dtypes.bfloat16))
    order = cyclic_rows(row_count, holders)
    root = math.sqrt(NX)
    cosines, sines = host_pair(np.arange(MX) - MX // 2, order, NX)
    cosines, sines = [t.reshape(MX, holders, row_count) / root for t in (cosines, sines)]
    upper = np.stack([cosines, sines], 2)
    lower = np.stack([-sines, cosines], 2)
    height = np.stack([upper, lower], 0).reshape(2 * MX, -1).astype(ml_dtypes.bfloat16)
    real_part = np.asarray(height, np.float32).reshape(2 * MX, holders, 2, row_count)[:, :, 0]
    row_sum = real_part.sum((1, 2), dtype=np.float64).astype(np.float32)
    cos_t, sin_t = [t.transpose(1, 2, 0) for t in (cosines, sines)]
    up = np.concatenate([cos_t, -sin_t], 2)
    low = np.concatenate([sin_t, cos_t], 2)
    back_rows = jnp.asarray(np.concatenate([up, low], 1).astype(ml_dtypes.bfloat16))
    pairs = waves // 2
    place = np.zeros((2, variables, waves, pairs, 2, 2, SLOTS), np.float32)
    for q in range(2):
        for v in range(variables):
            for m in range(waves):
                place[q, v, m, m // 2, q, m % 2, v] = 1.0
    place = jnp.asarray(place.reshape(2, variables * waves, -1).astype(ml_dtypes.bfloat16))
    bias_row = np.zeros((MX, pairs, 2, 2, SLOTS), np.float32)
    bias_row[:, 0, :, 0, variables] = row_sum.reshape(2, MX).T
    bias_row = jnp.asarray(bias_row.reshape(MX, -1))
    packs = first_core.shape[0] // EIGHT
    first_spread = np.einsum("pk,bc->kpbc", np.eye(packs), np.repeat(np.eye(rank), EIGHT, axis=1))
    first_spread = jnp.asarray(first_spread.reshape(packs, packs * rank, rank * EIGHT).astype(ml_dtypes.bfloat16))
    spread = np.eye(8)[:, None, :, None, None] * np.eye(rank)[None, :, None, None, :] * np.ones((1, 1, 1, 4, 1))
    spread = jnp.asarray(spread.reshape(8 * rank, 32 * rank).astype(ml_dtypes.bfloat16))

    used = (variables + 4) // 4 * 4
    lift = jnp.concatenate(
        [lift_weight, (math.sqrt(points) * lift_bias).astype(jnp.bfloat16)[None],
         jnp.zeros((used - variables - 1, channels), jnp.bfloat16)], 0
    )
    count = input_core.shape[0]
    lift = lax.dynamic_slice_in_dim(lift, lax.axis_index("batch") * count, count, 1)
    inner = jnp.einsum("vc,cde->dve", lift, input_core, preferred_element_type=jnp.float32)
    inner = inner.astype(jnp.bfloat16).reshape(rank, used * rank)
    first = first_core.reshape(packs, EIGHT, rank, rank).transpose(2, 1, 0, 3).reshape(rank * EIGHT, packs * rank)
    outer = output_core.transpose(1, 0, 3, 2).reshape(2 * count, rank * rank)
    mixed = mix(
        fields, forward, first, inner, outer, jnp.asarray(height), place, bias_row,
        second_core.reshape(waves * rank, rank), first_spread, spread, lax.axis_size("batch"),
    )
    return finish(
        mixed, back_rows, fields, width, lift_weight, skip_weight, lift_bias, skip_bias, out_weight.T, out_bias
    )[None]


def solution(mesh):
    placed = (
        P("batch", None, ("mode", "cores"), None),
        P(),
        P(),
        P("batch", None, None),
        P(("mode", "cores"), None, None),
        P("batch", None, None),
        P("batch", None, None, None),
        P(),
        P(),
        P(),
        P(),
    )
    fits = (
        mesh.shape["mode"] == 4 and mesh.shape["cores"] == 2 and MY // 8 == WAVES
        and mesh.shape["batch"] == 4 and MX // 4 % EIGHT == 0 and NX // 8 == 128
    )
    return jax.shard_map(
        fast_shards if fits else shards,
        mesh=mesh,
        in_specs=placed,
        out_specs=P("batch", None, ("mode", "cores"), None),
        check_vma=False,
    )
```

```python
import functools
import math

import jax
import jax.numpy as jnp
import ml_dtypes
import numpy as np
from jax import lax
from jax.experimental import pallas as pl
from jax.experimental.pallas import tpu as pltpu
from jax.sharding import PartitionSpec as P

NX = 1024
NY = 1024
MX = 128
MY = 128


TWO_PI = 2.0 * math.pi


def wave_pair(waves, points, length):
    phase_step = waves[:, None] * points[None, :] % length
    angles = phase_step.astype(jnp.float32) * (TWO_PI / length)
    return (jnp.cos(angles), jnp.sin(angles))


def width_forward(length, wave_count):
    points = jnp.arange(length, dtype=jnp.int32)
    waves = jnp.arange(wave_count, dtype=jnp.int32)
    cosines, sine_part = wave_pair(points, waves, length)
    stacked = jnp.stack([cosines, -sine_part], axis=1) / math.sqrt(length)
    return stacked.astype(jnp.bfloat16)


def height_forward(row_index, wave_count, length):
    waves = jnp.arange(wave_count, dtype=jnp.int32) - wave_count // 2
    cosines, sine_part = wave_pair(waves, row_index, length)
    upper = jnp.stack([cosines, sine_part], axis=1)
    lower = jnp.stack([-sine_part, cosines], axis=1)
    return (jnp.stack([upper, lower], axis=0) / math.sqrt(length)).astype(jnp.bfloat16)


def height_inverse(row_index, wave_count, length):
    waves = jnp.arange(wave_count, dtype=jnp.int32) - wave_count // 2
    cosines, sine_part = wave_pair(row_index, waves, length)
    upper = jnp.stack([cosines, -sine_part], axis=1)
    lower = jnp.stack([sine_part, cosines], axis=1)
    return (jnp.stack([upper, lower], axis=0) / math.sqrt(length)).astype(jnp.bfloat16)


def width_inverse(waves, length):
    points = jnp.arange(length, dtype=jnp.int32)
    cosines, sine_part = wave_pair(waves, points, length)
    weight = jnp.where(waves == 0, 1.0, 2.0).astype(jnp.float32)[:, None]
    stacked = jnp.stack([cosines * weight, -sine_part * weight], axis=0) / math.sqrt(length)
    return stacked.astype(jnp.bfloat16)


def bias_modes(lift_bias, wave_index, length):
    real_row = (
        jnp.where(wave_index == 0, 1.0, 0.0).astype(jnp.float32)[:, None]
        * (math.sqrt(length) * lift_bias)[None, :]
    )
    return jnp.stack([real_row, jnp.zeros_like(real_row)], axis=0)


def lift_modes(modes, lift_weight, lift_bias, wave_index):
    lifted_modes = jnp.einsum(
        "fabpmv,vc->fabpmc", modes, lift_weight, preferred_element_type=jnp.float32
    )
    return (lifted_modes + bias_modes(lift_bias, wave_index, NY)).astype(jnp.bfloat16)


def grid_rows(stored, row_count, holder_count):
    return stored % row_count * holder_count + stored // row_count


def shards(
    fields,
    lift_weight,
    lift_bias,
    first_core,
    second_core,
    input_core,
    output_core,
    skip_weight,
    skip_bias,
    out_weight,
    out_bias,
):
    mode_count = lax.axis_size("mode")
    core_count = lax.axis_size("cores")
    row_count = fields.shape[2]
    block_size = second_core.shape[0]
    block_start = (lax.axis_index("mode") * core_count + lax.axis_index("cores")) * block_size
    local_waves = block_start + jnp.arange(block_size, dtype=jnp.int32)
    lifted = (
        jnp.einsum("fvxy,vc->fxyc", fields, lift_weight, preferred_element_type=jnp.float32)
        + lift_bias
    ).astype(jnp.bfloat16)
    field_modes = jnp.einsum(
        "fvxy,ypk->fxpkv", fields, width_forward(NY, MY), preferred_element_type=jnp.float32
    ).astype(jnp.bfloat16)
    field_modes = field_modes[:, None]
    gathered = (
        lax.all_gather(first_core, "batch", axis=0, tiled=True),
        lax.all_gather(input_core, "batch", axis=0, tiled=True),
        lax.all_gather(output_core, "batch", axis=0, tiled=True),
    )
    first_whole, input_whole, output_whole = gathered
    mode_factor = jnp.einsum(
        "kab,mbd->kmad", first_whole, second_core, preferred_element_type=jnp.float32
    ).astype(jnp.bfloat16)
    arrived = lax.all_to_all(
        field_modes, ("mode", "cores"), split_axis=4, concat_axis=2, tiled=True
    )
    rows_held = jnp.arange(NX, dtype=jnp.int32)[None, :]
    by_mode = lift_modes(arrived, lift_weight, lift_bias, local_waves)
    lead_rows = rows_held.shape[0]
    side_rows = rows_held.shape[1]
    flat_rows = grid_rows(rows_held.reshape(-1), row_count, mode_count * core_count)
    height_table = height_forward(flat_rows, MX, NX).reshape(2, MX, 2, lead_rows, side_rows)
    spectrum = jnp.einsum(
        "qkpab,fabpmc->fqkmc", height_table, by_mode, preferred_element_type=jnp.float32
    ).astype(jnp.bfloat16)
    projected = jnp.einsum(
        "fqkmc,cbe->fqkmbe", spectrum, input_whole, preferred_element_type=jnp.float32
    ).astype(jnp.bfloat16)
    carried = jnp.einsum(
        "kmab,fqkmbe->fqkmae", mode_factor, projected, preferred_element_type=jnp.float32
    ).astype(jnp.bfloat16)
    traced = jnp.einsum(
        "fqkmae,osea->fqkmso", carried, output_whole, preferred_element_type=jnp.float32
    )
    real_part = traced[:, 0, :, :, 0, :] - traced[:, 1, :, :, 1, :]
    imaginary = traced[:, 0, :, :, 1, :] + traced[:, 1, :, :, 0, :]
    mixed_modes = jnp.stack([real_part, imaginary], axis=1).astype(jnp.bfloat16)
    height_back = height_inverse(flat_rows, MX, NX).reshape(2, lead_rows, side_rows, 2, MX)
    col_modes = jnp.einsum(
        "pabqk,fqkmc->fabpmc", height_back, mixed_modes, preferred_element_type=jnp.float32
    ).astype(jnp.bfloat16)
    returned = lax.all_to_all(col_modes, ("mode", "cores"), split_axis=2, concat_axis=4, tiled=True)
    waves_held = jnp.arange(MY, dtype=jnp.int32)
    width_back = width_inverse(waves_held, NY)
    spatial = jnp.einsum(
        "fxpmc,pmy->fxyc", returned[:, 0], width_back, preferred_element_type=jnp.float32
    )
    skip_term = jnp.einsum("fxyc,cd->fxyd", lifted, skip_weight, preferred_element_type=jnp.float32)
    active = jax.nn.gelu(spatial + skip_term + skip_bias, approximate=False).astype(jnp.bfloat16)
    result = (
        jnp.einsum("fxyc,cv->fvxy", active, out_weight, preferred_element_type=jnp.float32)
        + out_bias[:, None, None]
    )
    return result.astype(jnp.bfloat16)


def cyclic_rows(row_count, holders):
    return (np.arange(row_count)[None, :] * holders + np.arange(holders)[:, None]).reshape(-1)


def host_pair(waves, points, length):
    steps = np.asarray(waves)[:, None] * np.asarray(points)[None, :] % length
    angles = steps.astype(np.float32) * np.float32(TWO_PI / length)
    return np.cos(angles), np.sin(angles)


def dense(a, b, contract=((1,), (0,))):
    return lax.dot_general(a, b, (contract, ((), ())), preferred_element_type=jnp.float32)


MESH = pl.DeviceIdType.MESH
WAVES = 16
SLOTS = 32
EIGHT = 8
CHUNKS = (32, 48, 48)
STARTS = (0, 32, 80)
LANES = 512
ROWS = 128
PARTS = 2
TURN = 8


def whole(a):
    return pl.BlockSpec(a.shape, lambda *_: (0,) * a.ndim)


def mix_kernel(
    fields_far, forward, first_own, inner_own, outer_own, height_far, place_far, bias_row, second, first_spread, spread,
    mixed, fields, height, place, modes, arrived, first, inner, outer, stacked, placed, inner_wide, turned_inner, weights, rows,
    blocks, closing, carried, turned, load, send_plane, recv_plane, send_near, recv_near, send_modes, recv_modes,
):
    variables, row_count, points = fields.shape
    holders, lead, flat = arrived.shape
    waves = lead // 2
    kx_count = height.shape[0] // 2
    planes = first.shape[0]
    rank = inner.shape[1]
    channels = mixed.shape[0]
    pairs = waves // 2
    wide = 4 * rank
    slots = inner.shape[2] // rank
    packs = kx_count // EIGHT
    share = variables // PARTS
    mode, batch, core = lax.axis_index("mode"), lax.axis_index("batch"), lax.axis_index("cores")
    me = mode * 2 + core
    near = (mode + 1 - 2 * (mode % 2), batch, core)

    def load_part(c):
        here = pl.ds(c * share, share)
        return pltpu.make_async_copy(fields_far.at[here], fields.at[here], load.at[c])

    def load_table(n):
        return pltpu.make_async_copy((height_far, place_far)[n], (height, place)[n], load.at[PARTS + n])

    for c in range(PARTS):
        load_part(c).start()
    for n in range(2):
        load_table(n).start()

    def flip(bit, change):
        return bit + change - 2 * bit * change

    def peer(t):
        chip, side, line = flip(mode // 2, t // 4), flip(mode % 2, t // 2 % 2), flip(core, t % 2)
        return (chip * 2 + side, batch, line), chip * 4 + side * 2 + line

    def plane(step):
        return (mode, (batch + step) % planes, core)

    barrier = pltpu.get_barrier_semaphore()
    greeted = [peer(t)[0] for t in range(1, holders)] + [plane(step) for step in range(1, planes)]
    for device in greeted:
        pl.semaphore_signal(barrier, inc=1, device_id=device, device_id_type=MESH)
    pl.semaphore_wait(barrier, len(greeted))

    shards_own = (first_own, inner_own, outer_own)
    shards_all = (first, inner, outer)

    def half(n):
        size = shards_own[n].shape[0] // 2
        return pl.ds(pl.multiple_of((mode % 2) * size, size), size)

    def plane_copy(step, n):
        return pltpu.make_async_remote_copy(
            src_ref=shards_own[n].at[half(n)], dst_ref=shards_all[n].at[batch, half(n)],
            send_sem=send_plane.at[step - 1, n], recv_sem=recv_plane.at[step - 1, n],
            device_id=plane(step), device_id_type=MESH,
        )

    def near_copy(step, n):
        held = shards_all[n].at[(batch + planes - step) % planes, half(n)]
        return pltpu.make_async_remote_copy(
            src_ref=held, dst_ref=held, send_sem=send_near.at[step - 1, n], recv_sem=recv_near.at[step - 1, n],
            device_id=near, device_id_type=MESH,
        )

    def modes_copy(t, c):
        device, index = peer(t)
        lanes = pl.ds(c * share * row_count, share * row_count)
        return pltpu.make_async_remote_copy(
            src_ref=modes.at[index, :, lanes], dst_ref=arrived.at[me, :, lanes],
            send_sem=send_modes.at[t - 1, c], recv_sem=recv_modes.at[t - 1, c],
            device_id=device, device_id_type=MESH,
        )

    for n in range(3):
        for step in range(1, planes):
            plane_copy(step, n).start()
    for n in range(3):
        shards_all[n][batch] = shards_own[n][...]

    for c in range(PARTS):
        load_part(c).wait()
        for v in range(c * share, (c + 1) * share, 2):
            both = fields[v:v + 2].reshape(2 * row_count, points)
            got = dense(forward[...], both, ((1,), (1,))).astype(jnp.bfloat16)
            modes[:, :, v * row_count:(v + 2) * row_count] = got.reshape(holders, lead, 2 * row_count)
        for t in range(holders - 1, 0, -1):
            modes_copy(t, c).start()
    arrived[me] = modes[me]

    for n in range(2):
        for step in range(1, planes):
            plane_copy(step, n).wait_recv()
            near_copy(step, n).start()
    for n in range(2):
        for step in range(1, planes):
            near_copy(step, n).wait_recv()

    total = inner[0].astype(jnp.float32)
    for z in range(1, planes):
        total = total + inner[z].astype(jnp.float32)
    total = total.astype(jnp.bfloat16)
    for part in range(slots // 4):
        inner_wide[:, part * 4 * wide:(part + 1) * 4 * wide] = dense(
            total[:, part * wide:(part + 1) * wide], spread[:wide, :4 * wide]
        ).astype(jnp.bfloat16)

    down = lax.broadcasted_iota(jnp.int32, (rank * EIGHT, rank * EIGHT), 0) % EIGHT
    along = lax.broadcasted_iota(jnp.int32, (rank * EIGHT, rank * EIGHT), 1) % EIGHT
    same = down == along
    for z in range(planes):
        for k in range(packs // planes):
            full = dense(first[z], first_spread[k])
            blocks[z * (packs // planes) + k] = jnp.where(same, full, 0.0).astype(jnp.bfloat16)

    turned_inner[...] = jnp.zeros_like(turned_inner)
    group_of = lax.broadcasted_iota(jnp.int32, (SLOTS, wide), 1) // rank

    def weight_step(j, carry):
        start = pl.multiple_of(j * 2 * rank, 2 * rank)
        joined = dense(second[pl.ds(start, 2 * rank), :], inner_wide[...])
        for m in range(2):
            for v in range(slots):
                turned_inner[m, :, v, :] = joined[m * rank:(m + 1) * rank, v * wide:(v + 1) * wide]
        for m in range(2):
            for b in range(rank):
                value = turned_inner[m, b]
                for q in range(2):
                    weights[j, (q * 2 + m) * SLOTS:(q * 2 + m + 1) * SLOTS, b * wide:(b + 1) * wide] = jnp.where(
                        group_of == m * 2 + q, value, 0.0
                    ).astype(jnp.bfloat16)
        return carry

    lax.fori_loop(0, pairs, weight_step, 0)

    for step in range(1, planes):
        plane_copy(step, 2).wait_recv()
        near_copy(step, 2).start()
    for step in range(1, planes):
        near_copy(step, 2).wait_recv()
    count = channels // planes
    lanes = lax.broadcasted_iota(jnp.int32, (count, 8 * wide), 1)
    part_of = lanes // rank % 2
    wave_of = lanes // (2 * rank) % 2
    for part in range(rank // 8):
        for z in range(planes):
            columns = slice(part * 8 * rank, (part + 1) * 8 * rank)
            real = dense(outer[z, :count, columns], spread[...])
            imaginary = dense(outer[z, count:, columns], spread[...])
            for r in range(2):
                value = jnp.where(part_of == 0, imaginary, real) if r else jnp.where(part_of == 0, real, -imaginary)
                for m in range(2):
                    start = (m * 2 + r) * channels + z * count
                    closing[start:start + count, part * 8 * wide:(part + 1) * 8 * wide] = (
                        jnp.where(wave_of == m, value, 0.0).astype(jnp.bfloat16)
                    )

    for n in range(2):
        load_table(n).wait()
    for c in range(PARTS):
        for t in range(1, holders):
            modes_copy(t, c).wait_recv()
    for d in range(holders):
        for p in range(2):
            for v in range(variables):
                stacked[v * waves:(v + 1) * waves, (d * 2 + p) * row_count:(d * 2 + p + 1) * row_count] = (
                    arrived[d, p * waves:(p + 1) * waves, v * row_count:(v + 1) * row_count]
                )
    by = dense(height[...], stacked[...], ((1,), (1,))).astype(jnp.bfloat16)
    first_wave = (me == 0).astype(jnp.float32)
    placed[...] = (
        dense(by[:kx_count], place[0]) + dense(by[kx_count:], place[1]) + bias_row[...] * first_wave
    ).astype(jnp.bfloat16)

    def pair_step(j, carry):
        column = pl.ds(pl.multiple_of(j * wide, wide), wide)
        own = placed[:, column]
        for part in range(rank // 8):
            got = dense(own, weights[j, :, part * 8 * wide:(part + 1) * 8 * wide])
            for k in range(packs):
                rows[k, part * 64:(part + 1) * 64, column] = jnp.concatenate(
                    [got[k * EIGHT:(k + 1) * EIGHT, b * wide:(b + 1) * wide] for b in range(8)], axis=0
                ).astype(jnp.bfloat16)
        return carry

    lax.fori_loop(0, pairs, pair_step, 0)

    def first_step(k, carry):
        here = pl.ds(pl.multiple_of(k * 2 * EIGHT, 2 * EIGHT), 2 * EIGHT)
        for part in range(pairs // 2):
            one, two = [
                dense(blocks[2 * k + i], rows[2 * k + i, :, part * 2 * wide:(part + 1) * 2 * wide]) for i in range(2)
            ]
            for j in range(2):
                side = slice(j * wide, (j + 1) * wide)
                for a in range(rank):
                    level = slice(a * EIGHT, (a + 1) * EIGHT)
                    carried[part * 2 + j, here, a * wide:(a + 1) * wide] = jnp.concatenate(
                        [one[level, side], two[level, side]], axis=0
                    ).astype(jnp.bfloat16)
        return carry

    lax.fori_loop(0, packs // 2, first_step, 0)

    for part in range(pairs // 2):
        both = carried[part * 2:part * 2 + 2].reshape(2 * kx_count, rank * wide)
        got = dense(closing[...], both, ((1,), (1,)))
        for m in range(2):
            for r in range(2):
                for j in range(2):
                    turned[:, (part * 2 + j) * 2 + m, r * kx_count:(r + 1) * kx_count] = got[
                        (m * 2 + r) * channels:(m * 2 + r + 1) * channels, j * kx_count:(j + 1) * kx_count
                    ]
    mixed[...] = turned[...].astype(jnp.bfloat16)

    for n in range(3):
        for step in range(1, planes):
            plane_copy(step, n).wait_send()
            near_copy(step, n).wait_send()
    for c in range(PARTS):
        for t in range(1, holders):
            modes_copy(t, c).wait_send()


def mix(fields, forward, first, inner, outer, height, place, bias_row, second, first_spread, spread, planes):
    variables, row_count, points = fields.shape
    holders = forward.shape[0] // (2 * WAVES)
    waves = WAVES
    kx2, depth = height.shape
    rank = inner.shape[0]
    channels = outer.shape[0] // 2 * planes
    wide = 4 * rank
    slots = inner.shape[1] // rank
    packs = kx2 // 2 // EIGHT
    operands = (fields, forward, first, inner, outer, height, place, bias_row, second, first_spread, spread)
    return pl.pallas_call(
        mix_kernel,
        in_specs=[pl.BlockSpec(memory_space=pl.ANY if n in (0, 5, 6) else pltpu.VMEM) for n in range(len(operands))],
        out_specs=pl.BlockSpec(memory_space=pltpu.VMEM),
        out_shape=jax.ShapeDtypeStruct((channels, waves, kx2), jnp.bfloat16),
        scratch_shapes=[
            pltpu.VMEM(fields.shape, jnp.bfloat16),
            pltpu.VMEM(height.shape, jnp.bfloat16),
            pltpu.VMEM(place.shape, jnp.bfloat16),
            pltpu.VMEM((holders, 2 * waves, variables * row_count), jnp.bfloat16),
            pltpu.VMEM((holders, 2 * waves, variables * row_count), jnp.bfloat16),
            pltpu.VMEM((planes,) + first.shape, jnp.bfloat16),
            pltpu.VMEM((planes,) + inner.shape, jnp.bfloat16),
            pltpu.VMEM((planes,) + outer.shape, jnp.bfloat16),
            pltpu.VMEM((place.shape[1], depth), jnp.bfloat16),
            pltpu.VMEM((kx2 // 2, waves // 2 * wide), jnp.bfloat16),
            pltpu.VMEM((rank, slots * wide), jnp.bfloat16),
            pltpu.VMEM((2, rank, SLOTS, wide), jnp.float32),
            pltpu.VMEM((waves // 2, 4 * SLOTS, rank * wide), jnp.bfloat16),
            pltpu.VMEM((packs, rank * EIGHT, waves // 2 * wide), jnp.bfloat16),
            pltpu.VMEM((packs, rank * EIGHT, rank * EIGHT), jnp.bfloat16),
            pltpu.VMEM((4 * channels, rank * wide), jnp.bfloat16),
            pltpu.VMEM((waves // 2, kx2 // 2, rank * wide), jnp.bfloat16),
            pltpu.VMEM((channels, waves, kx2), jnp.float32),
            pltpu.SemaphoreType.DMA((PARTS + 2,)),
            pltpu.SemaphoreType.DMA((planes - 1, 3)),
            pltpu.SemaphoreType.DMA((planes - 1, 3)),
            pltpu.SemaphoreType.DMA((planes - 1, 3)),
            pltpu.SemaphoreType.DMA((planes - 1, 3)),
            pltpu.SemaphoreType.DMA((holders - 1, PARTS)),
            pltpu.SemaphoreType.DMA((holders - 1, PARTS)),
        ],
        compiler_params=pltpu.CompilerParams(
            collective_id=1, has_side_effects=True, vmem_limit_bytes=60 * 2**20
        ),
        name="mix",
    )(*operands)


def gelu(h):
    return h * (0.5 + 0.5 * lax.erf(h * (1.0 / math.sqrt(2.0))))


def finish_kernel(
    mixed, back_far, fields_far, width, lift_weight, skip_weight, lift_bias, skip_bias, out_weight, out_bias, tall, wide,
    result_far, gathered, back, fields, source, cols, total, skip, closing, last_bias, active, load, leave, send, recv,
):
    channels, waves, kx2 = mixed.shape
    variables, row_count, points = fields.shape
    inner = variables * EIGHT
    steps = row_count // EIGHT // 2
    mode, batch, core = lax.axis_index("mode"), lax.axis_index("batch"), lax.axis_index("cores")
    near = (mode + 1 - 2 * (mode % 2), batch, core)
    by_x = ((mode + 2) % 4, batch, core)
    by_y = (mode, batch, 1 - core)

    def owner(device):
        return device[0] * 2 + device[2]

    me = owner((mode, batch, core))
    at_x, at_y = owner(by_x), owner(by_y)
    across = owner((by_x[0], batch, by_y[2]))

    barrier = pltpu.get_barrier_semaphore()
    for device in (near, by_x, by_y):
        pl.semaphore_signal(barrier, inc=1, device_id=device, device_id_type=MESH)
    pl.semaphore_wait(barrier, 3)

    def piece(holder, first, count):
        return gathered.at[pl.ds(first, count), pl.ds(pl.multiple_of(holder * waves, waves), waves), :]

    def copy(g, kind):
        low, share = STARTS[g], CHUNKS[g]
        half = share // 2
        own = mixed.at[pl.ds(low, share)]
        home = piece(me, low, share)
        x_all, y_all = piece(at_x, low, share), piece(at_y, low, share)
        x_low, y_high = piece(at_x, low, half), piece(at_y, low + half, half)
        d_low, d_high = piece(across, low, half), piece(across, low + half, half)
        from_, to, device = (
            (own, home, near), (own, home, by_x), (own, home, by_y),
            (x_all, x_all, near), (y_all, y_all, near),
            (x_low, x_low, by_y), (y_high, y_high, by_x),
            (d_low, d_low, near), (d_high, d_high, near),
        )[kind]
        return pltpu.make_async_remote_copy(
            src_ref=from_, dst_ref=to, send_sem=send.at[g, kind], recv_sem=recv.at[g, kind],
            device_id=device, device_id_type=MESH,
        )

    def begin(g, kinds):
        for kind in kinds:
            copy(g, kind).start()

    def came(g, kinds):
        for kind in kinds:
            copy(g, kind).wait_recv()

    def relay(g):
        came(g, (1, 2))
        begin(g, (5, 6, 3, 4))
        if g + 1 < len(CHUNKS):
            begin(g + 1, (1, 2, 0))

    def relay_last(g):
        came(g, (5, 6))
        begin(g, (7, 8))

    begin(0, (1, 2, 0))
    loads = [
        pltpu.make_async_copy(fields_far, fields, load.at[0]),
        pltpu.make_async_copy(back_far.at[me], back, load.at[1]),
    ]
    for one in loads:
        one.start()
    gathered[:, pl.ds(pl.multiple_of(me * waves, waves), waves), :] = mixed[...]

    depth = skip.shape[1]
    line = lax.broadcasted_iota(jnp.int32, (depth - inner, points), 0)
    ones = jnp.where(line < 2, 1.0, 0.0).astype(jnp.bfloat16)
    for one in loads:
        one.wait()
    for x in range(steps):
        rows = fields[:, x * 2 * EIGHT:(x + 1) * 2 * EIGHT, :]
        for h in range(2):
            source[x * 2 + h, :inner, :] = rows[:, h * EIGHT:(h + 1) * EIGHT, :].reshape(inner, points)
            source[x * 2 + h, inner:, :] = ones
    relay(0)

    direct = dense(lift_weight[...], skip_weight[...]).astype(jnp.bfloat16)
    row_bias = lax.dot_general(
        jnp.broadcast_to(lift_bias[...], (8, channels)), skip_weight[...].astype(jnp.float32),
        (((1,), (0,)), ((), ())), preferred_element_type=jnp.float32, precision=lax.Precision.HIGHEST,
    )[:1] + skip_bias[...]
    size = 256
    down = lax.broadcasted_iota(jnp.int32, (size, depth), 0) % EIGHT
    along = lax.broadcasted_iota(jnp.int32, (size, depth), 1)
    for part in range(channels * EIGHT // size):
        here = slice(part * size, (part + 1) * size)
        picked = dense(tall[here, :], direct, ((1,), (1,))).astype(jnp.bfloat16)
        spread = dense(picked, wide[:variables, :depth])
        column = jnp.sum(tall[here, :].astype(jnp.float32) * row_bias, axis=1, keepdims=True)
        high = column.astype(jnp.bfloat16).astype(jnp.float32)
        rest = jnp.where(along == inner, high, jnp.where(along == inner + 1, column - high, 0.0))
        skip[here, :] = jnp.where(
            along < inner, jnp.where(down == along % EIGHT, spread, 0.0), rest
        ).astype(jnp.bfloat16)
    chosen = dense(tall[:inner, :variables], out_weight[...]).astype(jnp.bfloat16)
    down = lax.broadcasted_iota(jnp.int32, (inner, channels * EIGHT), 0) % EIGHT
    along = lax.broadcasted_iota(jnp.int32, (inner, channels * EIGHT), 1) % EIGHT
    closing[...] = jnp.where(down == along, dense(chosen, wide[...]), 0.0).astype(jnp.bfloat16)
    column = jnp.sum(tall[:inner, :variables].astype(jnp.float32) * out_bias[...], axis=1, keepdims=True)
    last_bias[...] = jnp.broadcast_to(column, last_bias.shape)
    relay_last(0)

    def turn(g):
        def step(c, carry):
            both = gathered[pl.ds(STARTS[g] + TURN * c, TURN)].reshape(TURN * waves * 8, kx2)
            got = dense(back[...], both, ((1,), (1,)))
            size = got.shape[1] // TURN
            for k in range(TURN // 2):
                place = pl.ds(pl.multiple_of(c * TURN * EIGHT + k * 2 * EIGHT, 2 * EIGHT), 2 * EIGHT)
                for p in range(2):
                    for x in range(row_count // EIGHT):
                        rows = got[p * row_count + x * EIGHT:p * row_count + (x + 1) * EIGHT, :]
                        cols[x, place, p * size:(p + 1) * size] = jnp.concatenate(
                            [rows[:, 2 * k * size:(2 * k + 1) * size], rows[:, (2 * k + 1) * size:(2 * k + 2) * size]],
                            axis=0,
                        ).astype(jnp.bfloat16)
            return carry

        lax.fori_loop(0, CHUNKS[g] // TURN, step, 0)

    def leave_rows(i):
        place = pl.ds(pl.multiple_of(i * 2 * EIGHT, 2 * EIGHT), 2 * EIGHT)
        return pltpu.make_async_copy(fields.at[:, place, :], result_far.at[:, place, :], leave.at[i])

    def finish_rows(g, low, high):
        start, size = STARTS[g] * EIGHT, CHUNKS[g] * EIGHT

        def step(i, carry):
            for lane in range(points // LANES):
                lanes = slice(lane * LANES, (lane + 1) * LANES)
                done = []
                for h in range(2):
                    x = 2 * i + h
                    for part in range(0, size, ROWS):
                        height = (
                            dense(cols[x, part:part + ROWS, :], width[:, lanes])
                            + dense(skip[start + part:start + part + ROWS, :], source[x, :, lanes])
                        )
                        active[lane * 2 + h, part:part + ROWS, :] = gelu(height).astype(jnp.bfloat16)
                for h in range(2):
                    x = 2 * i + h
                    got = dense(closing[:, start:start + size], active[lane * 2 + h, :size, :])
                    if g == 0:
                        got = got + jnp.concatenate([last_bias[...]] * (LANES // 128), axis=1)
                    else:
                        got = got + total[x, :, lanes]
                    if g + 1 < len(CHUNKS):
                        total[x, :, lanes] = got
                    else:
                        done.append(got.reshape(variables, EIGHT, LANES))
                if done:
                    place = pl.ds(pl.multiple_of(i * 2 * EIGHT, 2 * EIGHT), 2 * EIGHT)
                    fields[:, place, lanes] = jnp.concatenate(done, axis=1).astype(jnp.bfloat16)
            if g + 1 == len(CHUNKS):
                leave_rows(i).start()
            return carry

        lax.fori_loop(low, high, step, 0)

    for g in range(len(CHUNKS)):
        came(g, (0, 3, 4, 7, 8))
        turn(g)
        if g + 1 < len(CHUNKS):
            finish_rows(g, 0, steps // 4)
            relay(g + 1)
            finish_rows(g, steps // 4, 3 * steps // 4)
            relay_last(g + 1)
            finish_rows(g, 3 * steps // 4, steps)
        else:
            finish_rows(g, 0, steps)
    for g in range(len(CHUNKS)):
        for kind in range(9):
            copy(g, kind).wait_send()

    def leave_step(i, carry):
        leave_rows(i).wait()
        return carry

    lax.fori_loop(0, steps, leave_step, 0)


def finish(mixed, back, fields, width, lift_weight, skip_weight, lift_bias, skip_bias, out_weight, out_bias):
    channels, waves, kx2 = mixed.shape
    variables, row_count, points = fields.shape
    tall = jnp.asarray(np.repeat(np.eye(channels), EIGHT, axis=0).astype(ml_dtypes.bfloat16))
    wide = jnp.asarray(np.repeat(np.eye(channels), EIGHT, axis=1).astype(ml_dtypes.bfloat16))
    operands = (
        mixed, back, fields, width, lift_weight, skip_weight, lift_bias[None], skip_bias[None], out_weight,
        out_bias[None], tall, wide,
    )
    blocks = row_count // EIGHT
    inner = variables * EIGHT
    depth = inner + 2 * EIGHT
    return pl.pallas_call(
        finish_kernel,
        in_specs=[pl.BlockSpec(memory_space=pl.ANY if n in (1, 2) else pltpu.VMEM) for n in range(len(operands))],
        out_specs=pl.BlockSpec(memory_space=pl.ANY),
        out_shape=jax.ShapeDtypeStruct(fields.shape, jnp.bfloat16),
        scratch_shapes=[
            pltpu.VMEM((channels, 8 * waves, kx2), jnp.bfloat16),
            pltpu.VMEM(back.shape[1:], jnp.bfloat16),
            pltpu.VMEM(fields.shape, jnp.bfloat16),
            pltpu.VMEM((blocks, depth, points), jnp.bfloat16),
            pltpu.VMEM((blocks, max(CHUNKS) * EIGHT, width.shape[0]), jnp.bfloat16),
            pltpu.VMEM((blocks, inner, points), jnp.float32),
            pltpu.VMEM((channels * EIGHT, depth), jnp.bfloat16),
            pltpu.VMEM((inner, channels * EIGHT), jnp.bfloat16),
            pltpu.VMEM((inner, 128), jnp.float32),
            pltpu.VMEM((points // LANES * 2, max(CHUNKS) * EIGHT, LANES), jnp.bfloat16),
            pltpu.SemaphoreType.DMA((2,)),
            pltpu.SemaphoreType.DMA((blocks // 2,)),
            pltpu.SemaphoreType.DMA((len(CHUNKS), 9)),
            pltpu.SemaphoreType.DMA((len(CHUNKS), 9)),
        ],
        compiler_params=pltpu.CompilerParams(
            collective_id=0, has_side_effects=True, vmem_limit_bytes=60 * 2**20
        ),
        name="finish",
    )(*operands)


def fast_shards(
    fields, lift_weight, lift_bias, first_core, second_core, input_core, output_core,
    skip_weight, skip_bias, out_weight, out_bias,
):
    holders = lax.axis_size("mode") * lax.axis_size("cores")
    waves, rank, _ = second_core.shape
    _, variables, row_count, points = fields.shape
    channels = lift_weight.shape[1]
    fields = fields[0]

    cosines, sines = host_pair(np.arange(MY), np.arange(points), points)
    root = math.sqrt(points)
    forward = np.stack([cosines, -sines], 0).reshape(2, holders, waves, points).transpose(1, 0, 2, 3)
    forward = jnp.asarray((forward.reshape(2 * MY, points) / root).astype(np.float32).astype(ml_dtypes.bfloat16))
    weight = np.where(np.arange(MY) == 0, 1.0, 2.0).astype(np.float32)[:, None]
    width = np.concatenate([cosines * weight, -sines * weight], 0) / root
    width = jnp.asarray(width.astype(ml_dtypes.bfloat16))
    order = cyclic_rows(row_count, holders)
    root = math.sqrt(NX)
    cosines, sines = host_pair(np.arange(MX) - MX // 2, order, NX)
    cosines, sines = [t.reshape(MX, holders, row_count) / root for t in (cosines, sines)]
    upper = np.stack([cosines, sines], 2)
    lower = np.stack([-sines, cosines], 2)
    height = np.stack([upper, lower], 0).reshape(2 * MX, -1).astype(ml_dtypes.bfloat16)
    real_part = np.asarray(height, np.float32).reshape(2 * MX, holders, 2, row_count)[:, :, 0]
    row_sum = real_part.sum((1, 2), dtype=np.float64).astype(np.float32)
    cos_t, sin_t = [t.transpose(1, 2, 0) for t in (cosines, sines)]
    up = np.concatenate([cos_t, -sin_t], 2)
    low = np.concatenate([sin_t, cos_t], 2)
    back_rows = jnp.asarray(np.concatenate([up, low], 1).astype(ml_dtypes.bfloat16))
    pairs = waves // 2
    place = np.zeros((2, variables, waves, pairs, 2, 2, SLOTS), np.float32)
    for q in range(2):
        for v in range(variables):
            for m in range(waves):
                place[q, v, m, m // 2, q, m % 2, v] = 1.0
    place = jnp.asarray(place.reshape(2, variables * waves, -1).astype(ml_dtypes.bfloat16))
    bias_row = np.zeros((MX, pairs, 2, 2, SLOTS), np.float32)
    bias_row[:, 0, :, 0, variables] = row_sum.reshape(2, MX).T
    bias_row = jnp.asarray(bias_row.reshape(MX, -1))
    packs = first_core.shape[0] // EIGHT
    first_spread = np.einsum("pk,bc->kpbc", np.eye(packs), np.repeat(np.eye(rank), EIGHT, axis=1))
    first_spread = jnp.asarray(first_spread.reshape(packs, packs * rank, rank * EIGHT).astype(ml_dtypes.bfloat16))
    spread = np.eye(8)[:, None, :, None, None] * np.eye(rank)[None, :, None, None, :] * np.ones((1, 1, 1, 4, 1))
    spread = jnp.asarray(spread.reshape(8 * rank, 32 * rank).astype(ml_dtypes.bfloat16))

    used = (variables + 4) // 4 * 4
    lift = jnp.concatenate(
        [lift_weight, (math.sqrt(points) * lift_bias).astype(jnp.bfloat16)[None],
         jnp.zeros((used - variables - 1, channels), jnp.bfloat16)], 0
    )
    count = input_core.shape[0]
    lift = lax.dynamic_slice_in_dim(lift, lax.axis_index("batch") * count, count, 1)
    inner = jnp.einsum("vc,cde->dve", lift, input_core, preferred_element_type=jnp.float32)
    inner = inner.astype(jnp.bfloat16).reshape(rank, used * rank)
    first = first_core.reshape(packs, EIGHT, rank, rank).transpose(2, 1, 0, 3).reshape(rank * EIGHT, packs * rank)
    outer = output_core.transpose(1, 0, 3, 2).reshape(2 * count, rank * rank)
    mixed = mix(
        fields, forward, first, inner, outer, jnp.asarray(height), place, bias_row,
        second_core.reshape(waves * rank, rank), first_spread, spread, lax.axis_size("batch"),
    )
    return finish(
        mixed, back_rows, fields, width, lift_weight, skip_weight, lift_bias, skip_bias, out_weight.T, out_bias
    )[None]


def solution(mesh):
    placed = (
        P("batch", None, ("mode", "cores"), None),
        P(),
        P(),
        P("batch", None, None),
        P(("mode", "cores"), None, None),
        P("batch", None, None),
        P("batch", None, None, None),
        P(),
        P(),
        P(),
        P(),
    )
    fits = (
        mesh.shape["mode"] == 4 and mesh.shape["cores"] == 2 and MY // 8 == WAVES
        and mesh.shape["batch"] == 4 and MX // 4 % EIGHT == 0 and NX // 8 == 128
    )
    return jax.shard_map(
        fast_shards if fits else shards,
        mesh=mesh,
        in_specs=placed,
        out_specs=P("batch", None, ("mode", "cores"), None),
        check_vma=False,
    )
```

```python
import functools
import math

import jax
import jax.numpy as jnp
import ml_dtypes
import numpy as np
from jax import lax
from jax.experimental import pallas as pl
from jax.experimental.pallas import tpu as pltpu
from jax.sharding import PartitionSpec as P

NX = 1024
NY = 1024
MX = 128
MY = 128


TWO_PI = 2.0 * math.pi


def wave_pair(waves, points, length):
    phase_step = waves[:, None] * points[None, :] % length
    angles = phase_step.astype(jnp.float32) * (TWO_PI / length)
    return (jnp.cos(angles), jnp.sin(angles))


def width_forward(length, wave_count):
    points = jnp.arange(length, dtype=jnp.int32)
    waves = jnp.arange(wave_count, dtype=jnp.int32)
    cosines, sine_part = wave_pair(points, waves, length)
    stacked = jnp.stack([cosines, -sine_part], axis=1) / math.sqrt(length)
    return stacked.astype(jnp.bfloat16)


def height_forward(row_index, wave_count, length):
    waves = jnp.arange(wave_count, dtype=jnp.int32) - wave_count // 2
    cosines, sine_part = wave_pair(waves, row_index, length)
    upper = jnp.stack([cosines, sine_part], axis=1)
    lower = jnp.stack([-sine_part, cosines], axis=1)
    return (jnp.stack([upper, lower], axis=0) / math.sqrt(length)).astype(jnp.bfloat16)


def height_inverse(row_index, wave_count, length):
    waves = jnp.arange(wave_count, dtype=jnp.int32) - wave_count // 2
    cosines, sine_part = wave_pair(row_index, waves, length)
    upper = jnp.stack([cosines, -sine_part], axis=1)
    lower = jnp.stack([sine_part, cosines], axis=1)
    return (jnp.stack([upper, lower], axis=0) / math.sqrt(length)).astype(jnp.bfloat16)


def width_inverse(waves, length):
    points = jnp.arange(length, dtype=jnp.int32)
    cosines, sine_part = wave_pair(waves, points, length)
    weight = jnp.where(waves == 0, 1.0, 2.0).astype(jnp.float32)[:, None]
    stacked = jnp.stack([cosines * weight, -sine_part * weight], axis=0) / math.sqrt(length)
    return stacked.astype(jnp.bfloat16)


def bias_modes(lift_bias, wave_index, length):
    real_row = (
        jnp.where(wave_index == 0, 1.0, 0.0).astype(jnp.float32)[:, None]
        * (math.sqrt(length) * lift_bias)[None, :]
    )
    return jnp.stack([real_row, jnp.zeros_like(real_row)], axis=0)


def lift_modes(modes, lift_weight, lift_bias, wave_index):
    lifted_modes = jnp.einsum(
        "fabpmv,vc->fabpmc", modes, lift_weight, preferred_element_type=jnp.float32
    )
    return (lifted_modes + bias_modes(lift_bias, wave_index, NY)).astype(jnp.bfloat16)


def grid_rows(stored, row_count, holder_count):
    return stored % row_count * holder_count + stored // row_count


def shards(
    fields,
    lift_weight,
    lift_bias,
    first_core,
    second_core,
    input_core,
    output_core,
    skip_weight,
    skip_bias,
    out_weight,
    out_bias,
):
    mode_count = lax.axis_size("mode")
    core_count = lax.axis_size("cores")
    row_count = fields.shape[2]
    block_size = second_core.shape[0]
    block_start = (lax.axis_index("mode") * core_count + lax.axis_index("cores")) * block_size
    local_waves = block_start + jnp.arange(block_size, dtype=jnp.int32)
    lifted = (
        jnp.einsum("fvxy,vc->fxyc", fields, lift_weight, preferred_element_type=jnp.float32)
        + lift_bias
    ).astype(jnp.bfloat16)
    field_modes = jnp.einsum(
        "fvxy,ypk->fxpkv", fields, width_forward(NY, MY), preferred_element_type=jnp.float32
    ).astype(jnp.bfloat16)
    field_modes = field_modes[:, None]
    gathered = (
        lax.all_gather(first_core, "batch", axis=0, tiled=True),
        lax.all_gather(input_core, "batch", axis=0, tiled=True),
        lax.all_gather(output_core, "batch", axis=0, tiled=True),
    )
    first_whole, input_whole, output_whole = gathered
    mode_factor = jnp.einsum(
        "kab,mbd->kmad", first_whole, second_core, preferred_element_type=jnp.float32
    ).astype(jnp.bfloat16)
    arrived = lax.all_to_all(
        field_modes, ("mode", "cores"), split_axis=4, concat_axis=2, tiled=True
    )
    rows_held = jnp.arange(NX, dtype=jnp.int32)[None, :]
    by_mode = lift_modes(arrived, lift_weight, lift_bias, local_waves)
    lead_rows = rows_held.shape[0]
    side_rows = rows_held.shape[1]
    flat_rows = grid_rows(rows_held.reshape(-1), row_count, mode_count * core_count)
    height_table = height_forward(flat_rows, MX, NX).reshape(2, MX, 2, lead_rows, side_rows)
    spectrum = jnp.einsum(
        "qkpab,fabpmc->fqkmc", height_table, by_mode, preferred_element_type=jnp.float32
    ).astype(jnp.bfloat16)
    projected = jnp.einsum(
        "fqkmc,cbe->fqkmbe", spectrum, input_whole, preferred_element_type=jnp.float32
    ).astype(jnp.bfloat16)
    carried = jnp.einsum(
        "kmab,fqkmbe->fqkmae", mode_factor, projected, preferred_element_type=jnp.float32
    ).astype(jnp.bfloat16)
    traced = jnp.einsum(
        "fqkmae,osea->fqkmso", carried, output_whole, preferred_element_type=jnp.float32
    )
    real_part = traced[:, 0, :, :, 0, :] - traced[:, 1, :, :, 1, :]
    imaginary = traced[:, 0, :, :, 1, :] + traced[:, 1, :, :, 0, :]
    mixed_modes = jnp.stack([real_part, imaginary], axis=1).astype(jnp.bfloat16)
    height_back = height_inverse(flat_rows, MX, NX).reshape(2, lead_rows, side_rows, 2, MX)
    col_modes = jnp.einsum(
        "pabqk,fqkmc->fabpmc", height_back, mixed_modes, preferred_element_type=jnp.float32
    ).astype(jnp.bfloat16)
    returned = lax.all_to_all(col_modes, ("mode", "cores"), split_axis=2, concat_axis=4, tiled=True)
    waves_held = jnp.arange(MY, dtype=jnp.int32)
    width_back = width_inverse(waves_held, NY)
    spatial = jnp.einsum(
        "fxpmc,pmy->fxyc", returned[:, 0], width_back, preferred_element_type=jnp.float32
    )
    skip_term = jnp.einsum("fxyc,cd->fxyd", lifted, skip_weight, preferred_element_type=jnp.float32)
    active = jax.nn.gelu(spatial + skip_term + skip_bias, approximate=False).astype(jnp.bfloat16)
    result = (
        jnp.einsum("fxyc,cv->fvxy", active, out_weight, preferred_element_type=jnp.float32)
        + out_bias[:, None, None]
    )
    return result.astype(jnp.bfloat16)


def cyclic_rows(row_count, holders):
    return (np.arange(row_count)[None, :] * holders + np.arange(holders)[:, None]).reshape(-1)


def host_pair(waves, points, length):
    steps = np.asarray(waves)[:, None] * np.asarray(points)[None, :] % length
    angles = steps.astype(np.float32) * np.float32(TWO_PI / length)
    return np.cos(angles), np.sin(angles)


def dense(a, b, contract=((1,), (0,))):
    return lax.dot_general(a, b, (contract, ((), ())), preferred_element_type=jnp.float32)


MESH = pl.DeviceIdType.MESH
WAVES = 16
SLOTS = 32
EIGHT = 8
CHUNKS = (32, 48, 48)
STARTS = (0, 32, 80)
LANES = 512
ROWS = 128
PARTS = 2
TURN = 8


def whole(a):
    return pl.BlockSpec(a.shape, lambda *_: (0,) * a.ndim)


def mix_kernel(
    fields_far, forward, first_core, inner_own, outer_own, height_far, place_far, bias_row, second, first_spread, spread,
    mixed, first_wide, first_turned, first_own, fields, height, place, modes, arrived, first, inner, outer, stacked, placed, inner_wide, turned_inner, weights, rows,
    blocks, closing, carried, turned, load, send_plane, recv_plane, send_near, recv_near, send_modes, recv_modes,
):
    variables, row_count, points = fields.shape
    holders, lead, flat = arrived.shape
    waves = lead // 2
    kx_count = height.shape[0] // 2
    planes = first.shape[0]
    rank = inner.shape[1]
    channels = mixed.shape[0]
    pairs = waves // 2
    wide = 4 * rank
    slots = inner.shape[2] // rank
    packs = kx_count // EIGHT
    share = variables // PARTS
    mode, batch, core = lax.axis_index("mode"), lax.axis_index("batch"), lax.axis_index("cores")
    me = mode * 2 + core
    near = (mode + 1 - 2 * (mode % 2), batch, core)

    def load_part(c):
        here = pl.ds(c * share, share)
        return pltpu.make_async_copy(fields_far.at[here], fields.at[here], load.at[c])

    def load_table(n):
        return pltpu.make_async_copy((height_far, place_far)[n], (height, place)[n], load.at[PARTS + n])

    for c in range(PARTS):
        load_part(c).start()
    for n in range(2):
        load_table(n).start()

    def flip(bit, change):
        return bit + change - 2 * bit * change

    def peer(t):
        chip, side, line = flip(mode // 2, t // 4), flip(mode % 2, t // 2 % 2), flip(core, t % 2)
        return (chip * 2 + side, batch, line), chip * 4 + side * 2 + line

    def plane(step):
        return (mode, (batch + step) % planes, core)

    barrier = pltpu.get_barrier_semaphore()
    greeted = [peer(t)[0] for t in range(1, holders)] + [plane(step) for step in range(1, planes)]
    for device in greeted:
        pl.semaphore_signal(barrier, inc=1, device_id=device, device_id_type=MESH)
    pl.semaphore_wait(barrier, len(greeted))

    shards_own = (first_own, inner_own, outer_own)
    shards_all = (first, inner, outer)

    def half(n):
        size = shards_own[n].shape[0] // 2
        return pl.ds(pl.multiple_of((mode % 2) * size, size), size)

    def plane_copy(step, n):
        return pltpu.make_async_remote_copy(
            src_ref=shards_own[n].at[half(n)], dst_ref=shards_all[n].at[batch, half(n)],
            send_sem=send_plane.at[step - 1, n], recv_sem=recv_plane.at[step - 1, n],
            device_id=plane(step), device_id_type=MESH,
        )

    def near_copy(step, n):
        held = shards_all[n].at[(batch + planes - step) % planes, half(n)]
        return pltpu.make_async_remote_copy(
            src_ref=held, dst_ref=held, send_sem=send_near.at[step - 1, n], recv_sem=recv_near.at[step - 1, n],
            device_id=near, device_id_type=MESH,
        )

    def modes_copy(t, c):
        device, index = peer(t)
        lanes = pl.ds(c * share * row_count, share * row_count)
        return pltpu.make_async_remote_copy(
            src_ref=modes.at[index, :, lanes], dst_ref=arrived.at[me, :, lanes],
            send_sem=send_modes.at[t - 1, c], recv_sem=recv_modes.at[t - 1, c],
            device_id=device, device_id_type=MESH,
        )

    first_wide[...] = first_core[...].astype(jnp.float32)
    along = lax.broadcasted_iota(jnp.int32, (rank, first_own.shape[1]), 1)
    down = lax.broadcasted_iota(jnp.int32, (rank, first_own.shape[1]), 0)
    joined = None
    for k in range(packs // planes):
        for a in range(rank):
            first_turned[k, a * EIGHT:(a + 1) * EIGHT, :] = first_wide[k * EIGHT:(k + 1) * EIGHT, a, :]
        here = jnp.where(along == down + k * rank, 1.0, 0.0).astype(jnp.bfloat16)
        got = dense(first_turned[k].astype(jnp.bfloat16), here)
        joined = got if joined is None else joined + got
    first_own[...] = joined.astype(jnp.bfloat16)

    for n in range(3):
        for step in range(1, planes):
            plane_copy(step, n).start()
    for n in range(3):
        shards_all[n][batch] = shards_own[n][...]

    for c in range(PARTS):
        load_part(c).wait()
        for v in range(c * share, (c + 1) * share, 2):
            both = fields[v:v + 2].reshape(2 * row_count, points)
            got = dense(forward[...], both, ((1,), (1,))).astype(jnp.bfloat16)
            modes[:, :, v * row_count:(v + 2) * row_count] = got.reshape(holders, lead, 2 * row_count)
        for t in range(holders - 1, 0, -1):
            modes_copy(t, c).start()
    arrived[me] = modes[me]

    for n in range(2):
        for step in range(1, planes):
            plane_copy(step, n).wait_recv()
            near_copy(step, n).start()
    for n in range(2):
        for step in range(1, planes):
            near_copy(step, n).wait_recv()

    total = inner[0].astype(jnp.float32)
    for z in range(1, planes):
        total = total + inner[z].astype(jnp.float32)
    total = total.astype(jnp.bfloat16)
    for part in range(slots // 4):
        inner_wide[:, part * 4 * wide:(part + 1) * 4 * wide] = dense(
            total[:, part * wide:(part + 1) * wide], spread[:wide, :4 * wide]
        ).astype(jnp.bfloat16)

    down = lax.broadcasted_iota(jnp.int32, (rank * EIGHT, rank * EIGHT), 0) % EIGHT
    along = lax.broadcasted_iota(jnp.int32, (rank * EIGHT, rank * EIGHT), 1) % EIGHT
    same = down == along
    for z in range(planes):
        for k in range(packs // planes):
            full = dense(first[z], first_spread[k])
            blocks[z * (packs // planes) + k] = jnp.where(same, full, 0.0).astype(jnp.bfloat16)

    turned_inner[...] = jnp.zeros_like(turned_inner)
    group_of = lax.broadcasted_iota(jnp.int32, (SLOTS, wide), 1) // rank

    def weight_step(j, carry):
        start = pl.multiple_of(j * 2 * rank, 2 * rank)
        joined = dense(second[pl.ds(start, 2 * rank), :], inner_wide[...])
        for m in range(2):
            for v in range(slots):
                turned_inner[m, :, v, :] = joined[m * rank:(m + 1) * rank, v * wide:(v + 1) * wide]
        for m in range(2):
            for b in range(rank):
                value = turned_inner[m, b]
                for q in range(2):
                    weights[j, (q * 2 + m) * SLOTS:(q * 2 + m + 1) * SLOTS, b * wide:(b + 1) * wide] = jnp.where(
                        group_of == m * 2 + q, value, 0.0
                    ).astype(jnp.bfloat16)
        return carry

    lax.fori_loop(0, pairs, weight_step, 0)

    for step in range(1, planes):
        plane_copy(step, 2).wait_recv()
        near_copy(step, 2).start()
    for step in range(1, planes):
        near_copy(step, 2).wait_recv()
    count = channels // planes
    lanes = lax.broadcasted_iota(jnp.int32, (count, 8 * wide), 1)
    part_of = lanes // rank % 2
    wave_of = lanes // (2 * rank) % 2
    for part in range(rank // 8):
        for z in range(planes):
            columns = slice(part * 8 * rank, (part + 1) * 8 * rank)
            real = dense(outer[z, :count, columns], spread[...])
            imaginary = dense(outer[z, count:, columns], spread[...])
            for r in range(2):
                value = jnp.where(part_of == 0, imaginary, real) if r else jnp.where(part_of == 0, real, -imaginary)
                for m in range(2):
                    start = (m * 2 + r) * channels + z * count
                    closing[start:start + count, part * 8 * wide:(part + 1) * 8 * wide] = (
                        jnp.where(wave_of == m, value, 0.0).astype(jnp.bfloat16)
                    )

    for n in range(2):
        load_table(n).wait()
    for c in range(PARTS):
        for t in range(1, holders):
            modes_copy(t, c).wait_recv()
    for d in range(holders):
        for p in range(2):
            for v in range(variables):
                stacked[v * waves:(v + 1) * waves, (d * 2 + p) * row_count:(d * 2 + p + 1) * row_count] = (
                    arrived[d, p * waves:(p + 1) * waves, v * row_count:(v + 1) * row_count]
                )
    by = dense(height[...], stacked[...], ((1,), (1,))).astype(jnp.bfloat16)
    first_wave = (me == 0).astype(jnp.float32)
    placed[...] = (
        dense(by[:kx_count], place[0]) + dense(by[kx_count:], place[1]) + bias_row[...] * first_wave
    ).astype(jnp.bfloat16)

    def pair_step(j, carry):
        column = pl.ds(pl.multiple_of(j * wide, wide), wide)
        own = placed[:, column]
        for part in range(rank // 8):
            got = dense(own, weights[j, :, part * 8 * wide:(part + 1) * 8 * wide])
            for k in range(packs):
                rows[k, part * 64:(part + 1) * 64, column] = jnp.concatenate(
                    [got[k * EIGHT:(k + 1) * EIGHT, b * wide:(b + 1) * wide] for b in range(8)], axis=0
                ).astype(jnp.bfloat16)
        return carry

    lax.fori_loop(0, pairs, pair_step, 0)

    def first_step(k, carry):
        here = pl.ds(pl.multiple_of(k * 2 * EIGHT, 2 * EIGHT), 2 * EIGHT)
        for part in range(pairs // 2):
            one, two = [
                dense(blocks[2 * k + i], rows[2 * k + i, :, part * 2 * wide:(part + 1) * 2 * wide]) for i in range(2)
            ]
            for j in range(2):
                side = slice(j * wide, (j + 1) * wide)
                for a in range(rank):
                    level = slice(a * EIGHT, (a + 1) * EIGHT)
                    carried[part * 2 + j, here, a * wide:(a + 1) * wide] = jnp.concatenate(
                        [one[level, side], two[level, side]], axis=0
                    ).astype(jnp.bfloat16)
        return carry

    lax.fori_loop(0, packs // 2, first_step, 0)

    for part in range(pairs // 2):
        both = carried[part * 2:part * 2 + 2].reshape(2 * kx_count, rank * wide)
        got = dense(closing[...], both, ((1,), (1,)))
        for m in range(2):
            for r in range(2):
                for j in range(2):
                    turned[:, (part * 2 + j) * 2 + m, r * kx_count:(r + 1) * kx_count] = got[
                        (m * 2 + r) * channels:(m * 2 + r + 1) * channels, j * kx_count:(j + 1) * kx_count
                    ]
    mixed[...] = turned[...].astype(jnp.bfloat16)

    for n in range(3):
        for step in range(1, planes):
            plane_copy(step, n).wait_send()
            near_copy(step, n).wait_send()
    for c in range(PARTS):
        for t in range(1, holders):
            modes_copy(t, c).wait_send()


def mix(fields, forward, first, inner, outer, height, place, bias_row, second, first_spread, spread, planes):
    variables, row_count, points = fields.shape
    holders = forward.shape[0] // (2 * WAVES)
    waves = WAVES
    kx2, depth = height.shape
    rank = inner.shape[0]
    channels = outer.shape[0] // 2 * planes
    wide = 4 * rank
    slots = inner.shape[1] // rank
    packs = kx2 // 2 // EIGHT
    joined = (rank * EIGHT, first.shape[0] // EIGHT * rank)
    operands = (fields, forward, first, inner, outer, height, place, bias_row, second, first_spread, spread)
    return pl.pallas_call(
        mix_kernel,
        in_specs=[pl.BlockSpec(memory_space=pl.ANY if n in (0, 5, 6) else pltpu.VMEM) for n in range(len(operands))],
        out_specs=pl.BlockSpec(memory_space=pltpu.VMEM),
        out_shape=jax.ShapeDtypeStruct((channels, waves, kx2), jnp.bfloat16),
        scratch_shapes=[
            pltpu.VMEM(first.shape, jnp.float32),
            pltpu.VMEM((first.shape[0] // EIGHT, rank * EIGHT, rank), jnp.float32),
            pltpu.VMEM(joined, jnp.bfloat16),
            pltpu.VMEM(fields.shape, jnp.bfloat16),
            pltpu.VMEM(height.shape, jnp.bfloat16),
            pltpu.VMEM(place.shape, jnp.bfloat16),
            pltpu.VMEM((holders, 2 * waves, variables * row_count), jnp.bfloat16),
            pltpu.VMEM((holders, 2 * waves, variables * row_count), jnp.bfloat16),
            pltpu.VMEM((planes,) + joined, jnp.bfloat16),
            pltpu.VMEM((planes,) + inner.shape, jnp.bfloat16),
            pltpu.VMEM((planes,) + outer.shape, jnp.bfloat16),
            pltpu.VMEM((place.shape[1], depth), jnp.bfloat16),
            pltpu.VMEM((kx2 // 2, waves // 2 * wide), jnp.bfloat16),
            pltpu.VMEM((rank, slots * wide), jnp.bfloat16),
            pltpu.VMEM((2, rank, SLOTS, wide), jnp.float32),
            pltpu.VMEM((waves // 2, 4 * SLOTS, rank * wide), jnp.bfloat16),
            pltpu.VMEM((packs, rank * EIGHT, waves // 2 * wide), jnp.bfloat16),
            pltpu.VMEM((packs, rank * EIGHT, rank * EIGHT), jnp.bfloat16),
            pltpu.VMEM((4 * channels, rank * wide), jnp.bfloat16),
            pltpu.VMEM((waves // 2, kx2 // 2, rank * wide), jnp.bfloat16),
            pltpu.VMEM((channels, waves, kx2), jnp.float32),
            pltpu.SemaphoreType.DMA((PARTS + 2,)),
            pltpu.SemaphoreType.DMA((planes - 1, 3)),
            pltpu.SemaphoreType.DMA((planes - 1, 3)),
            pltpu.SemaphoreType.DMA((planes - 1, 3)),
            pltpu.SemaphoreType.DMA((planes - 1, 3)),
            pltpu.SemaphoreType.DMA((holders - 1, PARTS)),
            pltpu.SemaphoreType.DMA((holders - 1, PARTS)),
        ],
        compiler_params=pltpu.CompilerParams(
            collective_id=1, has_side_effects=True, vmem_limit_bytes=60 * 2**20
        ),
        name="mix",
    )(*operands)


def twice_gelu(h):
    return h + h * lax.erf(h * (1.0 / math.sqrt(2.0)))


def finish_kernel(
    mixed, back_far, fields_far, width, lift_weight, skip_weight, lift_bias, skip_bias, out_weight, out_bias, tall, wide,
    result_far, gathered, back, fields, source, cols, total, skip, closing, last_bias, active, load, leave, send, recv,
):
    channels, waves, kx2 = mixed.shape
    variables, row_count, points = fields.shape
    inner = variables * EIGHT
    steps = row_count // EIGHT // 2
    mode, batch, core = lax.axis_index("mode"), lax.axis_index("batch"), lax.axis_index("cores")
    near = (mode + 1 - 2 * (mode % 2), batch, core)
    by_x = ((mode + 2) % 4, batch, core)
    by_y = (mode, batch, 1 - core)

    def owner(device):
        return device[0] * 2 + device[2]

    me = owner((mode, batch, core))
    at_x, at_y = owner(by_x), owner(by_y)
    across = owner((by_x[0], batch, by_y[2]))

    barrier = pltpu.get_barrier_semaphore()
    for device in (near, by_x, by_y):
        pl.semaphore_signal(barrier, inc=1, device_id=device, device_id_type=MESH)
    pl.semaphore_wait(barrier, 3)

    def piece(holder, first, count):
        return gathered.at[pl.ds(first, count), pl.ds(pl.multiple_of(holder * waves, waves), waves), :]

    def copy(g, kind):
        low, share = STARTS[g], CHUNKS[g]
        half = share // 2
        own = mixed.at[pl.ds(low, share)]
        home = piece(me, low, share)
        x_all, y_all = piece(at_x, low, share), piece(at_y, low, share)
        x_low, y_high = piece(at_x, low, half), piece(at_y, low + half, half)
        d_low, d_high = piece(across, low, half), piece(across, low + half, half)
        from_, to, device = (
            (own, home, near), (own, home, by_x), (own, home, by_y),
            (x_all, x_all, near), (y_all, y_all, near),
            (x_low, x_low, by_y), (y_high, y_high, by_x),
            (d_low, d_low, near), (d_high, d_high, near),
        )[kind]
        return pltpu.make_async_remote_copy(
            src_ref=from_, dst_ref=to, send_sem=send.at[g, kind], recv_sem=recv.at[g, kind],
            device_id=device, device_id_type=MESH,
        )

    def begin(g, kinds):
        for kind in kinds:
            copy(g, kind).start()

    def came(g, kinds):
        for kind in kinds:
            copy(g, kind).wait_recv()

    def relay(g):
        came(g, (1, 2))
        begin(g, (5, 6, 3, 4))
        if g + 1 < len(CHUNKS):
            begin(g + 1, (1, 2, 0))

    def relay_last(g):
        came(g, (5, 6))
        begin(g, (7, 8))

    begin(0, (1, 2, 0))
    loads = [
        pltpu.make_async_copy(fields_far, fields, load.at[0]),
        pltpu.make_async_copy(back_far.at[me], back, load.at[1]),
    ]
    for one in loads:
        one.start()
    gathered[:, pl.ds(pl.multiple_of(me * waves, waves), waves), :] = mixed[...]

    depth = skip.shape[1]
    line = lax.broadcasted_iota(jnp.int32, (depth - inner, points), 0)
    ones = jnp.where(line < 2, 1.0, 0.0).astype(jnp.bfloat16)
    for one in loads:
        one.wait()
    for x in range(steps):
        rows = fields[:, x * 2 * EIGHT:(x + 1) * 2 * EIGHT, :]
        for h in range(2):
            source[x * 2 + h, :inner, :] = rows[:, h * EIGHT:(h + 1) * EIGHT, :].reshape(inner, points)
            source[x * 2 + h, inner:, :] = ones
    relay(0)

    direct = dense(lift_weight[...], skip_weight[...]).astype(jnp.bfloat16)
    row_bias = lax.dot_general(
        jnp.broadcast_to(lift_bias[...], (8, channels)), skip_weight[...].astype(jnp.float32),
        (((1,), (0,)), ((), ())), preferred_element_type=jnp.float32, precision=lax.Precision.HIGHEST,
    )[:1] + skip_bias[...]
    size = 256
    down = lax.broadcasted_iota(jnp.int32, (size, depth), 0) % EIGHT
    along = lax.broadcasted_iota(jnp.int32, (size, depth), 1)
    for part in range(channels * EIGHT // size):
        here = slice(part * size, (part + 1) * size)
        picked = dense(tall[here, :], direct, ((1,), (1,))).astype(jnp.bfloat16)
        spread = dense(picked, wide[:variables, :depth])
        column = jnp.sum(tall[here, :].astype(jnp.float32) * row_bias, axis=1, keepdims=True)
        high = column.astype(jnp.bfloat16).astype(jnp.float32)
        rest = jnp.where(along == inner, high, jnp.where(along == inner + 1, column - high, 0.0))
        skip[here, :] = jnp.where(
            along < inner, jnp.where(down == along % EIGHT, spread, 0.0), rest
        ).astype(jnp.bfloat16)
    chosen = dense(tall[:inner, :variables], out_weight[...]).astype(jnp.bfloat16)
    down = lax.broadcasted_iota(jnp.int32, (inner, channels * EIGHT), 0) % EIGHT
    along = lax.broadcasted_iota(jnp.int32, (inner, channels * EIGHT), 1) % EIGHT
    closing[...] = jnp.where(down == along, 0.5 * dense(chosen, wide[...]), 0.0).astype(jnp.bfloat16)
    column = jnp.sum(tall[:inner, :variables].astype(jnp.float32) * out_bias[...], axis=1, keepdims=True)
    last_bias[...] = jnp.broadcast_to(column, last_bias.shape)
    relay_last(0)

    def turn(g):
        def step(c, carry):
            both = gathered[pl.ds(STARTS[g] + TURN * c, TURN)].reshape(TURN * waves * 8, kx2)
            got = dense(back[...], both, ((1,), (1,)))
            size = got.shape[1] // TURN
            for k in range(TURN // 2):
                place = pl.ds(pl.multiple_of(c * TURN * EIGHT + k * 2 * EIGHT, 2 * EIGHT), 2 * EIGHT)
                for p in range(2):
                    for x in range(row_count // EIGHT):
                        rows = got[p * row_count + x * EIGHT:p * row_count + (x + 1) * EIGHT, :]
                        cols[x, place, p * size:(p + 1) * size] = jnp.concatenate(
                            [rows[:, 2 * k * size:(2 * k + 1) * size], rows[:, (2 * k + 1) * size:(2 * k + 2) * size]],
                            axis=0,
                        ).astype(jnp.bfloat16)
            return carry

        lax.fori_loop(0, CHUNKS[g] // TURN, step, 0)

    def leave_rows(i):
        place = pl.ds(pl.multiple_of(i * 2 * EIGHT, 2 * EIGHT), 2 * EIGHT)
        return pltpu.make_async_copy(fields.at[:, place, :], result_far.at[:, place, :], leave.at[i])

    def finish_rows(g, low, high):
        start, size = STARTS[g] * EIGHT, CHUNKS[g] * EIGHT

        def step(i, carry):
            for lane in range(points // LANES):
                lanes = slice(lane * LANES, (lane + 1) * LANES)
                done = []
                for h in range(2):
                    x = 2 * i + h
                    for part in range(0, size, ROWS):
                        height = (
                            dense(cols[x, part:part + ROWS, :], width[:, lanes])
                            + dense(skip[start + part:start + part + ROWS, :], source[x, :, lanes])
                        )
                        active[lane * 2 + h, part:part + ROWS, :] = twice_gelu(height).astype(jnp.bfloat16)
                for h in range(2):
                    x = 2 * i + h
                    got = dense(closing[:, start:start + size], active[lane * 2 + h, :size, :])
                    if g == 0:
                        got = got + jnp.concatenate([last_bias[...]] * (LANES // 128), axis=1)
                    else:
                        got = got + total[x, :, lanes]
                    if g + 1 < len(CHUNKS):
                        total[x, :, lanes] = got
                    else:
                        done.append(got.reshape(variables, EIGHT, LANES))
                if done:
                    place = pl.ds(pl.multiple_of(i * 2 * EIGHT, 2 * EIGHT), 2 * EIGHT)
                    fields[:, place, lanes] = jnp.concatenate(done, axis=1).astype(jnp.bfloat16)
            if g + 1 == len(CHUNKS):
                leave_rows(i).start()
            return carry

        lax.fori_loop(low, high, step, 0)

    for g in range(len(CHUNKS)):
        came(g, (0, 3, 4, 7, 8))
        turn(g)
        if g + 1 < len(CHUNKS):
            finish_rows(g, 0, steps // 4)
            relay(g + 1)
            finish_rows(g, steps // 4, 3 * steps // 4)
            relay_last(g + 1)
            finish_rows(g, 3 * steps // 4, steps)
        else:
            finish_rows(g, 0, steps)
    for g in range(len(CHUNKS)):
        for kind in range(9):
            copy(g, kind).wait_send()

    def leave_step(i, carry):
        leave_rows(i).wait()
        return carry

    lax.fori_loop(0, steps, leave_step, 0)


def finish(mixed, back, fields, width, lift_weight, skip_weight, lift_bias, skip_bias, out_weight, out_bias):
    channels, waves, kx2 = mixed.shape
    variables, row_count, points = fields.shape
    tall = jnp.asarray(np.repeat(np.eye(channels), EIGHT, axis=0).astype(ml_dtypes.bfloat16))
    wide = jnp.asarray(np.repeat(np.eye(channels), EIGHT, axis=1).astype(ml_dtypes.bfloat16))
    operands = (
        mixed, back, fields, width, lift_weight, skip_weight, lift_bias[None], skip_bias[None], out_weight,
        out_bias[None], tall, wide,
    )
    blocks = row_count // EIGHT
    inner = variables * EIGHT
    depth = inner + 2 * EIGHT
    return pl.pallas_call(
        finish_kernel,
        in_specs=[pl.BlockSpec(memory_space=pl.ANY if n in (1, 2) else pltpu.VMEM) for n in range(len(operands))],
        out_specs=pl.BlockSpec(memory_space=pl.ANY),
        out_shape=jax.ShapeDtypeStruct(fields.shape, jnp.bfloat16),
        scratch_shapes=[
            pltpu.VMEM((channels, 8 * waves, kx2), jnp.bfloat16),
            pltpu.VMEM(back.shape[1:], jnp.bfloat16),
            pltpu.VMEM(fields.shape, jnp.bfloat16),
            pltpu.VMEM((blocks, depth, points), jnp.bfloat16),
            pltpu.VMEM((blocks, max(CHUNKS) * EIGHT, width.shape[0]), jnp.bfloat16),
            pltpu.VMEM((blocks, inner, points), jnp.float32),
            pltpu.VMEM((channels * EIGHT, depth), jnp.bfloat16),
            pltpu.VMEM((inner, channels * EIGHT), jnp.bfloat16),
            pltpu.VMEM((inner, 128), jnp.float32),
            pltpu.VMEM((points // LANES * 2, max(CHUNKS) * EIGHT, LANES), jnp.bfloat16),
            pltpu.SemaphoreType.DMA((2,)),
            pltpu.SemaphoreType.DMA((blocks // 2,)),
            pltpu.SemaphoreType.DMA((len(CHUNKS), 9)),
            pltpu.SemaphoreType.DMA((len(CHUNKS), 9)),
        ],
        compiler_params=pltpu.CompilerParams(
            collective_id=0, has_side_effects=True, vmem_limit_bytes=60 * 2**20
        ),
        name="finish",
    )(*operands)


def fast_shards(
    fields, lift_weight, lift_bias, first_core, second_core, input_core, output_core,
    skip_weight, skip_bias, out_weight, out_bias,
):
    holders = lax.axis_size("mode") * lax.axis_size("cores")
    waves, rank, _ = second_core.shape
    _, variables, row_count, points = fields.shape
    channels = lift_weight.shape[1]
    fields = fields[0]

    cosines, sines = host_pair(np.arange(MY), np.arange(points), points)
    root = math.sqrt(points)
    forward = np.stack([cosines, -sines], 0).reshape(2, holders, waves, points).transpose(1, 0, 2, 3)
    forward = jnp.asarray((forward.reshape(2 * MY, points) / root).astype(np.float32).astype(ml_dtypes.bfloat16))
    weight = np.where(np.arange(MY) == 0, 1.0, 2.0).astype(np.float32)[:, None]
    width = np.concatenate([cosines * weight, -sines * weight], 0) / root
    width = jnp.asarray(width.astype(ml_dtypes.bfloat16))
    order = cyclic_rows(row_count, holders)
    root = math.sqrt(NX)
    cosines, sines = host_pair(np.arange(MX) - MX // 2, order, NX)
    cosines, sines = [t.reshape(MX, holders, row_count) / root for t in (cosines, sines)]
    upper = np.stack([cosines, sines], 2)
    lower = np.stack([-sines, cosines], 2)
    height = np.stack([upper, lower], 0).reshape(2 * MX, -1).astype(ml_dtypes.bfloat16)
    real_part = np.asarray(height, np.float32).reshape(2 * MX, holders, 2, row_count)[:, :, 0]
    row_sum = real_part.sum((1, 2), dtype=np.float64).astype(np.float32)
    cos_t, sin_t = [t.transpose(1, 2, 0) for t in (cosines, sines)]
    up = np.concatenate([cos_t, -sin_t], 2)
    low = np.concatenate([sin_t, cos_t], 2)
    back_rows = jnp.asarray(np.concatenate([up, low], 1).astype(ml_dtypes.bfloat16))
    pairs = waves // 2
    place = np.zeros((2, variables, waves, pairs, 2, 2, SLOTS), np.float32)
    for q in range(2):
        for v in range(variables):
            for m in range(waves):
                place[q, v, m, m // 2, q, m % 2, v] = 1.0
    place = jnp.asarray(place.reshape(2, variables * waves, -1).astype(ml_dtypes.bfloat16))
    bias_row = np.zeros((MX, pairs, 2, 2, SLOTS), np.float32)
    bias_row[:, 0, :, 0, variables] = row_sum.reshape(2, MX).T
    bias_row = jnp.asarray(bias_row.reshape(MX, -1))
    packs = first_core.shape[0] // EIGHT
    first_spread = np.einsum("pk,bc->kpbc", np.eye(packs), np.repeat(np.eye(rank), EIGHT, axis=1))
    first_spread = jnp.asarray(first_spread.reshape(packs, packs * rank, rank * EIGHT).astype(ml_dtypes.bfloat16))
    spread = np.eye(8)[:, None, :, None, None] * np.eye(rank)[None, :, None, None, :] * np.ones((1, 1, 1, 4, 1))
    spread = jnp.asarray(spread.reshape(8 * rank, 32 * rank).astype(ml_dtypes.bfloat16))

    used = (variables + 4) // 4 * 4
    lift = jnp.concatenate(
        [lift_weight, (math.sqrt(points) * lift_bias).astype(jnp.bfloat16)[None],
         jnp.zeros((used - variables - 1, channels), jnp.bfloat16)], 0
    )
    count = input_core.shape[0]
    lift = lax.dynamic_slice_in_dim(lift, lax.axis_index("batch") * count, count, 1)
    inner = jnp.einsum("vc,cde->dve", lift, input_core, preferred_element_type=jnp.float32)
    inner = inner.astype(jnp.bfloat16).reshape(rank, used * rank)
    outer = output_core.transpose(1, 0, 3, 2).reshape(2 * count, rank * rank)
    mixed = mix(
        fields, forward, first_core, inner, outer, jnp.asarray(height), place, bias_row,
        second_core.reshape(waves * rank, rank), first_spread, spread, lax.axis_size("batch"),
    )
    return finish(
        mixed, back_rows, fields, width, lift_weight, skip_weight, lift_bias, skip_bias, out_weight.T, out_bias
    )[None]


def solution(mesh):
    placed = (
        P("batch", None, ("mode", "cores"), None),
        P(),
        P(),
        P("batch", None, None),
        P(("mode", "cores"), None, None),
        P("batch", None, None),
        P("batch", None, None, None),
        P(),
        P(),
        P(),
        P(),
    )
    fits = (
        mesh.shape["mode"] == 4 and mesh.shape["cores"] == 2 and MY // 8 == WAVES
        and mesh.shape["batch"] == 4 and MX // 4 % EIGHT == 0 and NX // 8 == 128
    )
    return jax.shard_map(
        fast_shards if fits else shards,
        mesh=mesh,
        in_specs=placed,
        out_specs=P("batch", None, ("mode", "cores"), None),
        check_vma=False,
    )
```

```python
import functools
import math

import jax
import jax.numpy as jnp
import ml_dtypes
import numpy as np
from jax import lax
from jax.experimental import pallas as pl
from jax.experimental.pallas import tpu as pltpu
from jax.sharding import PartitionSpec as P

NX = 1024
NY = 1024
MX = 128
MY = 128


TWO_PI = 2.0 * math.pi


def wave_pair(waves, points, length):
    phase_step = waves[:, None] * points[None, :] % length
    angles = phase_step.astype(jnp.float32) * (TWO_PI / length)
    return (jnp.cos(angles), jnp.sin(angles))


def width_forward(length, wave_count):
    points = jnp.arange(length, dtype=jnp.int32)
    waves = jnp.arange(wave_count, dtype=jnp.int32)
    cosines, sine_part = wave_pair(points, waves, length)
    stacked = jnp.stack([cosines, -sine_part], axis=1) / math.sqrt(length)
    return stacked.astype(jnp.bfloat16)


def height_forward(row_index, wave_count, length):
    waves = jnp.arange(wave_count, dtype=jnp.int32) - wave_count // 2
    cosines, sine_part = wave_pair(waves, row_index, length)
    upper = jnp.stack([cosines, sine_part], axis=1)
    lower = jnp.stack([-sine_part, cosines], axis=1)
    return (jnp.stack([upper, lower], axis=0) / math.sqrt(length)).astype(jnp.bfloat16)


def height_inverse(row_index, wave_count, length):
    waves = jnp.arange(wave_count, dtype=jnp.int32) - wave_count // 2
    cosines, sine_part = wave_pair(row_index, waves, length)
    upper = jnp.stack([cosines, -sine_part], axis=1)
    lower = jnp.stack([sine_part, cosines], axis=1)
    return (jnp.stack([upper, lower], axis=0) / math.sqrt(length)).astype(jnp.bfloat16)


def width_inverse(waves, length):
    points = jnp.arange(length, dtype=jnp.int32)
    cosines, sine_part = wave_pair(waves, points, length)
    weight = jnp.where(waves == 0, 1.0, 2.0).astype(jnp.float32)[:, None]
    stacked = jnp.stack([cosines * weight, -sine_part * weight], axis=0) / math.sqrt(length)
    return stacked.astype(jnp.bfloat16)


def bias_modes(lift_bias, wave_index, length):
    real_row = (
        jnp.where(wave_index == 0, 1.0, 0.0).astype(jnp.float32)[:, None]
        * (math.sqrt(length) * lift_bias)[None, :]
    )
    return jnp.stack([real_row, jnp.zeros_like(real_row)], axis=0)


def lift_modes(modes, lift_weight, lift_bias, wave_index):
    lifted_modes = jnp.einsum(
        "fabpmv,vc->fabpmc", modes, lift_weight, preferred_element_type=jnp.float32
    )
    return (lifted_modes + bias_modes(lift_bias, wave_index, NY)).astype(jnp.bfloat16)


def grid_rows(stored, row_count, holder_count):
    return stored % row_count * holder_count + stored // row_count


def shards(
    fields,
    lift_weight,
    lift_bias,
    first_core,
    second_core,
    input_core,
    output_core,
    skip_weight,
    skip_bias,
    out_weight,
    out_bias,
):
    mode_count = lax.axis_size("mode")
    core_count = lax.axis_size("cores")
    row_count = fields.shape[2]
    block_size = second_core.shape[0]
    block_start = (lax.axis_index("mode") * core_count + lax.axis_index("cores")) * block_size
    local_waves = block_start + jnp.arange(block_size, dtype=jnp.int32)
    lifted = (
        jnp.einsum("fvxy,vc->fxyc", fields, lift_weight, preferred_element_type=jnp.float32)
        + lift_bias
    ).astype(jnp.bfloat16)
    field_modes = jnp.einsum(
        "fvxy,ypk->fxpkv", fields, width_forward(NY, MY), preferred_element_type=jnp.float32
    ).astype(jnp.bfloat16)
    field_modes = field_modes[:, None]
    gathered = (
        lax.all_gather(first_core, "batch", axis=0, tiled=True),
        lax.all_gather(input_core, "batch", axis=0, tiled=True),
        lax.all_gather(output_core, "batch", axis=0, tiled=True),
    )
    first_whole, input_whole, output_whole = gathered
    mode_factor = jnp.einsum(
        "kab,mbd->kmad", first_whole, second_core, preferred_element_type=jnp.float32
    ).astype(jnp.bfloat16)
    arrived = lax.all_to_all(
        field_modes, ("mode", "cores"), split_axis=4, concat_axis=2, tiled=True
    )
    rows_held = jnp.arange(NX, dtype=jnp.int32)[None, :]
    by_mode = lift_modes(arrived, lift_weight, lift_bias, local_waves)
    lead_rows = rows_held.shape[0]
    side_rows = rows_held.shape[1]
    flat_rows = grid_rows(rows_held.reshape(-1), row_count, mode_count * core_count)
    height_table = height_forward(flat_rows, MX, NX).reshape(2, MX, 2, lead_rows, side_rows)
    spectrum = jnp.einsum(
        "qkpab,fabpmc->fqkmc", height_table, by_mode, preferred_element_type=jnp.float32
    ).astype(jnp.bfloat16)
    projected = jnp.einsum(
        "fqkmc,cbe->fqkmbe", spectrum, input_whole, preferred_element_type=jnp.float32
    ).astype(jnp.bfloat16)
    carried = jnp.einsum(
        "kmab,fqkmbe->fqkmae", mode_factor, projected, preferred_element_type=jnp.float32
    ).astype(jnp.bfloat16)
    traced = jnp.einsum(
        "fqkmae,osea->fqkmso", carried, output_whole, preferred_element_type=jnp.float32
    )
    real_part = traced[:, 0, :, :, 0, :] - traced[:, 1, :, :, 1, :]
    imaginary = traced[:, 0, :, :, 1, :] + traced[:, 1, :, :, 0, :]
    mixed_modes = jnp.stack([real_part, imaginary], axis=1).astype(jnp.bfloat16)
    height_back = height_inverse(flat_rows, MX, NX).reshape(2, lead_rows, side_rows, 2, MX)
    col_modes = jnp.einsum(
        "pabqk,fqkmc->fabpmc", height_back, mixed_modes, preferred_element_type=jnp.float32
    ).astype(jnp.bfloat16)
    returned = lax.all_to_all(col_modes, ("mode", "cores"), split_axis=2, concat_axis=4, tiled=True)
    waves_held = jnp.arange(MY, dtype=jnp.int32)
    width_back = width_inverse(waves_held, NY)
    spatial = jnp.einsum(
        "fxpmc,pmy->fxyc", returned[:, 0], width_back, preferred_element_type=jnp.float32
    )
    skip_term = jnp.einsum("fxyc,cd->fxyd", lifted, skip_weight, preferred_element_type=jnp.float32)
    active = jax.nn.gelu(spatial + skip_term + skip_bias, approximate=False).astype(jnp.bfloat16)
    result = (
        jnp.einsum("fxyc,cv->fvxy", active, out_weight, preferred_element_type=jnp.float32)
        + out_bias[:, None, None]
    )
    return result.astype(jnp.bfloat16)


def cyclic_rows(row_count, holders):
    return (np.arange(row_count)[None, :] * holders + np.arange(holders)[:, None]).reshape(-1)


def host_pair(waves, points, length):
    steps = np.asarray(waves)[:, None] * np.asarray(points)[None, :] % length
    angles = steps.astype(np.float32) * np.float32(TWO_PI / length)
    return np.cos(angles), np.sin(angles)


def dense(a, b, contract=((1,), (0,))):
    return lax.dot_general(a, b, (contract, ((), ())), preferred_element_type=jnp.float32)


MESH = pl.DeviceIdType.MESH
WAVES = 16
SLOTS = 32
EIGHT = 8
CHUNKS = (32, 48, 48)
STARTS = (0, 32, 80)
LANES = 512
ROWS = 128
PARTS = 2
TURN = 16


def whole(a):
    return pl.BlockSpec(a.shape, lambda *_: (0,) * a.ndim)


def mix_kernel(
    fields_far, forward, first_core, inner_own, outer_own, height_far, place_far, bias_row, second, first_spread, spread,
    mixed, first_wide, first_turned, first_own, fields, height, place, modes, arrived, first, inner, outer, stacked, placed, inner_wide, turned_inner, weights, rows,
    blocks, closing, carried, turned, load, send_plane, recv_plane, send_near, recv_near, send_modes, recv_modes,
):
    variables, row_count, points = fields.shape
    holders, lead, flat = arrived.shape
    waves = lead // 2
    kx_count = height.shape[0] // 2
    planes = first.shape[0]
    rank = inner.shape[1]
    channels = mixed.shape[0]
    pairs = waves // 2
    wide = 4 * rank
    slots = inner.shape[2] // rank
    packs = kx_count // EIGHT
    share = variables // PARTS
    mode, batch, core = lax.axis_index("mode"), lax.axis_index("batch"), lax.axis_index("cores")
    me = mode * 2 + core
    near = (mode + 1 - 2 * (mode % 2), batch, core)

    def load_part(c):
        here = pl.ds(c * share, share)
        return pltpu.make_async_copy(fields_far.at[here], fields.at[here], load.at[c])

    def load_table(n):
        return pltpu.make_async_copy((height_far, place_far)[n], (height, place)[n], load.at[PARTS + n])

    for c in range(PARTS):
        load_part(c).start()
    for n in range(2):
        load_table(n).start()

    def flip(bit, change):
        return bit + change - 2 * bit * change

    def peer(t):
        chip, side, line = flip(mode // 2, t // 4), flip(mode % 2, t // 2 % 2), flip(core, t % 2)
        return (chip * 2 + side, batch, line), chip * 4 + side * 2 + line

    def plane(step):
        return (mode, (batch + step) % planes, core)

    barrier = pltpu.get_barrier_semaphore()
    greeted = [peer(t)[0] for t in range(1, holders)] + [plane(step) for step in range(1, planes)]
    for device in greeted:
        pl.semaphore_signal(barrier, inc=1, device_id=device, device_id_type=MESH)
    pl.semaphore_wait(barrier, len(greeted))

    shards_own = (first_own, inner_own, outer_own)
    shards_all = (first, inner, outer)

    def half(n):
        size = shards_own[n].shape[0] // 2
        return pl.ds(pl.multiple_of((mode % 2) * size, size), size)

    def plane_copy(step, n):
        return pltpu.make_async_remote_copy(
            src_ref=shards_own[n].at[half(n)], dst_ref=shards_all[n].at[batch, half(n)],
            send_sem=send_plane.at[step - 1, n], recv_sem=recv_plane.at[step - 1, n],
            device_id=plane(step), device_id_type=MESH,
        )

    def near_copy(step, n):
        held = shards_all[n].at[(batch + planes - step) % planes, half(n)]
        return pltpu.make_async_remote_copy(
            src_ref=held, dst_ref=held, send_sem=send_near.at[step - 1, n], recv_sem=recv_near.at[step - 1, n],
            device_id=near, device_id_type=MESH,
        )

    def modes_copy(t, c):
        device, index = peer(t)
        lanes = pl.ds(c * share * row_count, share * row_count)
        return pltpu.make_async_remote_copy(
            src_ref=modes.at[index, :, lanes], dst_ref=arrived.at[me, :, lanes],
            send_sem=send_modes.at[t - 1, c], recv_sem=recv_modes.at[t - 1, c],
            device_id=device, device_id_type=MESH,
        )

    first_wide[...] = first_core[...].astype(jnp.float32)
    along = lax.broadcasted_iota(jnp.int32, (rank, first_own.shape[1]), 1)
    down = lax.broadcasted_iota(jnp.int32, (rank, first_own.shape[1]), 0)
    joined = None
    for k in range(packs // planes):
        for a in range(rank):
            first_turned[k, a * EIGHT:(a + 1) * EIGHT, :] = first_wide[k * EIGHT:(k + 1) * EIGHT, a, :]
        here = jnp.where(along == down + k * rank, 1.0, 0.0).astype(jnp.bfloat16)
        got = dense(first_turned[k].astype(jnp.bfloat16), here)
        joined = got if joined is None else joined + got
    first_own[...] = joined.astype(jnp.bfloat16)

    for n in range(3):
        for step in range(1, planes):
            plane_copy(step, n).start()
    for n in range(3):
        shards_all[n][batch] = shards_own[n][...]

    for c in range(PARTS):
        load_part(c).wait()
        for v in range(c * share, (c + 1) * share, 2):
            both = fields[v:v + 2].reshape(2 * row_count, points)
            got = dense(forward[...], both, ((1,), (1,))).astype(jnp.bfloat16)
            modes[:, :, v * row_count:(v + 2) * row_count] = got.reshape(holders, lead, 2 * row_count)
        for t in range(holders - 1, 0, -1):
            modes_copy(t, c).start()
    arrived[me] = modes[me]

    for n in range(2):
        for step in range(1, planes):
            plane_copy(step, n).wait_recv()
            near_copy(step, n).start()
    for n in range(2):
        for step in range(1, planes):
            near_copy(step, n).wait_recv()

    total = inner[0].astype(jnp.float32)
    for z in range(1, planes):
        total = total + inner[z].astype(jnp.float32)
    total = total.astype(jnp.bfloat16)
    for part in range(slots // 4):
        inner_wide[:, part * 4 * wide:(part + 1) * 4 * wide] = dense(
            total[:, part * wide:(part + 1) * wide], spread[:wide, :4 * wide]
        ).astype(jnp.bfloat16)

    down = lax.broadcasted_iota(jnp.int32, (rank * EIGHT, rank * EIGHT), 0) % EIGHT
    along = lax.broadcasted_iota(jnp.int32, (rank * EIGHT, rank * EIGHT), 1) % EIGHT
    same = down == along
    for z in range(planes):
        for k in range(packs // planes):
            full = dense(first[z], first_spread[k])
            blocks[z * (packs // planes) + k] = jnp.where(same, full, 0.0).astype(jnp.bfloat16)

    turned_inner[...] = jnp.zeros_like(turned_inner)
    group_of = lax.broadcasted_iota(jnp.int32, (SLOTS, wide), 1) // rank

    def weight_step(j, carry):
        start = pl.multiple_of(j * 2 * rank, 2 * rank)
        joined = dense(second[pl.ds(start, 2 * rank), :], inner_wide[...])
        for m in range(2):
            for v in range(slots):
                turned_inner[m, :, v, :] = joined[m * rank:(m + 1) * rank, v * wide:(v + 1) * wide]
        for m in range(2):
            for b in range(rank):
                value = turned_inner[m, b]
                for q in range(2):
                    weights[j, (q * 2 + m) * SLOTS:(q * 2 + m + 1) * SLOTS, b * wide:(b + 1) * wide] = jnp.where(
                        group_of == m * 2 + q, value, 0.0
                    ).astype(jnp.bfloat16)
        return carry

    lax.fori_loop(0, pairs, weight_step, 0)

    for step in range(1, planes):
        plane_copy(step, 2).wait_recv()
        near_copy(step, 2).start()
    for step in range(1, planes):
        near_copy(step, 2).wait_recv()
    count = channels // planes
    lanes = lax.broadcasted_iota(jnp.int32, (count, 8 * wide), 1)
    part_of = lanes // rank % 2
    wave_of = lanes // (2 * rank) % 2
    for part in range(rank // 8):
        for z in range(planes):
            columns = slice(part * 8 * rank, (part + 1) * 8 * rank)
            real = dense(outer[z, :count, columns], spread[...])
            imaginary = dense(outer[z, count:, columns], spread[...])
            for r in range(2):
                value = jnp.where(part_of == 0, imaginary, real) if r else jnp.where(part_of == 0, real, -imaginary)
                for m in range(2):
                    start = (m * 2 + r) * channels + z * count
                    closing[start:start + count, part * 8 * wide:(part + 1) * 8 * wide] = (
                        jnp.where(wave_of == m, value, 0.0).astype(jnp.bfloat16)
                    )

    for n in range(2):
        load_table(n).wait()
    for c in range(PARTS):
        for t in range(1, holders):
            modes_copy(t, c).wait_recv()
    for d in range(holders):
        for p in range(2):
            for v in range(variables):
                stacked[v * waves:(v + 1) * waves, (d * 2 + p) * row_count:(d * 2 + p + 1) * row_count] = (
                    arrived[d, p * waves:(p + 1) * waves, v * row_count:(v + 1) * row_count]
                )
    by = dense(height[...], stacked[...], ((1,), (1,))).astype(jnp.bfloat16)
    first_wave = (me == 0).astype(jnp.float32)
    placed[...] = (
        dense(by[:kx_count], place[0]) + dense(by[kx_count:], place[1]) + bias_row[...] * first_wave
    ).astype(jnp.bfloat16)

    def pair_step(j, carry):
        column = pl.ds(pl.multiple_of(j * wide, wide), wide)
        own = placed[:, column]
        for part in range(rank // 8):
            got = dense(own, weights[j, :, part * 8 * wide:(part + 1) * 8 * wide])
            for k in range(packs):
                rows[k, part * 64:(part + 1) * 64, column] = jnp.concatenate(
                    [got[k * EIGHT:(k + 1) * EIGHT, b * wide:(b + 1) * wide] for b in range(8)], axis=0
                ).astype(jnp.bfloat16)
        return carry

    lax.fori_loop(0, pairs, pair_step, 0)

    def first_step(k, carry):
        here = pl.ds(pl.multiple_of(k * 2 * EIGHT, 2 * EIGHT), 2 * EIGHT)
        for part in range(pairs // 2):
            one, two = [
                dense(blocks[2 * k + i], rows[2 * k + i, :, part * 2 * wide:(part + 1) * 2 * wide]) for i in range(2)
            ]
            for j in range(2):
                side = slice(j * wide, (j + 1) * wide)
                for a in range(rank):
                    level = slice(a * EIGHT, (a + 1) * EIGHT)
                    carried[part * 2 + j, here, a * wide:(a + 1) * wide] = jnp.concatenate(
                        [one[level, side], two[level, side]], axis=0
                    ).astype(jnp.bfloat16)
        return carry

    lax.fori_loop(0, packs // 2, first_step, 0)

    for part in range(pairs // 2):
        both = carried[part * 2:part * 2 + 2].reshape(2 * kx_count, rank * wide)
        got = dense(closing[...], both, ((1,), (1,)))
        for m in range(2):
            for r in range(2):
                for j in range(2):
                    turned[:, (part * 2 + j) * 2 + m, r * kx_count:(r + 1) * kx_count] = got[
                        (m * 2 + r) * channels:(m * 2 + r + 1) * channels, j * kx_count:(j + 1) * kx_count
                    ]
    mixed[...] = turned[...].astype(jnp.bfloat16)

    for n in range(3):
        for step in range(1, planes):
            plane_copy(step, n).wait_send()
            near_copy(step, n).wait_send()
    for c in range(PARTS):
        for t in range(1, holders):
            modes_copy(t, c).wait_send()


def mix(fields, forward, first, inner, outer, height, place, bias_row, second, first_spread, spread, planes):
    variables, row_count, points = fields.shape
    holders = forward.shape[0] // (2 * WAVES)
    waves = WAVES
    kx2, depth = height.shape
    rank = inner.shape[0]
    channels = outer.shape[0] // 2 * planes
    wide = 4 * rank
    slots = inner.shape[1] // rank
    packs = kx2 // 2 // EIGHT
    joined = (rank * EIGHT, first.shape[0] // EIGHT * rank)
    operands = (fields, forward, first, inner, outer, height, place, bias_row, second, first_spread, spread)
    return pl.pallas_call(
        mix_kernel,
        in_specs=[pl.BlockSpec(memory_space=pl.ANY if n in (0, 5, 6) else pltpu.VMEM) for n in range(len(operands))],
        out_specs=pl.BlockSpec(memory_space=pltpu.VMEM),
        out_shape=jax.ShapeDtypeStruct((channels, waves, kx2), jnp.bfloat16),
        scratch_shapes=[
            pltpu.VMEM(first.shape, jnp.float32),
            pltpu.VMEM((first.shape[0] // EIGHT, rank * EIGHT, rank), jnp.float32),
            pltpu.VMEM(joined, jnp.bfloat16),
            pltpu.VMEM(fields.shape, jnp.bfloat16),
            pltpu.VMEM(height.shape, jnp.bfloat16),
            pltpu.VMEM(place.shape, jnp.bfloat16),
            pltpu.VMEM((holders, 2 * waves, variables * row_count), jnp.bfloat16),
            pltpu.VMEM((holders, 2 * waves, variables * row_count), jnp.bfloat16),
            pltpu.VMEM((planes,) + joined, jnp.bfloat16),
            pltpu.VMEM((planes,) + inner.shape, jnp.bfloat16),
            pltpu.VMEM((planes,) + outer.shape, jnp.bfloat16),
            pltpu.VMEM((place.shape[1], depth), jnp.bfloat16),
            pltpu.VMEM((kx2 // 2, waves // 2 * wide), jnp.bfloat16),
            pltpu.VMEM((rank, slots * wide), jnp.bfloat16),
            pltpu.VMEM((2, rank, SLOTS, wide), jnp.float32),
            pltpu.VMEM((waves // 2, 4 * SLOTS, rank * wide), jnp.bfloat16),
            pltpu.VMEM((packs, rank * EIGHT, waves // 2 * wide), jnp.bfloat16),
            pltpu.VMEM((packs, rank * EIGHT, rank * EIGHT), jnp.bfloat16),
            pltpu.VMEM((4 * channels, rank * wide), jnp.bfloat16),
            pltpu.VMEM((waves // 2, kx2 // 2, rank * wide), jnp.bfloat16),
            pltpu.VMEM((channels, waves, kx2), jnp.float32),
            pltpu.SemaphoreType.DMA((PARTS + 2,)),
            pltpu.SemaphoreType.DMA((planes - 1, 3)),
            pltpu.SemaphoreType.DMA((planes - 1, 3)),
            pltpu.SemaphoreType.DMA((planes - 1, 3)),
            pltpu.SemaphoreType.DMA((planes - 1, 3)),
            pltpu.SemaphoreType.DMA((holders - 1, PARTS)),
            pltpu.SemaphoreType.DMA((holders - 1, PARTS)),
        ],
        compiler_params=pltpu.CompilerParams(
            collective_id=1, has_side_effects=True, vmem_limit_bytes=60 * 2**20
        ),
        name="mix",
    )(*operands)


def twice_gelu(h):
    return h + h * lax.erf(h * (1.0 / math.sqrt(2.0)))


def finish_kernel(
    mixed, back_far, fields_far, width, lift_weight, skip_weight, lift_bias, skip_bias, out_weight, out_bias, tall, wide,
    result_far, gathered, back, fields, source, cols, total, skip, closing, last_bias, active, load, leave, send, recv,
):
    channels, waves, kx2 = mixed.shape
    variables, row_count, points = fields.shape
    inner = variables * EIGHT
    steps = row_count // EIGHT // 2
    mode, batch, core = lax.axis_index("mode"), lax.axis_index("batch"), lax.axis_index("cores")
    near = (mode + 1 - 2 * (mode % 2), batch, core)
    by_x = ((mode + 2) % 4, batch, core)
    by_y = (mode, batch, 1 - core)

    def owner(device):
        return device[0] * 2 + device[2]

    me = owner((mode, batch, core))
    at_x, at_y = owner(by_x), owner(by_y)
    across = owner((by_x[0], batch, by_y[2]))

    barrier = pltpu.get_barrier_semaphore()
    for device in (near, by_x, by_y):
        pl.semaphore_signal(barrier, inc=1, device_id=device, device_id_type=MESH)
    pl.semaphore_wait(barrier, 3)

    def piece(holder, first, count):
        return gathered.at[pl.ds(first, count), pl.ds(pl.multiple_of(holder * waves, waves), waves), :]

    def copy(g, kind):
        low, share = STARTS[g], CHUNKS[g]
        half = share // 2
        own = mixed.at[pl.ds(low, share)]
        home = piece(me, low, share)
        x_all, y_all = piece(at_x, low, share), piece(at_y, low, share)
        x_low, y_high = piece(at_x, low, half), piece(at_y, low + half, half)
        d_low, d_high = piece(across, low, half), piece(across, low + half, half)
        from_, to, device = (
            (own, home, near), (own, home, by_x), (own, home, by_y),
            (x_all, x_all, near), (y_all, y_all, near),
            (x_low, x_low, by_y), (y_high, y_high, by_x),
            (d_low, d_low, near), (d_high, d_high, near),
        )[kind]
        return pltpu.make_async_remote_copy(
            src_ref=from_, dst_ref=to, send_sem=send.at[g, kind], recv_sem=recv.at[g, kind],
            device_id=device, device_id_type=MESH,
        )

    def begin(g, kinds):
        for kind in kinds:
            copy(g, kind).start()

    def came(g, kinds):
        for kind in kinds:
            copy(g, kind).wait_recv()

    def relay(g):
        came(g, (1, 2))
        begin(g, (5, 6, 3, 4))
        if g + 1 < len(CHUNKS):
            begin(g + 1, (1, 2, 0))

    def relay_last(g):
        came(g, (5, 6))
        begin(g, (7, 8))

    begin(0, (1, 2, 0))
    loads = [
        pltpu.make_async_copy(fields_far, fields, load.at[0]),
        pltpu.make_async_copy(back_far.at[me], back, load.at[1]),
    ]
    for one in loads:
        one.start()
    gathered[:, pl.ds(pl.multiple_of(me * waves, waves), waves), :] = mixed[...]

    depth = skip.shape[1]
    line = lax.broadcasted_iota(jnp.int32, (depth - inner, points), 0)
    ones = jnp.where(line < 2, 1.0, 0.0).astype(jnp.bfloat16)
    for one in loads:
        one.wait()
    for x in range(steps):
        rows = fields[:, x * 2 * EIGHT:(x + 1) * 2 * EIGHT, :]
        for h in range(2):
            source[x * 2 + h, :inner, :] = rows[:, h * EIGHT:(h + 1) * EIGHT, :].reshape(inner, points)
            source[x * 2 + h, inner:, :] = ones
    relay(0)

    direct = dense(lift_weight[...], skip_weight[...]).astype(jnp.bfloat16)
    row_bias = lax.dot_general(
        jnp.broadcast_to(lift_bias[...], (8, channels)), skip_weight[...].astype(jnp.float32),
        (((1,), (0,)), ((), ())), preferred_element_type=jnp.float32, precision=lax.Precision.HIGHEST,
    )[:1] + skip_bias[...]
    size = 256
    down = lax.broadcasted_iota(jnp.int32, (size, depth), 0) % EIGHT
    along = lax.broadcasted_iota(jnp.int32, (size, depth), 1)
    for part in range(channels * EIGHT // size):
        here = slice(part * size, (part + 1) * size)
        picked = dense(tall[here, :], direct, ((1,), (1,))).astype(jnp.bfloat16)
        spread = dense(picked, wide[:variables, :depth])
        column = jnp.sum(tall[here, :].astype(jnp.float32) * row_bias, axis=1, keepdims=True)
        high = column.astype(jnp.bfloat16).astype(jnp.float32)
        rest = jnp.where(along == inner, high, jnp.where(along == inner + 1, column - high, 0.0))
        skip[here, :] = jnp.where(
            along < inner, jnp.where(down == along % EIGHT, spread, 0.0), rest
        ).astype(jnp.bfloat16)
    chosen = dense(tall[:inner, :variables], out_weight[...]).astype(jnp.bfloat16)
    down = lax.broadcasted_iota(jnp.int32, (inner, channels * EIGHT), 0) % EIGHT
    along = lax.broadcasted_iota(jnp.int32, (inner, channels * EIGHT), 1) % EIGHT
    closing[...] = jnp.where(down == along, 0.5 * dense(chosen, wide[...]), 0.0).astype(jnp.bfloat16)
    column = jnp.sum(tall[:inner, :variables].astype(jnp.float32) * out_bias[...], axis=1, keepdims=True)
    last_bias[...] = jnp.broadcast_to(column, last_bias.shape)
    relay_last(0)

    def turn(g):
        def step(c, carry):
            both = gathered[pl.ds(STARTS[g] + TURN * c, TURN)].reshape(TURN * waves * 8, kx2)
            got = dense(back[...], both, ((1,), (1,)))
            size = got.shape[1] // TURN
            for k in range(TURN // 2):
                place = pl.ds(pl.multiple_of(c * TURN * EIGHT + k * 2 * EIGHT, 2 * EIGHT), 2 * EIGHT)
                for p in range(2):
                    for x in range(row_count // EIGHT):
                        rows = got[p * row_count + x * EIGHT:p * row_count + (x + 1) * EIGHT, :]
                        cols[x, place, p * size:(p + 1) * size] = jnp.concatenate(
                            [rows[:, 2 * k * size:(2 * k + 1) * size], rows[:, (2 * k + 1) * size:(2 * k + 2) * size]],
                            axis=0,
                        ).astype(jnp.bfloat16)
            return carry

        lax.fori_loop(0, CHUNKS[g] // TURN, step, 0)

    def leave_rows(i):
        place = pl.ds(pl.multiple_of(i * 2 * EIGHT, 2 * EIGHT), 2 * EIGHT)
        return pltpu.make_async_copy(fields.at[:, place, :], result_far.at[:, place, :], leave.at[i])

    def finish_rows(g, low, high):
        start, size = STARTS[g] * EIGHT, CHUNKS[g] * EIGHT

        def step(i, carry):
            for lane in range(points // LANES):
                lanes = slice(lane * LANES, (lane + 1) * LANES)
                done = []
                for h in range(2):
                    x = 2 * i + h
                    for part in range(0, size, ROWS):
                        height = (
                            dense(cols[x, part:part + ROWS, :], width[:, lanes])
                            + dense(skip[start + part:start + part + ROWS, :], source[x, :, lanes])
                        )
                        active[lane * 2 + h, part:part + ROWS, :] = twice_gelu(height).astype(jnp.bfloat16)
                for h in range(2):
                    x = 2 * i + h
                    got = dense(closing[:, start:start + size], active[lane * 2 + h, :size, :])
                    if g == 0:
                        got = got + jnp.concatenate([last_bias[...]] * (LANES // 128), axis=1)
                    else:
                        got = got + total[x, :, lanes]
                    if g + 1 < len(CHUNKS):
                        total[x, :, lanes] = got
                    else:
                        done.append(got.reshape(variables, EIGHT, LANES))
                if done:
                    place = pl.ds(pl.multiple_of(i * 2 * EIGHT, 2 * EIGHT), 2 * EIGHT)
                    fields[:, place, lanes] = jnp.concatenate(done, axis=1).astype(jnp.bfloat16)
            if g + 1 == len(CHUNKS):
                leave_rows(i).start()
            return carry

        lax.fori_loop(low, high, step, 0)

    for g in range(len(CHUNKS)):
        came(g, (0, 3, 4, 7, 8))
        turn(g)
        if g + 1 < len(CHUNKS):
            finish_rows(g, 0, steps // 4)
            relay(g + 1)
            finish_rows(g, steps // 4, 3 * steps // 4)
            relay_last(g + 1)
            finish_rows(g, 3 * steps // 4, steps)
        else:
            finish_rows(g, 0, steps)
    for g in range(len(CHUNKS)):
        for kind in range(9):
            copy(g, kind).wait_send()

    def leave_step(i, carry):
        leave_rows(i).wait()
        return carry

    lax.fori_loop(0, steps, leave_step, 0)


def finish(mixed, back, fields, width, lift_weight, skip_weight, lift_bias, skip_bias, out_weight, out_bias):
    channels, waves, kx2 = mixed.shape
    variables, row_count, points = fields.shape
    tall = jnp.asarray(np.repeat(np.eye(channels), EIGHT, axis=0).astype(ml_dtypes.bfloat16))
    wide = jnp.asarray(np.repeat(np.eye(channels), EIGHT, axis=1).astype(ml_dtypes.bfloat16))
    operands = (
        mixed, back, fields, width, lift_weight, skip_weight, lift_bias[None], skip_bias[None], out_weight,
        out_bias[None], tall, wide,
    )
    blocks = row_count // EIGHT
    inner = variables * EIGHT
    depth = inner + 2 * EIGHT
    return pl.pallas_call(
        finish_kernel,
        in_specs=[pl.BlockSpec(memory_space=pl.ANY if n in (1, 2) else pltpu.VMEM) for n in range(len(operands))],
        out_specs=pl.BlockSpec(memory_space=pl.ANY),
        out_shape=jax.ShapeDtypeStruct(fields.shape, jnp.bfloat16),
        scratch_shapes=[
            pltpu.VMEM((channels, 8 * waves, kx2), jnp.bfloat16),
            pltpu.VMEM(back.shape[1:], jnp.bfloat16),
            pltpu.VMEM(fields.shape, jnp.bfloat16),
            pltpu.VMEM((blocks, depth, points), jnp.bfloat16),
            pltpu.VMEM((blocks, max(CHUNKS) * EIGHT, width.shape[0]), jnp.bfloat16),
            pltpu.VMEM((blocks, inner, points), jnp.float32),
            pltpu.VMEM((channels * EIGHT, depth), jnp.bfloat16),
            pltpu.VMEM((inner, channels * EIGHT), jnp.bfloat16),
            pltpu.VMEM((inner, 128), jnp.float32),
            pltpu.VMEM((points // LANES * 2, max(CHUNKS) * EIGHT, LANES), jnp.bfloat16),
            pltpu.SemaphoreType.DMA((2,)),
            pltpu.SemaphoreType.DMA((blocks // 2,)),
            pltpu.SemaphoreType.DMA((len(CHUNKS), 9)),
            pltpu.SemaphoreType.DMA((len(CHUNKS), 9)),
        ],
        compiler_params=pltpu.CompilerParams(
            collective_id=0, has_side_effects=True, vmem_limit_bytes=60 * 2**20
        ),
        name="finish",
    )(*operands)


def fast_shards(
    fields, lift_weight, lift_bias, first_core, second_core, input_core, output_core,
    skip_weight, skip_bias, out_weight, out_bias,
):
    holders = lax.axis_size("mode") * lax.axis_size("cores")
    waves, rank, _ = second_core.shape
    _, variables, row_count, points = fields.shape
    channels = lift_weight.shape[1]
    fields = fields[0]

    cosines, sines = host_pair(np.arange(MY), np.arange(points), points)
    root = math.sqrt(points)
    forward = np.stack([cosines, -sines], 0).reshape(2, holders, waves, points).transpose(1, 0, 2, 3)
    forward = jnp.asarray((forward.reshape(2 * MY, points) / root).astype(np.float32).astype(ml_dtypes.bfloat16))
    weight = np.where(np.arange(MY) == 0, 1.0, 2.0).astype(np.float32)[:, None]
    width = np.concatenate([cosines * weight, -sines * weight], 0) / root
    width = jnp.asarray(width.astype(ml_dtypes.bfloat16))
    order = cyclic_rows(row_count, holders)
    root = math.sqrt(NX)
    cosines, sines = host_pair(np.arange(MX) - MX // 2, order, NX)
    cosines, sines = [t.reshape(MX, holders, row_count) / root for t in (cosines, sines)]
    upper = np.stack([cosines, sines], 2)
    lower = np.stack([-sines, cosines], 2)
    height = np.stack([upper, lower], 0).reshape(2 * MX, -1).astype(ml_dtypes.bfloat16)
    real_part = np.asarray(height, np.float32).reshape(2 * MX, holders, 2, row_count)[:, :, 0]
    row_sum = real_part.sum((1, 2), dtype=np.float64).astype(np.float32)
    cos_t, sin_t = [t.transpose(1, 2, 0) for t in (cosines, sines)]
    up = np.concatenate([cos_t, -sin_t], 2)
    low = np.concatenate([sin_t, cos_t], 2)
    back_rows = jnp.asarray(np.concatenate([up, low], 1).astype(ml_dtypes.bfloat16))
    pairs = waves // 2
    place = np.zeros((2, variables, waves, pairs, 2, 2, SLOTS), np.float32)
    for q in range(2):
        for v in range(variables):
            for m in range(waves):
                place[q, v, m, m // 2, q, m % 2, v] = 1.0
    place = jnp.asarray(place.reshape(2, variables * waves, -1).astype(ml_dtypes.bfloat16))
    bias_row = np.zeros((MX, pairs, 2, 2, SLOTS), np.float32)
    bias_row[:, 0, :, 0, variables] = row_sum.reshape(2, MX).T
    bias_row = jnp.asarray(bias_row.reshape(MX, -1))
    packs = first_core.shape[0] // EIGHT
    first_spread = np.einsum("pk,bc->kpbc", np.eye(packs), np.repeat(np.eye(rank), EIGHT, axis=1))
    first_spread = jnp.asarray(first_spread.reshape(packs, packs * rank, rank * EIGHT).astype(ml_dtypes.bfloat16))
    spread = np.eye(8)[:, None, :, None, None] * np.eye(rank)[None, :, None, None, :] * np.ones((1, 1, 1, 4, 1))
    spread = jnp.asarray(spread.reshape(8 * rank, 32 * rank).astype(ml_dtypes.bfloat16))

    used = (variables + 4) // 4 * 4
    lift = jnp.concatenate(
        [lift_weight, (math.sqrt(points) * lift_bias).astype(jnp.bfloat16)[None],
         jnp.zeros((used - variables - 1, channels), jnp.bfloat16)], 0
    )
    count = input_core.shape[0]
    lift = lax.dynamic_slice_in_dim(lift, lax.axis_index("batch") * count, count, 1)
    inner = jnp.einsum("vc,cde->dve", lift, input_core, preferred_element_type=jnp.float32)
    inner = inner.astype(jnp.bfloat16).reshape(rank, used * rank)
    outer = output_core.transpose(1, 0, 3, 2).reshape(2 * count, rank * rank)
    mixed = mix(
        fields, forward, first_core, inner, outer, jnp.asarray(height), place, bias_row,
        second_core.reshape(waves * rank, rank), first_spread, spread, lax.axis_size("batch"),
    )
    return finish(
        mixed, back_rows, fields, width, lift_weight, skip_weight, lift_bias, skip_bias, out_weight.T, out_bias
    )[None]


def solution(mesh):
    placed = (
        P("batch", None, ("mode", "cores"), None),
        P(),
        P(),
        P("batch", None, None),
        P(("mode", "cores"), None, None),
        P("batch", None, None),
        P("batch", None, None, None),
        P(),
        P(),
        P(),
        P(),
    )
    fits = (
        mesh.shape["mode"] == 4 and mesh.shape["cores"] == 2 and MY // 8 == WAVES
        and mesh.shape["batch"] == 4 and MX // 4 % EIGHT == 0 and NX // 8 == 128
    )
    return jax.shard_map(
        fast_shards if fits else shards,
        mesh=mesh,
        in_specs=placed,
        out_specs=P("batch", None, ("mode", "cores"), None),
        check_vma=False,
    )
```

```python
import functools
import math

import jax
import jax.numpy as jnp
import ml_dtypes
import numpy as np
from jax import lax
from jax.experimental import pallas as pl
from jax.experimental.pallas import tpu as pltpu
from jax.sharding import PartitionSpec as P

NX = 1024
NY = 1024
MX = 128
MY = 128


TWO_PI = 2.0 * math.pi


def wave_pair(waves, points, length):
    phase_step = waves[:, None] * points[None, :] % length
    angles = phase_step.astype(jnp.float32) * (TWO_PI / length)
    return (jnp.cos(angles), jnp.sin(angles))


def width_forward(length, wave_count):
    points = jnp.arange(length, dtype=jnp.int32)
    waves = jnp.arange(wave_count, dtype=jnp.int32)
    cosines, sine_part = wave_pair(points, waves, length)
    stacked = jnp.stack([cosines, -sine_part], axis=1) / math.sqrt(length)
    return stacked.astype(jnp.bfloat16)


def height_forward(row_index, wave_count, length):
    waves = jnp.arange(wave_count, dtype=jnp.int32) - wave_count // 2
    cosines, sine_part = wave_pair(waves, row_index, length)
    upper = jnp.stack([cosines, sine_part], axis=1)
    lower = jnp.stack([-sine_part, cosines], axis=1)
    return (jnp.stack([upper, lower], axis=0) / math.sqrt(length)).astype(jnp.bfloat16)


def height_inverse(row_index, wave_count, length):
    waves = jnp.arange(wave_count, dtype=jnp.int32) - wave_count // 2
    cosines, sine_part = wave_pair(row_index, waves, length)
    upper = jnp.stack([cosines, -sine_part], axis=1)
    lower = jnp.stack([sine_part, cosines], axis=1)
    return (jnp.stack([upper, lower], axis=0) / math.sqrt(length)).astype(jnp.bfloat16)


def width_inverse(waves, length):
    points = jnp.arange(length, dtype=jnp.int32)
    cosines, sine_part = wave_pair(waves, points, length)
    weight = jnp.where(waves == 0, 1.0, 2.0).astype(jnp.float32)[:, None]
    stacked = jnp.stack([cosines * weight, -sine_part * weight], axis=0) / math.sqrt(length)
    return stacked.astype(jnp.bfloat16)


def bias_modes(lift_bias, wave_index, length):
    real_row = (
        jnp.where(wave_index == 0, 1.0, 0.0).astype(jnp.float32)[:, None]
        * (math.sqrt(length) * lift_bias)[None, :]
    )
    return jnp.stack([real_row, jnp.zeros_like(real_row)], axis=0)


def lift_modes(modes, lift_weight, lift_bias, wave_index):
    lifted_modes = jnp.einsum(
        "fabpmv,vc->fabpmc", modes, lift_weight, preferred_element_type=jnp.float32
    )
    return (lifted_modes + bias_modes(lift_bias, wave_index, NY)).astype(jnp.bfloat16)


def grid_rows(stored, row_count, holder_count):
    return stored % row_count * holder_count + stored // row_count


def shards(
    fields,
    lift_weight,
    lift_bias,
    first_core,
    second_core,
    input_core,
    output_core,
    skip_weight,
    skip_bias,
    out_weight,
    out_bias,
):
    mode_count = lax.axis_size("mode")
    core_count = lax.axis_size("cores")
    row_count = fields.shape[2]
    block_size = second_core.shape[0]
    block_start = (lax.axis_index("mode") * core_count + lax.axis_index("cores")) * block_size
    local_waves = block_start + jnp.arange(block_size, dtype=jnp.int32)
    lifted = (
        jnp.einsum("fvxy,vc->fxyc", fields, lift_weight, preferred_element_type=jnp.float32)
        + lift_bias
    ).astype(jnp.bfloat16)
    field_modes = jnp.einsum(
        "fvxy,ypk->fxpkv", fields, width_forward(NY, MY), preferred_element_type=jnp.float32
    ).astype(jnp.bfloat16)
    field_modes = field_modes[:, None]
    gathered = (
        lax.all_gather(first_core, "batch", axis=0, tiled=True),
        lax.all_gather(input_core, "batch", axis=0, tiled=True),
        lax.all_gather(output_core, "batch", axis=0, tiled=True),
    )
    first_whole, input_whole, output_whole = gathered
    mode_factor = jnp.einsum(
        "kab,mbd->kmad", first_whole, second_core, preferred_element_type=jnp.float32
    ).astype(jnp.bfloat16)
    arrived = lax.all_to_all(
        field_modes, ("mode", "cores"), split_axis=4, concat_axis=2, tiled=True
    )
    rows_held = jnp.arange(NX, dtype=jnp.int32)[None, :]
    by_mode = lift_modes(arrived, lift_weight, lift_bias, local_waves)
    lead_rows = rows_held.shape[0]
    side_rows = rows_held.shape[1]
    flat_rows = grid_rows(rows_held.reshape(-1), row_count, mode_count * core_count)
    height_table = height_forward(flat_rows, MX, NX).reshape(2, MX, 2, lead_rows, side_rows)
    spectrum = jnp.einsum(
        "qkpab,fabpmc->fqkmc", height_table, by_mode, preferred_element_type=jnp.float32
    ).astype(jnp.bfloat16)
    projected = jnp.einsum(
        "fqkmc,cbe->fqkmbe", spectrum, input_whole, preferred_element_type=jnp.float32
    ).astype(jnp.bfloat16)
    carried = jnp.einsum(
        "kmab,fqkmbe->fqkmae", mode_factor, projected, preferred_element_type=jnp.float32
    ).astype(jnp.bfloat16)
    traced = jnp.einsum(
        "fqkmae,osea->fqkmso", carried, output_whole, preferred_element_type=jnp.float32
    )
    real_part = traced[:, 0, :, :, 0, :] - traced[:, 1, :, :, 1, :]
    imaginary = traced[:, 0, :, :, 1, :] + traced[:, 1, :, :, 0, :]
    mixed_modes = jnp.stack([real_part, imaginary], axis=1).astype(jnp.bfloat16)
    height_back = height_inverse(flat_rows, MX, NX).reshape(2, lead_rows, side_rows, 2, MX)
    col_modes = jnp.einsum(
        "pabqk,fqkmc->fabpmc", height_back, mixed_modes, preferred_element_type=jnp.float32
    ).astype(jnp.bfloat16)
    returned = lax.all_to_all(col_modes, ("mode", "cores"), split_axis=2, concat_axis=4, tiled=True)
    waves_held = jnp.arange(MY, dtype=jnp.int32)
    width_back = width_inverse(waves_held, NY)
    spatial = jnp.einsum(
        "fxpmc,pmy->fxyc", returned[:, 0], width_back, preferred_element_type=jnp.float32
    )
    skip_term = jnp.einsum("fxyc,cd->fxyd", lifted, skip_weight, preferred_element_type=jnp.float32)
    active = jax.nn.gelu(spatial + skip_term + skip_bias, approximate=False).astype(jnp.bfloat16)
    result = (
        jnp.einsum("fxyc,cv->fvxy", active, out_weight, preferred_element_type=jnp.float32)
        + out_bias[:, None, None]
    )
    return result.astype(jnp.bfloat16)


def cyclic_rows(row_count, holders):
    return (np.arange(row_count)[None, :] * holders + np.arange(holders)[:, None]).reshape(-1)


def host_pair(waves, points, length):
    steps = np.asarray(waves)[:, None] * np.asarray(points)[None, :] % length
    angles = steps.astype(np.float32) * np.float32(TWO_PI / length)
    return np.cos(angles), np.sin(angles)


def dense(a, b, contract=((1,), (0,))):
    return lax.dot_general(a, b, (contract, ((), ())), preferred_element_type=jnp.float32)


MESH = pl.DeviceIdType.MESH
WAVES = 16
SLOTS = 32
EIGHT = 8
CHUNKS = (32, 48, 48)
STARTS = (0, 32, 80)
LANES = 512
ROWS = 128
PARTS = 2
TURN = 16


def whole(a):
    return pl.BlockSpec(a.shape, lambda *_: (0,) * a.ndim)


def mix_kernel(
    fields_far, forward, first_core, inner_own, outer_own, height_far, place_far, bias_row, second, first_spread, spread,
    mixed, first_wide, first_turned, first_own, fields, height, place, modes, arrived, first, inner, outer, stacked, placed, inner_wide, turned_inner, weights, rows,
    blocks, closing, carried, turned, load, send_plane, recv_plane, send_near, recv_near, send_modes, recv_modes,
):
    variables, row_count, points = fields.shape
    holders, lead, flat = arrived.shape
    waves = lead // 2
    kx_count = height.shape[0] // 2
    planes = first.shape[0]
    rank = inner.shape[1]
    channels = mixed.shape[0]
    pairs = waves // 2
    wide = 4 * rank
    slots = inner.shape[2] // rank
    packs = kx_count // EIGHT
    share = variables // PARTS
    mode, batch, core = lax.axis_index("mode"), lax.axis_index("batch"), lax.axis_index("cores")
    me = mode * 2 + core
    near = (mode + 1 - 2 * (mode % 2), batch, core)

    def load_part(c):
        here = pl.ds(c * share, share)
        return pltpu.make_async_copy(fields_far.at[here], fields.at[here], load.at[c])

    def load_table(n):
        return pltpu.make_async_copy((height_far, place_far)[n], (height, place)[n], load.at[PARTS + n])

    for c in range(PARTS):
        load_part(c).start()
    for n in range(2):
        load_table(n).start()

    def flip(bit, change):
        return bit + change - 2 * bit * change

    def peer(t):
        chip, side, line = flip(mode // 2, t // 4), flip(mode % 2, t // 2 % 2), flip(core, t % 2)
        return (chip * 2 + side, batch, line), chip * 4 + side * 2 + line

    def plane(step):
        return (mode, (batch + step) % planes, core)

    barrier = pltpu.get_barrier_semaphore()
    greeted = [peer(t)[0] for t in range(1, holders)] + [plane(step) for step in range(1, planes)]
    for device in greeted:
        pl.semaphore_signal(barrier, inc=1, device_id=device, device_id_type=MESH)
    pl.semaphore_wait(barrier, len(greeted))

    shards_own = (first_own, inner_own, outer_own)
    shards_all = (first, inner, outer)

    def half(n):
        size = shards_own[n].shape[0] // 2
        return pl.ds(pl.multiple_of((mode % 2) * size, size), size)

    def plane_copy(step, n):
        return pltpu.make_async_remote_copy(
            src_ref=shards_own[n].at[half(n)], dst_ref=shards_all[n].at[batch, half(n)],
            send_sem=send_plane.at[step - 1, n], recv_sem=recv_plane.at[step - 1, n],
            device_id=plane(step), device_id_type=MESH,
        )

    def near_copy(step, n):
        held = shards_all[n].at[(batch + planes - step) % planes, half(n)]
        return pltpu.make_async_remote_copy(
            src_ref=held, dst_ref=held, send_sem=send_near.at[step - 1, n], recv_sem=recv_near.at[step - 1, n],
            device_id=near, device_id_type=MESH,
        )

    def modes_copy(t, c):
        device, index = peer(t)
        lanes = pl.ds(c * share * row_count, share * row_count)
        return pltpu.make_async_remote_copy(
            src_ref=modes.at[index, :, lanes], dst_ref=arrived.at[me, :, lanes],
            send_sem=send_modes.at[t - 1, c], recv_sem=recv_modes.at[t - 1, c],
            device_id=device, device_id_type=MESH,
        )

    first_wide[...] = first_core[...].astype(jnp.float32)
    along = lax.broadcasted_iota(jnp.int32, (rank, first_own.shape[1]), 1)
    down = lax.broadcasted_iota(jnp.int32, (rank, first_own.shape[1]), 0)
    joined = None
    for k in range(packs // planes):
        for a in range(rank):
            first_turned[k, a * EIGHT:(a + 1) * EIGHT, :] = first_wide[k * EIGHT:(k + 1) * EIGHT, a, :]
        here = jnp.where(along == down + k * rank, 1.0, 0.0).astype(jnp.bfloat16)
        got = dense(first_turned[k].astype(jnp.bfloat16), here)
        joined = got if joined is None else joined + got
    first_own[...] = joined.astype(jnp.bfloat16)

    for n in range(3):
        for step in range(1, planes):
            plane_copy(step, n).start()
    for n in range(3):
        shards_all[n][batch] = shards_own[n][...]

    for c in range(PARTS):
        load_part(c).wait()
        for v in range(c * share, (c + 1) * share, 2):
            both = fields[v:v + 2].reshape(2 * row_count, points)
            got = dense(forward[...], both, ((1,), (1,))).astype(jnp.bfloat16)
            modes[:, :, v * row_count:(v + 2) * row_count] = got.reshape(holders, lead, 2 * row_count)
        for t in range(holders - 1, 0, -1):
            modes_copy(t, c).start()
    arrived[me] = modes[me]

    for n in range(2):
        for step in range(1, planes):
            plane_copy(step, n).wait_recv()
            near_copy(step, n).start()
    for n in range(2):
        for step in range(1, planes):
            near_copy(step, n).wait_recv()

    total = inner[0].astype(jnp.float32)
    for z in range(1, planes):
        total = total + inner[z].astype(jnp.float32)
    total = total.astype(jnp.bfloat16)
    for part in range(slots // 4):
        inner_wide[:, part * 4 * wide:(part + 1) * 4 * wide] = dense(
            total[:, part * wide:(part + 1) * wide], spread[:wide, :4 * wide]
        ).astype(jnp.bfloat16)

    down = lax.broadcasted_iota(jnp.int32, (rank * EIGHT, rank * EIGHT), 0) % EIGHT
    along = lax.broadcasted_iota(jnp.int32, (rank * EIGHT, rank * EIGHT), 1) % EIGHT
    same = down == along
    for z in range(planes):
        for k in range(packs // planes):
            full = dense(first[z], first_spread[k])
            blocks[z * (packs // planes) + k] = jnp.where(same, full, 0.0).astype(jnp.bfloat16)

    turned_inner[...] = jnp.zeros_like(turned_inner)
    group_of = lax.broadcasted_iota(jnp.int32, (SLOTS, wide), 1) // rank

    def weight_step(j, carry):
        start = pl.multiple_of(j * 2 * rank, 2 * rank)
        joined = dense(second[pl.ds(start, 2 * rank), :], inner_wide[...])
        for m in range(2):
            for v in range(slots):
                turned_inner[m, :, v, :] = joined[m * rank:(m + 1) * rank, v * wide:(v + 1) * wide]
        for m in range(2):
            for b in range(rank):
                value = turned_inner[m, b]
                for q in range(2):
                    weights[j, (q * 2 + m) * SLOTS:(q * 2 + m + 1) * SLOTS, b * wide:(b + 1) * wide] = jnp.where(
                        group_of == m * 2 + q, value, 0.0
                    ).astype(jnp.bfloat16)
        return carry

    lax.fori_loop(0, pairs // 2, weight_step, 0)
    for step in range(1, planes):
        plane_copy(step, 2).wait_recv()
        near_copy(step, 2).start()
    lax.fori_loop(pairs // 2, pairs, weight_step, 0)
    for step in range(1, planes):
        near_copy(step, 2).wait_recv()
    count = channels // planes
    lanes = lax.broadcasted_iota(jnp.int32, (count, 8 * wide), 1)
    part_of = lanes // rank % 2
    wave_of = lanes // (2 * rank) % 2
    for part in range(rank // 8):
        for z in range(planes):
            columns = slice(part * 8 * rank, (part + 1) * 8 * rank)
            real = dense(outer[z, :count, columns], spread[...])
            imaginary = dense(outer[z, count:, columns], spread[...])
            for r in range(2):
                value = jnp.where(part_of == 0, imaginary, real) if r else jnp.where(part_of == 0, real, -imaginary)
                for m in range(2):
                    start = (m * 2 + r) * channels + z * count
                    closing[start:start + count, part * 8 * wide:(part + 1) * 8 * wide] = (
                        jnp.where(wave_of == m, value, 0.0).astype(jnp.bfloat16)
                    )

    for n in range(2):
        load_table(n).wait()
    for c in range(PARTS):
        for t in range(1, holders):
            modes_copy(t, c).wait_recv()
    for d in range(holders):
        for p in range(2):
            for v in range(variables):
                stacked[v * waves:(v + 1) * waves, (d * 2 + p) * row_count:(d * 2 + p + 1) * row_count] = (
                    arrived[d, p * waves:(p + 1) * waves, v * row_count:(v + 1) * row_count]
                )
    by = dense(height[...], stacked[...], ((1,), (1,))).astype(jnp.bfloat16)
    first_wave = (me == 0).astype(jnp.float32)
    placed[...] = (
        dense(by[:kx_count], place[0]) + dense(by[kx_count:], place[1]) + bias_row[...] * first_wave
    ).astype(jnp.bfloat16)

    def pair_step(j, carry):
        column = pl.ds(pl.multiple_of(j * wide, wide), wide)
        own = placed[:, column]
        for part in range(rank // 8):
            got = dense(own, weights[j, :, part * 8 * wide:(part + 1) * 8 * wide])
            for k in range(packs):
                rows[k, part * 64:(part + 1) * 64, column] = jnp.concatenate(
                    [got[k * EIGHT:(k + 1) * EIGHT, b * wide:(b + 1) * wide] for b in range(8)], axis=0
                ).astype(jnp.bfloat16)
        return carry

    lax.fori_loop(0, pairs, pair_step, 0)

    def first_step(k, carry):
        here = pl.ds(pl.multiple_of(k * 2 * EIGHT, 2 * EIGHT), 2 * EIGHT)
        for part in range(pairs // 2):
            one, two = [
                dense(blocks[2 * k + i], rows[2 * k + i, :, part * 2 * wide:(part + 1) * 2 * wide]) for i in range(2)
            ]
            for j in range(2):
                side = slice(j * wide, (j + 1) * wide)
                for a in range(rank):
                    level = slice(a * EIGHT, (a + 1) * EIGHT)
                    carried[part * 2 + j, here, a * wide:(a + 1) * wide] = jnp.concatenate(
                        [one[level, side], two[level, side]], axis=0
                    ).astype(jnp.bfloat16)
        return carry

    lax.fori_loop(0, packs // 2, first_step, 0)

    for part in range(pairs // 2):
        both = carried[part * 2:part * 2 + 2].reshape(2 * kx_count, rank * wide)
        got = dense(closing[...], both, ((1,), (1,)))
        for m in range(2):
            for r in range(2):
                for j in range(2):
                    turned[:, (part * 2 + j) * 2 + m, r * kx_count:(r + 1) * kx_count] = got[
                        (m * 2 + r) * channels:(m * 2 + r + 1) * channels, j * kx_count:(j + 1) * kx_count
                    ]
    mixed[...] = turned[...].astype(jnp.bfloat16)

    for n in range(3):
        for step in range(1, planes):
            plane_copy(step, n).wait_send()
            near_copy(step, n).wait_send()
    for c in range(PARTS):
        for t in range(1, holders):
            modes_copy(t, c).wait_send()


def mix(fields, forward, first, inner, outer, height, place, bias_row, second, first_spread, spread, planes):
    variables, row_count, points = fields.shape
    holders = forward.shape[0] // (2 * WAVES)
    waves = WAVES
    kx2, depth = height.shape
    rank = inner.shape[0]
    channels = outer.shape[0] // 2 * planes
    wide = 4 * rank
    slots = inner.shape[1] // rank
    packs = kx2 // 2 // EIGHT
    joined = (rank * EIGHT, first.shape[0] // EIGHT * rank)
    operands = (fields, forward, first, inner, outer, height, place, bias_row, second, first_spread, spread)
    return pl.pallas_call(
        mix_kernel,
        in_specs=[pl.BlockSpec(memory_space=pl.ANY if n in (0, 5, 6) else pltpu.VMEM) for n in range(len(operands))],
        out_specs=pl.BlockSpec(memory_space=pltpu.VMEM),
        out_shape=jax.ShapeDtypeStruct((channels, waves, kx2), jnp.bfloat16),
        scratch_shapes=[
            pltpu.VMEM(first.shape, jnp.float32),
            pltpu.VMEM((first.shape[0] // EIGHT, rank * EIGHT, rank), jnp.float32),
            pltpu.VMEM(joined, jnp.bfloat16),
            pltpu.VMEM(fields.shape, jnp.bfloat16),
            pltpu.VMEM(height.shape, jnp.bfloat16),
            pltpu.VMEM(place.shape, jnp.bfloat16),
            pltpu.VMEM((holders, 2 * waves, variables * row_count), jnp.bfloat16),
            pltpu.VMEM((holders, 2 * waves, variables * row_count), jnp.bfloat16),
            pltpu.VMEM((planes,) + joined, jnp.bfloat16),
            pltpu.VMEM((planes,) + inner.shape, jnp.bfloat16),
            pltpu.VMEM((planes,) + outer.shape, jnp.bfloat16),
            pltpu.VMEM((place.shape[1], depth), jnp.bfloat16),
            pltpu.VMEM((kx2 // 2, waves // 2 * wide), jnp.bfloat16),
            pltpu.VMEM((rank, slots * wide), jnp.bfloat16),
            pltpu.VMEM((2, rank, SLOTS, wide), jnp.float32),
            pltpu.VMEM((waves // 2, 4 * SLOTS, rank * wide), jnp.bfloat16),
            pltpu.VMEM((packs, rank * EIGHT, waves // 2 * wide), jnp.bfloat16),
            pltpu.VMEM((packs, rank * EIGHT, rank * EIGHT), jnp.bfloat16),
            pltpu.VMEM((4 * channels, rank * wide), jnp.bfloat16),
            pltpu.VMEM((waves // 2, kx2 // 2, rank * wide), jnp.bfloat16),
            pltpu.VMEM((channels, waves, kx2), jnp.float32),
            pltpu.SemaphoreType.DMA((PARTS + 2,)),
            pltpu.SemaphoreType.DMA((planes - 1, 3)),
            pltpu.SemaphoreType.DMA((planes - 1, 3)),
            pltpu.SemaphoreType.DMA((planes - 1, 3)),
            pltpu.SemaphoreType.DMA((planes - 1, 3)),
            pltpu.SemaphoreType.DMA((holders - 1, PARTS)),
            pltpu.SemaphoreType.DMA((holders - 1, PARTS)),
        ],
        compiler_params=pltpu.CompilerParams(
            collective_id=1, has_side_effects=True, vmem_limit_bytes=60 * 2**20
        ),
        name="mix",
    )(*operands)


def twice_gelu(h):
    return h + h * lax.erf(h * (1.0 / math.sqrt(2.0)))


def finish_kernel(
    mixed, back_far, fields_far, width, lift_weight, skip_weight, lift_bias, skip_bias, out_weight, out_bias, tall, wide,
    result_far, gathered, back, fields, source, cols, total, skip, closing, last_bias, active, load, leave, send, recv,
):
    channels, waves, kx2 = mixed.shape
    variables, row_count, points = fields.shape
    inner = variables * EIGHT
    steps = row_count // EIGHT // 2
    mode, batch, core = lax.axis_index("mode"), lax.axis_index("batch"), lax.axis_index("cores")
    near = (mode + 1 - 2 * (mode % 2), batch, core)
    by_x = ((mode + 2) % 4, batch, core)
    by_y = (mode, batch, 1 - core)

    def owner(device):
        return device[0] * 2 + device[2]

    me = owner((mode, batch, core))
    at_x, at_y = owner(by_x), owner(by_y)
    across = owner((by_x[0], batch, by_y[2]))

    barrier = pltpu.get_barrier_semaphore()
    for device in (near, by_x, by_y):
        pl.semaphore_signal(barrier, inc=1, device_id=device, device_id_type=MESH)
    pl.semaphore_wait(barrier, 3)

    def piece(holder, first, count):
        return gathered.at[pl.ds(first, count), pl.ds(pl.multiple_of(holder * waves, waves), waves), :]

    def copy(g, kind):
        low, share = STARTS[g], CHUNKS[g]
        half = share // 2
        own = mixed.at[pl.ds(low, share)]
        home = piece(me, low, share)
        x_all, y_all = piece(at_x, low, share), piece(at_y, low, share)
        x_low, y_high = piece(at_x, low, half), piece(at_y, low + half, half)
        d_low, d_high = piece(across, low, half), piece(across, low + half, half)
        from_, to, device = (
            (own, home, near), (own, home, by_x), (own, home, by_y),
            (x_all, x_all, near), (y_all, y_all, near),
            (x_low, x_low, by_y), (y_high, y_high, by_x),
            (d_low, d_low, near), (d_high, d_high, near),
        )[kind]
        return pltpu.make_async_remote_copy(
            src_ref=from_, dst_ref=to, send_sem=send.at[g, kind], recv_sem=recv.at[g, kind],
            device_id=device, device_id_type=MESH,
        )

    def begin(g, kinds):
        for kind in kinds:
            copy(g, kind).start()

    def came(g, kinds):
        for kind in kinds:
            copy(g, kind).wait_recv()

    def relay(g):
        came(g, (1, 2))
        begin(g, (5, 6, 3, 4))
        if g + 1 < len(CHUNKS):
            begin(g + 1, (1, 2, 0))

    def relay_last(g):
        came(g, (5, 6))
        begin(g, (7, 8))

    begin(0, (1, 2, 0))
    loads = [
        pltpu.make_async_copy(fields_far, fields, load.at[0]),
        pltpu.make_async_copy(back_far.at[me], back, load.at[1]),
    ]
    for one in loads:
        one.start()
    gathered[:, pl.ds(pl.multiple_of(me * waves, waves), waves), :] = mixed[...]

    depth = skip.shape[1]
    line = lax.broadcasted_iota(jnp.int32, (depth - inner, points), 0)
    ones = jnp.where(line < 2, 1.0, 0.0).astype(jnp.bfloat16)
    for one in loads:
        one.wait()
    for x in range(steps):
        rows = fields[:, x * 2 * EIGHT:(x + 1) * 2 * EIGHT, :]
        for h in range(2):
            source[x * 2 + h, :inner, :] = rows[:, h * EIGHT:(h + 1) * EIGHT, :].reshape(inner, points)
            source[x * 2 + h, inner:, :] = ones
    relay(0)

    direct = dense(lift_weight[...], skip_weight[...]).astype(jnp.bfloat16)
    row_bias = lax.dot_general(
        jnp.broadcast_to(lift_bias[...], (8, channels)), skip_weight[...].astype(jnp.float32),
        (((1,), (0,)), ((), ())), preferred_element_type=jnp.float32, precision=lax.Precision.HIGHEST,
    )[:1] + skip_bias[...]
    size = 256
    down = lax.broadcasted_iota(jnp.int32, (size, depth), 0) % EIGHT
    along = lax.broadcasted_iota(jnp.int32, (size, depth), 1)
    for part in range(channels * EIGHT // size):
        here = slice(part * size, (part + 1) * size)
        picked = dense(tall[here, :], direct, ((1,), (1,))).astype(jnp.bfloat16)
        spread = dense(picked, wide[:variables, :depth])
        column = jnp.sum(tall[here, :].astype(jnp.float32) * row_bias, axis=1, keepdims=True)
        high = column.astype(jnp.bfloat16).astype(jnp.float32)
        rest = jnp.where(along == inner, high, jnp.where(along == inner + 1, column - high, 0.0))
        skip[here, :] = jnp.where(
            along < inner, jnp.where(down == along % EIGHT, spread, 0.0), rest
        ).astype(jnp.bfloat16)
    chosen = dense(tall[:inner, :variables], out_weight[...]).astype(jnp.bfloat16)
    down = lax.broadcasted_iota(jnp.int32, (inner, channels * EIGHT), 0) % EIGHT
    along = lax.broadcasted_iota(jnp.int32, (inner, channels * EIGHT), 1) % EIGHT
    closing[...] = jnp.where(down == along, 0.5 * dense(chosen, wide[...]), 0.0).astype(jnp.bfloat16)
    column = jnp.sum(tall[:inner, :variables].astype(jnp.float32) * out_bias[...], axis=1, keepdims=True)
    last_bias[...] = jnp.broadcast_to(column, last_bias.shape)
    relay_last(0)

    def turn(g):
        def step(c, carry):
            both = gathered[pl.ds(STARTS[g] + TURN * c, TURN)].reshape(TURN * waves * 8, kx2)
            got = dense(back[...], both, ((1,), (1,)))
            size = got.shape[1] // TURN
            for k in range(TURN // 2):
                place = pl.ds(pl.multiple_of(c * TURN * EIGHT + k * 2 * EIGHT, 2 * EIGHT), 2 * EIGHT)
                for p in range(2):
                    for x in range(row_count // EIGHT):
                        rows = got[p * row_count + x * EIGHT:p * row_count + (x + 1) * EIGHT, :]
                        cols[x, place, p * size:(p + 1) * size] = jnp.concatenate(
                            [rows[:, 2 * k * size:(2 * k + 1) * size], rows[:, (2 * k + 1) * size:(2 * k + 2) * size]],
                            axis=0,
                        ).astype(jnp.bfloat16)
            return carry

        lax.fori_loop(0, CHUNKS[g] // TURN, step, 0)

    def leave_rows(i):
        place = pl.ds(pl.multiple_of(i * 2 * EIGHT, 2 * EIGHT), 2 * EIGHT)
        return pltpu.make_async_copy(fields.at[:, place, :], result_far.at[:, place, :], leave.at[i])

    def finish_rows(g, low, high):
        start, size = STARTS[g] * EIGHT, CHUNKS[g] * EIGHT

        def step(i, carry):
            for lane in range(points // LANES):
                lanes = slice(lane * LANES, (lane + 1) * LANES)
                done = []
                for h in range(2):
                    x = 2 * i + h
                    for part in range(0, size, ROWS):
                        height = (
                            dense(cols[x, part:part + ROWS, :], width[:, lanes])
                            + dense(skip[start + part:start + part + ROWS, :], source[x, :, lanes])
                        )
                        active[lane * 2 + h, part:part + ROWS, :] = twice_gelu(height).astype(jnp.bfloat16)
                for h in range(2):
                    x = 2 * i + h
                    got = dense(closing[:, start:start + size], active[lane * 2 + h, :size, :])
                    if g == 0:
                        got = got + jnp.concatenate([last_bias[...]] * (LANES // 128), axis=1)
                    else:
                        got = got + total[x, :, lanes]
                    if g + 1 < len(CHUNKS):
                        total[x, :, lanes] = got
                    else:
                        done.append(got.reshape(variables, EIGHT, LANES))
                if done:
                    place = pl.ds(pl.multiple_of(i * 2 * EIGHT, 2 * EIGHT), 2 * EIGHT)
                    fields[:, place, lanes] = jnp.concatenate(done, axis=1).astype(jnp.bfloat16)
            if g + 1 == len(CHUNKS):
                leave_rows(i).start()
            return carry

        lax.fori_loop(low, high, step, 0)

    for g in range(len(CHUNKS)):
        came(g, (0, 3, 4, 7, 8))
        turn(g)
        if g + 1 < len(CHUNKS):
            finish_rows(g, 0, steps // 4)
            relay(g + 1)
            finish_rows(g, steps // 4, 3 * steps // 4)
            relay_last(g + 1)
            finish_rows(g, 3 * steps // 4, steps)
        else:
            finish_rows(g, 0, steps)
    for g in range(len(CHUNKS)):
        for kind in range(9):
            copy(g, kind).wait_send()

    def leave_step(i, carry):
        leave_rows(i).wait()
        return carry

    lax.fori_loop(0, steps, leave_step, 0)


def finish(mixed, back, fields, width, lift_weight, skip_weight, lift_bias, skip_bias, out_weight, out_bias):
    channels, waves, kx2 = mixed.shape
    variables, row_count, points = fields.shape
    tall = jnp.asarray(np.repeat(np.eye(channels), EIGHT, axis=0).astype(ml_dtypes.bfloat16))
    wide = jnp.asarray(np.repeat(np.eye(channels), EIGHT, axis=1).astype(ml_dtypes.bfloat16))
    operands = (
        mixed, back, fields, width, lift_weight, skip_weight, lift_bias[None], skip_bias[None], out_weight,
        out_bias[None], tall, wide,
    )
    blocks = row_count // EIGHT
    inner = variables * EIGHT
    depth = inner + 2 * EIGHT
    return pl.pallas_call(
        finish_kernel,
        in_specs=[pl.BlockSpec(memory_space=pl.ANY if n in (1, 2) else pltpu.VMEM) for n in range(len(operands))],
        out_specs=pl.BlockSpec(memory_space=pl.ANY),
        out_shape=jax.ShapeDtypeStruct(fields.shape, jnp.bfloat16),
        scratch_shapes=[
            pltpu.VMEM((channels, 8 * waves, kx2), jnp.bfloat16),
            pltpu.VMEM(back.shape[1:], jnp.bfloat16),
            pltpu.VMEM(fields.shape, jnp.bfloat16),
            pltpu.VMEM((blocks, depth, points), jnp.bfloat16),
            pltpu.VMEM((blocks, max(CHUNKS) * EIGHT, width.shape[0]), jnp.bfloat16),
            pltpu.VMEM((blocks, inner, points), jnp.float32),
            pltpu.VMEM((channels * EIGHT, depth), jnp.bfloat16),
            pltpu.VMEM((inner, channels * EIGHT), jnp.bfloat16),
            pltpu.VMEM((inner, 128), jnp.float32),
            pltpu.VMEM((points // LANES * 2, max(CHUNKS) * EIGHT, LANES), jnp.bfloat16),
            pltpu.SemaphoreType.DMA((2,)),
            pltpu.SemaphoreType.DMA((blocks // 2,)),
            pltpu.SemaphoreType.DMA((len(CHUNKS), 9)),
            pltpu.SemaphoreType.DMA((len(CHUNKS), 9)),
        ],
        compiler_params=pltpu.CompilerParams(
            collective_id=0, has_side_effects=True, vmem_limit_bytes=60 * 2**20
        ),
        name="finish",
    )(*operands)


def fast_shards(
    fields, lift_weight, lift_bias, first_core, second_core, input_core, output_core,
    skip_weight, skip_bias, out_weight, out_bias,
):
    holders = lax.axis_size("mode") * lax.axis_size("cores")
    waves, rank, _ = second_core.shape
    _, variables, row_count, points = fields.shape
    channels = lift_weight.shape[1]
    fields = fields[0]

    cosines, sines = host_pair(np.arange(MY), np.arange(points), points)
    root = math.sqrt(points)
    forward = np.stack([cosines, -sines], 0).reshape(2, holders, waves, points).transpose(1, 0, 2, 3)
    forward = jnp.asarray((forward.reshape(2 * MY, points) / root).astype(np.float32).astype(ml_dtypes.bfloat16))
    weight = np.where(np.arange(MY) == 0, 1.0, 2.0).astype(np.float32)[:, None]
    width = np.concatenate([cosines * weight, -sines * weight], 0) / root
    width = jnp.asarray(width.astype(ml_dtypes.bfloat16))
    order = cyclic_rows(row_count, holders)
    root = math.sqrt(NX)
    cosines, sines = host_pair(np.arange(MX) - MX // 2, order, NX)
    cosines, sines = [t.reshape(MX, holders, row_count) / root for t in (cosines, sines)]
    upper = np.stack([cosines, sines], 2)
    lower = np.stack([-sines, cosines], 2)
    height = np.stack([upper, lower], 0).reshape(2 * MX, -1).astype(ml_dtypes.bfloat16)
    real_part = np.asarray(height, np.float32).reshape(2 * MX, holders, 2, row_count)[:, :, 0]
    row_sum = real_part.sum((1, 2), dtype=np.float64).astype(np.float32)
    cos_t, sin_t = [t.transpose(1, 2, 0) for t in (cosines, sines)]
    up = np.concatenate([cos_t, -sin_t], 2)
    low = np.concatenate([sin_t, cos_t], 2)
    back_rows = jnp.asarray(np.concatenate([up, low], 1).astype(ml_dtypes.bfloat16))
    pairs = waves // 2
    place = np.zeros((2, variables, waves, pairs, 2, 2, SLOTS), np.float32)
    for q in range(2):
        for v in range(variables):
            for m in range(waves):
                place[q, v, m, m // 2, q, m % 2, v] = 1.0
    place = jnp.asarray(place.reshape(2, variables * waves, -1).astype(ml_dtypes.bfloat16))
    bias_row = np.zeros((MX, pairs, 2, 2, SLOTS), np.float32)
    bias_row[:, 0, :, 0, variables] = row_sum.reshape(2, MX).T
    bias_row = jnp.asarray(bias_row.reshape(MX, -1))
    packs = first_core.shape[0] // EIGHT
    first_spread = np.einsum("pk,bc->kpbc", np.eye(packs), np.repeat(np.eye(rank), EIGHT, axis=1))
    first_spread = jnp.asarray(first_spread.reshape(packs, packs * rank, rank * EIGHT).astype(ml_dtypes.bfloat16))
    spread = np.eye(8)[:, None, :, None, None] * np.eye(rank)[None, :, None, None, :] * np.ones((1, 1, 1, 4, 1))
    spread = jnp.asarray(spread.reshape(8 * rank, 32 * rank).astype(ml_dtypes.bfloat16))

    used = (variables + 4) // 4 * 4
    lift = jnp.concatenate(
        [lift_weight, (math.sqrt(points) * lift_bias).astype(jnp.bfloat16)[None],
         jnp.zeros((used - variables - 1, channels), jnp.bfloat16)], 0
    )
    count = input_core.shape[0]
    lift = lax.dynamic_slice_in_dim(lift, lax.axis_index("batch") * count, count, 1)
    inner = jnp.einsum("vc,cde->dve", lift, input_core, preferred_element_type=jnp.float32)
    inner = inner.astype(jnp.bfloat16).reshape(rank, used * rank)
    outer = output_core.transpose(1, 0, 3, 2).reshape(2 * count, rank * rank)
    mixed = mix(
        fields, forward, first_core, inner, outer, jnp.asarray(height), place, bias_row,
        second_core.reshape(waves * rank, rank), first_spread, spread, lax.axis_size("batch"),
    )
    return finish(
        mixed, back_rows, fields, width, lift_weight, skip_weight, lift_bias, skip_bias, out_weight.T, out_bias
    )[None]


def solution(mesh):
    placed = (
        P("batch", None, ("mode", "cores"), None),
        P(),
        P(),
        P("batch", None, None),
        P(("mode", "cores"), None, None),
        P("batch", None, None),
        P("batch", None, None, None),
        P(),
        P(),
        P(),
        P(),
    )
    fits = (
        mesh.shape["mode"] == 4 and mesh.shape["cores"] == 2 and MY // 8 == WAVES
        and mesh.shape["batch"] == 4 and MX // 4 % EIGHT == 0 and NX // 8 == 128
    )
    return jax.shard_map(
        fast_shards if fits else shards,
        mesh=mesh,
        in_specs=placed,
        out_specs=P("batch", None, ("mode", "cores"), None),
        check_vma=False,
    )
```
